256 devices in a mesh: dp: 4 (over z_hi), dap: 64 (over y, x, z_lo, core).
Axes of the slice: x: 4, y: 4, z: 8 (z_hi: 4, z_lo: 2; z = z_hi * 2 + z_lo), core: 2. Of those that a mesh axis runs over, the one named last changes fastest.
Arguments:
- pair_state: bfloat16 [1024, 256, 128], P(('dp', 'dap')), parts along dimension 0, may hold values from -6 to 6
- cotangent: bfloat16 [1024, 256, 128], P(('dp', 'dap')), parts along dimension 0, may hold values from -6 to 6
- length: int32 [4], P('dp'), parts along dimension 0, may hold values from 128 to 256
- norm_gain: float32 [128], replicated, may hold values from 0.1 to 1.9
- norm_shift: float32 [128], replicated, may hold values from -3 to 3
- w_in: bfloat16 [128, 512], replicated, may hold values from -0.5 to 0.5
- w_bias: bfloat16 [128, 4], replicated, may hold values from -0.5 to 0.5
- w_out: bfloat16 [128, 128], replicated, may hold values from -0.5 to 0.5
Outputs:
- update: bfloat16 [1024, 256, 128], P(('dp', 'dap')), parts along dimension 0
- grad_pair: bfloat16 [1024, 256, 128], P(('dp', 'dap')), parts along dimension 0
- grad_w_in: float32 [512, 512], P('dp'), parts along dimension 0
- grad_w_out: float32 [512, 128], P('dp'), parts along dimension 0
- grad_w_bias: float32 [512, 4], P('dp'), parts along dimension 0
- grad_gain: float32 [512], P('dp'), parts along dimension 0
- grad_shift: float32 [512], P('dp'), parts along dimension 0
The draws below stay inside these ranges and needn't reach their ends.
There are 4 independent parts, one for each index of `dp`. The reference program is written for one: setup_inputs(seed, part) draws one part's arguments, and reference() takes and returns one part's arrays. A program takes and returns all parts, laid end to end along the dimension named above; an argument that names none is the same for every part. Nothing has to cross between parts.
All inputs are finite; a program needn't handle non-finite values.
Results may differ from the reference program's by a relative error of at most 0.02.
Values may be sent and summed in bfloat16 or wider, within the bound.
A program may use at most 64 MiB of HBM per device.

```python
import math
import jax
import jax.numpy as jnp
from jax import lax

C = 128
HEADS = 4
HEAD_DIM = 32
N = 256


def shard_levels(stream_key, extent, split, least, high):
    def one(position, parts):
        steps = jax.random.uniform(jax.random.fold_in(jax.random.fold_in(stream_key, 6), position), (parts,), jnp.float32, least / len(split), high / len(split))
        return jnp.repeat(jnp.exp(steps), extent[position] // parts).reshape((-1,) + (1,) * (len(extent) - position - 1))

    level = one(*split[0])
    for cut in split[1:]:
        level = level * one(*cut)
    return level


def normal_values(rng, extent, scale, reach, pieces=(), held_as=jnp.bfloat16):
    entries = jax.random.normal(rng, extent, jnp.float32) * scale
    if len(pieces) > 0:
        entries = shard_levels(rng, extent, pieces, -0.22, 0.18) * entries
    return jnp.clip(entries, min=-reach, max=reach).astype(held_as)


def setup_inputs(seed: int = 0, part: int = 0) -> dict:
    streams_of = jax.random.split(jax.random.key(seed), 9)
    part_keys = jax.random.split(jax.random.fold_in(streams_of[8], part), 9)
    return {
        "pair_state": normal_values(part_keys[0], (N, N, C), 1.0, 6.0, ((0, 64),)),
        "cotangent": normal_values(part_keys[1], (N, N, C), 1.0, 6.0, ((0, 64),)),
        "length": jax.random.randint(part_keys[2], (1,), N // 2, N + 1).astype(jnp.int32),
        "norm_gain": jnp.clip(1.0 + 0.18 * jax.random.normal(streams_of[3], (C,), jnp.float32), 0.1, 1.9),
        "norm_shift": normal_values(streams_of[4], (C,), 0.5, 3.0, (), jnp.float32),
        "w_in": normal_values(streams_of[5], (C, 4 * HEADS * HEAD_DIM), C ** -0.5, 0.5),
        "w_bias": normal_values(streams_of[6], (C, HEADS), C ** -0.5, 0.5),
        "w_out": normal_values(streams_of[7], (HEADS * HEAD_DIM, C), (HEADS * HEAD_DIM) ** -0.5, 0.5),
    }


norm_epsilon = 1e-05
neg_fill = -1000000000.0

def layer_norm(pair_state, norm_gain, norm_shift):
    values = pair_state.astype(jnp.float32)
    row_mean = lax.optimization_barrier(jnp.mean(values, -1, keepdims=True))
    centered = values - row_mean
    variance = lax.optimization_barrier(jnp.mean(centered * centered, -1, keepdims=True))
    inv_std = lax.rsqrt(variance + norm_epsilon)
    normed = centered * inv_std
    return ((normed * norm_gain + norm_shift).astype(jnp.bfloat16), normed, inv_std)

def column_scores(q_col, k_col, bias_all, mask_add, score_scale):
    raw = jnp.einsum('ihd,khd->hik', q_col.astype(jnp.float32), k_col.astype(jnp.float32))
    return raw * score_scale + bias_all.astype(jnp.float32) + mask_add

def reference(pair_state, cotangent, length, norm_gain, norm_shift, w_in, w_bias, w_out):
    head_count = w_bias.shape[1]
    inner = w_out.shape[0]
    head_width = inner // head_count
    score_scale = 1.0 / math.sqrt(head_width)
    full_len = pair_state.shape[0]
    chans = pair_state.shape[2]
    normed_pair, normed, inv_std = layer_norm(pair_state, norm_gain, norm_shift)
    bias_all = jnp.einsum('kic,ch->hik', normed_pair.astype(jnp.float32), w_bias.astype(jnp.float32)).astype(jnp.bfloat16)
    mask_add = jnp.where(jnp.arange(full_len) < length[0], 0.0, neg_fill).astype(jnp.float32)
    columns = jnp.swapaxes(normed_pair, 0, 1)
    cot_cols = jnp.swapaxes(cotangent, 0, 1)
    split4 = (full_len, head_count, head_width)

    def column_pass(running, items):
        bias_grad, grad_in, grad_out = running
        col_pair, col_cot = items
        projected = jnp.dot(col_pair, w_in, preferred_element_type=jnp.float32)
        q_col = projected[:, :inner].astype(jnp.bfloat16).reshape(split4)
        k_col = projected[:, inner:2 * inner].astype(jnp.bfloat16).reshape(split4)
        v_col = projected[:, 2 * inner:3 * inner].astype(jnp.bfloat16).reshape(split4)
        gate_vals = jax.nn.sigmoid(projected[:, 3 * inner:])
        scores = column_scores(q_col, k_col, bias_all, mask_add, score_scale)
        highest = lax.optimization_barrier(jnp.max(scores, -1, keepdims=True))
        powers = jnp.exp(scores - highest)
        totals = lax.optimization_barrier(jnp.sum(powers, -1))
        logsum = highest[..., 0] + jnp.log(totals)
        weights_low = powers.astype(jnp.bfloat16)
        attended = jnp.einsum('hik,khd->ihd', weights_low.astype(jnp.float32), v_col.astype(jnp.float32)) / jnp.transpose(totals)[:, :, None]
        attended_flat = attended.reshape(full_len, inner)
        gated_out = (gate_vals * attended_flat).astype(jnp.bfloat16)
        out_col = jnp.dot(gated_out, w_out, preferred_element_type=jnp.float32).astype(jnp.bfloat16)
        dgated = jnp.dot(col_cot, jnp.transpose(w_out), preferred_element_type=jnp.float32)
        grad_out = grad_out + jnp.dot(jnp.transpose(gated_out), col_cot, preferred_element_type=jnp.float32)
        dout_low = (dgated * gate_vals).astype(jnp.bfloat16)
        dgate_pre = dgated * attended_flat * gate_vals * (1.0 - gate_vals)
        delta_sum = jnp.transpose(lax.optimization_barrier(jnp.sum((dout_low.astype(jnp.float32) * attended_flat).reshape(split4), -1)))
        probs = jnp.exp(scores - logsum[:, :, None])
        probs_low = probs.astype(jnp.bfloat16).astype(jnp.float32)
        dout_heads = dout_low.reshape(split4).astype(jnp.float32)
        dvalue = jnp.einsum('hik,ihd->khd', probs_low, dout_heads)
        dweights = jnp.einsum('ihd,khd->hik', dout_heads, v_col.astype(jnp.float32))
        dscores = probs * (dweights - delta_sum[:, :, None])
        dscores_low = dscores.astype(jnp.bfloat16).astype(jnp.float32)
        dquery = jnp.einsum('hik,khd->ihd', dscores_low, k_col.astype(jnp.float32)) * score_scale
        key_grad = jnp.einsum('hik,ihd->khd', dscores_low, q_col.astype(jnp.float32)) * score_scale
        dprojected = jnp.concatenate([dquery.reshape(full_len, inner), key_grad.reshape(full_len, inner), dvalue.reshape(full_len, inner), dgate_pre], -1).astype(jnp.bfloat16)
        dcol = jnp.dot(dprojected, jnp.transpose(w_in), preferred_element_type=jnp.float32).astype(jnp.bfloat16)
        grad_in = grad_in + jnp.dot(jnp.transpose(col_pair), dprojected, preferred_element_type=jnp.float32)
        return ((bias_grad + dscores, grad_in, grad_out), (out_col, dcol))
    start_state = (jnp.zeros((head_count, full_len, full_len), jnp.float32), jnp.zeros((chans, 4 * inner), jnp.float32), jnp.zeros((inner, chans), jnp.float32))
    final_state, outputs = lax.scan(column_pass, start_state, (columns, cot_cols))
    bias_grad, grad_w_in, grad_w_out = final_state
    out_cols, dcols = outputs
    update = jnp.swapaxes(out_cols, 0, 1)
    bias_low = bias_grad.astype(jnp.bfloat16).astype(jnp.float32)
    dnormed = jnp.swapaxes(dcols, 0, 1).astype(jnp.float32) + jnp.einsum('hik,ch->kic', bias_low, w_bias.astype(jnp.float32))
    grad_w_bias = jnp.einsum('kic,hik->ch', normed_pair.astype(jnp.float32), bias_low)
    scaled = dnormed * norm_gain
    grad_pair = (inv_std * (scaled - lax.optimization_barrier(jnp.mean(scaled, -1, keepdims=True)) - normed * lax.optimization_barrier(jnp.mean(scaled * normed, -1, keepdims=True)))).astype(jnp.bfloat16)
    grad_gain = lax.optimization_barrier(jnp.sum(dnormed * normed, (0, 1)))
    grad_shift = lax.optimization_barrier(jnp.sum(dnormed, (0, 1)))
    return (update, grad_pair, grad_w_in, grad_w_out, grad_w_bias, grad_gain, grad_shift)
```

```python
import functools
import math

import jax
import jax.numpy as jnp
from jax import lax
from jax.experimental import pallas as pl
from jax.experimental.pallas import tpu as pltpu
from jax.sharding import PartitionSpec as P

EPS = 1e-05
NEG = -1000000000.0
LOG2E = 1.4426950408889634
MESH = pl.DeviceIdType.MESH
F32 = jnp.float32
BF16 = jnp.bfloat16
ROWS = 4
COLS = 4
HEADS = 4
DIM = 32
N = 256
CH = 128


def nn(a, b):
    return lax.dot_general(a, b, (((1,), (0,)), ((), ())), preferred_element_type=F32)


def nt(a, b):
    return lax.dot_general(a, b, (((1,), (1,)), ((), ())), preferred_element_type=F32)


def tn(a, b):
    return lax.dot_general(a, b, (((0,), (0,)), ((), ())), preferred_element_type=F32)


def place(source_of):
    o = lax.broadcasted_iota(jnp.int32, (256, 256), 0)
    i = lax.broadcasted_iota(jnp.int32, (256, 256), 1)
    return jnp.where(source_of(o) == i, 1.0, 0.0).astype(BF16)


def rec_to_erc(o):
    return ((o >> 2) & 3) * 64 + ((o >> 4) << 2) + (o & 3)


def erc_to_cer(o):
    return ((o >> 2) & 15) * 16 + (o & 3) * 4 + (o >> 6)


def erc_to_rec(o):
    return ((o >> 2) & 15) * 16 + (o >> 6) * 4 + (o & 3)


def cer_to_erc(o):
    return (o & 3) * 64 + (o >> 4) * 4 + ((o >> 2) & 3)


def kernel(
    group,
    x_ref,
    cot_ref,
    len_ref,
    gain_ref,
    shift_ref,
    win_ref,
    wb_ref,
    wo_ref,
    upd_ref,
    gp_ref,
    gwin_ref,
    gwo_ref,
    gwb_ref,
    gg_ref,
    gs_ref,
    normed_ref,
    inv_ref,
    np_ref,
    pair_s,
    pair_r,
    cot_s,
    cot_r,
    bias_s,
    bias_r,
    cols_ref,
    cotc_ref,
    biasm_ref,
    proj_ref,
    gate_ref,
    dgate_ref,
    gated_ref,
    dproj_ref,
    bacc_ref,
    tmp_ref,
    upd_s,
    upd_r,
    dcol_s,
    dcol_r,
    bg_s,
    bg_r,
    par_f,
    par_s,
    par_r,
    sum_s,
    sum_r,
    small_s,
    small_r,
    send_sem,
    recv_sem,
):
    me = lax.axis_index("dap")

    def each_peer(body):
        def step(t, carry):
            body(lax.rem(me + t, group))
            return carry

        lax.fori_loop(1, group, step, 0)

    def send(which, source_of, dest):
        def one(e):
            pltpu.make_async_remote_copy(
                src_ref=source_of(e),
                dst_ref=dest.at[me],
                send_sem=send_sem.at[which],
                recv_sem=recv_sem.at[which],
                device_id={"dap": e},
                device_id_type=MESH,
            ).start()

        each_peer(one)

    def wait_recv(which, dest):
        part = dest.at[pl.ds(0, group - 1)]
        pltpu.make_async_copy(part, part, recv_sem.at[which]).wait()

    def wait_send(which, dest):
        part = dest.at[pl.ds(0, group - 1)]
        pltpu.make_async_copy(part, part, send_sem.at[which]).wait()

    barrier = pltpu.get_barrier_semaphore()
    each_peer(
        lambda e: pl.semaphore_signal(barrier, inc=1, device_id={"dap": e}, device_id_type=MESH)
    )

    rec_erc = place(rec_to_erc)
    erc_cer = place(erc_to_cer)
    erc_rec = place(erc_to_rec)
    cer_erc = place(cer_to_erc)

    for b in range(4):
        block = jnp.concatenate([cot_ref[r, 64 * b : 64 * b + 64, :] for r in range(ROWS)], 0)
        cot_s[16 * b : 16 * b + 16] = nn(rec_erc, block).astype(BF16).reshape(16, 16, CH)
    cot_r[me] = cot_s[me]

    pl.semaphore_wait(barrier, group - 1)
    send(0, lambda e: cot_s.at[e], cot_r)

    gain = gain_ref[...]
    shift = shift_ref[...]
    row_of = lax.broadcasted_iota(jnp.int32, (16, CH), 0)
    pick = jnp.where(
        (lax.broadcasted_iota(jnp.int32, (16, HEADS), 0) & 3)
        == lax.broadcasted_iota(jnp.int32, (16, HEADS), 1),
        1.0,
        0.0,
    ).astype(BF16)
    wb16 = nt(pick, wb_ref[...])
    wbr = [jnp.where((row_of >> 2) == r, wb16, 0.0).astype(BF16) for r in range(ROWS)]
    bias = jnp.zeros((16, N), F32)
    for r in range(ROWS):
        x = x_ref[r].astype(F32)
        mean = jnp.mean(x, -1, keepdims=True)
        cen = x - mean
        var = jnp.mean(cen * cen, -1, keepdims=True)
        inv = lax.rsqrt(var + EPS)
        normed = cen * inv
        normed_ref[r] = normed
        inv_ref[r] = jnp.broadcast_to(inv, (N, CH))
        low = (normed * gain + shift).astype(BF16)
        np_ref[r] = low
        bias += nt(wbr[r], low)
    for b in range(4):
        block = jnp.concatenate([np_ref[r, 64 * b : 64 * b + 64, :] for r in range(ROWS)], 0)
        pair_s[16 * b : 16 * b + 16] = nn(rec_erc, block).astype(BF16).reshape(16, 16, CH)
    bias_s[...] = bias.astype(BF16)
    pair_r[me] = pair_s[me]
    bias_r[me] = bias_s[...]
    send(1, lambda e: pair_s.at[e], pair_r)
    send(2, lambda e: bias_s, bias_r)

    w_in = win_ref[...]
    w_in_t = jnp.transpose(w_in.astype(F32)).astype(BF16)
    w_out = wo_ref[...]

    wait_recv(1, pair_r)
    for b in range(4):
        got = nn(erc_cer, pair_r[16 * b : 16 * b + 16].reshape(256, CH)).astype(BF16)
        for c in range(COLS):
            cols_ref[c, 64 * b : 64 * b + 64, :] = got[64 * c : 64 * c + 64]
    for j in range(COLS):
        projected = nt(w_in_t, cols_ref[j])
        proj_ref[j] = projected[: 3 * CH].astype(BF16)
        gate_ref[j] = jax.nn.sigmoid(projected[3 * CH :])

    wait_recv(0, cot_r)
    for b in range(4):
        got = nn(erc_cer, cot_r[16 * b : 16 * b + 16].reshape(256, CH)).astype(BF16)
        for c in range(COLS):
            cotc_ref[c, 64 * b : 64 * b + 64, :] = got[64 * c : 64 * c + 64]
    for j in range(COLS):
        dgate_ref[j] = nt(w_out, cotc_ref[j])

    wait_recv(2, bias_r)
    key = lax.broadcasted_iota(jnp.int32, (64, N), 0)
    for b in range(4):
        got = nn(erc_cer, bias_r[16 * b : 16 * b + 16].reshape(256, N)) * LOG2E
        mask = jnp.where(key + 64 * b < len_ref[0], 0.0, NEG)
        for h in range(HEADS):
            biasm_ref[h, 64 * b : 64 * b + 64, :] = got[64 * h : 64 * h + 64] + mask

    scale = 1.0 / math.sqrt(DIM)
    bacc_ref[...] = jnp.zeros_like(bacc_ref)

    def column(j, carry):
        for h in range(HEADS):
            rows = slice(DIM * h, DIM * h + DIM)
            q = proj_ref[j, DIM * h : DIM * h + DIM, :]
            k = proj_ref[j, CH + DIM * h : CH + DIM * h + DIM, :]
            v = proj_ref[j, 2 * CH + DIM * h : 2 * CH + DIM * h + DIM, :]
            s = tn(k, q) * (scale * LOG2E) + biasm_ref[h]
            p = jnp.exp2(s - jnp.max(s, 0, keepdims=True))
            inv_total = 1.0 / jnp.sum(p, 0, keepdims=True)
            p_low = p.astype(BF16)
            att = nn(v, p_low) * inv_total
            gate = gate_ref[j, rows, :]
            dgated = dgate_ref[j, rows, :]
            gated_ref[j, rows, :] = (gate * att).astype(BF16)
            datt = ((dgated * gate) * inv_total).astype(BF16)
            delta = jnp.sum(datt.astype(F32) * att, 0, keepdims=True)
            ds = p * (tn(v, datt) - delta)
            bacc_ref[h] += ds
            ds_low = ds.astype(BF16)
            dq = nn(k, ds_low) * scale
            dk = nt(q, ds_low) * scale
            dv = nt(datt, p_low)
            dg = dgated * att * gate * (1.0 - gate)
            dproj_ref[j, DIM * h : DIM * h + DIM, :] = dq.astype(BF16)
            dproj_ref[j, CH + DIM * h : CH + DIM * h + DIM, :] = dk.astype(BF16)
            dproj_ref[j, 2 * CH + DIM * h : 2 * CH + DIM * h + DIM, :] = dv.astype(BF16)
            dproj_ref[j, 3 * CH + DIM * h : 3 * CH + DIM * h + DIM, :] = dg.astype(BF16)
        return carry

    lax.fori_loop(0, COLS, column, 0)

    for b in range(4):
        block = jnp.concatenate([bacc_ref[h, 64 * b : 64 * b + 64, :] for h in range(HEADS)], 0)
        bg_s[16 * b : 16 * b + 16] = nn(cer_erc, block.astype(BF16)).astype(BF16).reshape(16, 16, N)
    bg_r[me] = bg_s[me]
    send(3, lambda e: bg_s.at[e], bg_r)

    for j in range(COLS):
        tmp_ref[j] = tn(dproj_ref[j], w_in_t).astype(BF16)
    for b in range(4):
        block = jnp.concatenate([tmp_ref[j, 64 * b : 64 * b + 64, :] for j in range(COLS)], 0)
        dcol_s[16 * b : 16 * b + 16] = nn(cer_erc, block).astype(BF16).reshape(16, 16, CH)
    dcol_r[me] = dcol_s[me]
    send(4, lambda e: dcol_s.at[e], dcol_r)

    for j in range(COLS):
        tmp_ref[j] = tn(gated_ref[j], w_out).astype(BF16)
    for b in range(4):
        block = jnp.concatenate([tmp_ref[j, 64 * b : 64 * b + 64, :] for j in range(COLS)], 0)
        upd_s[16 * b : 16 * b + 16] = nn(cer_erc, block).astype(BF16).reshape(16, 16, CH)
    upd_r[me] = upd_s[me]
    send(5, lambda e: upd_s.at[e], upd_r)

    g_in = nn(dproj_ref[0], cols_ref[0])
    g_out = nn(gated_ref[0], cotc_ref[0])
    for j in range(1, COLS):
        g_in += nn(dproj_ref[j], cols_ref[j])
        g_out += nn(gated_ref[j], cotc_ref[j])
    par_f[...] = jnp.zeros_like(par_f)
    for e in range(group):
        par_f[16 * e : 16 * e + 8, :] = g_in[8 * e : 8 * e + 8]
    par_f[pl.ds(8, group, stride=16), :] = g_out[:group]
    par_f[pl.ds(9, group, stride=16), :] = g_out[group:]
    par_s[...] = par_f[...].astype(BF16).reshape(group, 16, CH)
    par_r[me] = par_s[me]
    send(6, lambda e: par_s.at[e], par_r)

    wait_recv(3, bg_r)
    share = bg_r[0].astype(F32)
    for s in range(1, group):
        share += bg_r[s].astype(F32)
    share = share.astype(BF16)

    wait_recv(6, par_r)
    total = par_r[0].astype(F32)
    for s in range(1, group):
        total += par_r[s].astype(F32)
    sum_s[...] = total.astype(BF16)
    sum_r[me] = sum_s[...]
    send(7, lambda e: sum_s, sum_r)

    wait_recv(4, dcol_r)
    for b in range(4):
        got = nn(erc_rec, dcol_r[16 * b : 16 * b + 16].reshape(256, CH)).astype(BF16)
        for r in range(ROWS):
            tmp_ref[r, 64 * b : 64 * b + 64, :] = got[64 * r : 64 * r + 64]
    gwb = jnp.zeros((16, CH), F32)
    grad_gain = jnp.zeros((1, CH), F32)
    grad_shift = jnp.zeros((1, CH), F32)
    for r in range(ROWS):
        normed = normed_ref[r]
        dn = tmp_ref[r].astype(F32) + tn(share, wbr[r])
        gwb += jnp.where((row_of >> 2) == r, nn(share, np_ref[r]), 0.0)
        grad_gain += jnp.sum(dn * normed, 0, keepdims=True)
        grad_shift += jnp.sum(dn, 0, keepdims=True)
        scaled = dn * gain
        mean_s = jnp.mean(scaled, -1, keepdims=True)
        mean_sn = jnp.mean(scaled * normed, -1, keepdims=True)
        gp_ref[r] = (inv_ref[r] * (scaled - mean_s - normed * mean_sn)).astype(BF16)
    small_s[...] = jnp.zeros_like(small_s)
    small_s[0:4, :] = gwb[0:4] + gwb[4:8] + gwb[8:12] + gwb[12:16]
    small_s[4:5, :] = grad_gain
    small_s[5:6, :] = grad_shift
    small_r[me] = small_s[...]
    send(8, lambda e: small_s, small_r)

    wait_recv(5, upd_r)
    for b in range(4):
        got = nn(erc_rec, upd_r[16 * b : 16 * b + 16].reshape(256, CH)).astype(BF16)
        for r in range(ROWS):
            upd_ref[r, 64 * b : 64 * b + 64, :] = got[64 * r : 64 * r + 64]

    wait_recv(7, sum_r)
    par_f[...] = sum_r[...].astype(F32).reshape(group * 16, CH)
    gwo_ref[0:group, :] = par_f[pl.ds(8, group, stride=16), :]
    gwo_ref[group:, :] = par_f[pl.ds(9, group, stride=16), :]
    for q in range(4):
        part = jnp.concatenate(
            [par_f[16 * e : 16 * e + 8, :] for e in range(16 * q, 16 * q + 16)], 0
        )
        gwin_ref[:, CH * q : CH * q + CH] = jnp.transpose(part)

    wait_recv(8, small_r)
    small = small_r[0]
    for s in range(1, group):
        small += small_r[s]
    gwb_ref[...] = jnp.transpose(small)[:, 0:HEADS]
    gg_ref[...] = small[4:5]
    gs_ref[...] = small[5:6]

    for which, dest in enumerate(
        (cot_r, pair_r, bias_r, bg_r, dcol_r, upd_r, par_r, sum_r, small_r)
    ):
        wait_send(which, dest)


def per_device(group, pair_state, cotangent, length, norm_gain, norm_shift, w_in, w_bias, w_out):
    vmem = pl.BlockSpec(memory_space=pltpu.VMEM)
    smem = pl.BlockSpec(memory_space=pltpu.SMEM)
    block = (group, 16, CH)
    wide = (group, 16, N)
    out = pl.pallas_call(
        functools.partial(kernel, group),
        out_shape=(
            jax.ShapeDtypeStruct((ROWS, N, CH), BF16),
            jax.ShapeDtypeStruct((ROWS, N, CH), BF16),
            jax.ShapeDtypeStruct((CH, 4 * CH), F32),
            jax.ShapeDtypeStruct((CH, CH), F32),
            jax.ShapeDtypeStruct((CH, HEADS), F32),
            jax.ShapeDtypeStruct((1, CH), F32),
            jax.ShapeDtypeStruct((1, CH), F32),
        ),
        in_specs=[vmem, vmem, smem] + [vmem] * 5,
        out_specs=[vmem] * 7,
        scratch_shapes=[
            pltpu.VMEM((ROWS, N, CH), F32),
            pltpu.VMEM((ROWS, N, CH), F32),
            pltpu.VMEM((ROWS, N, CH), BF16),
            pltpu.VMEM(block, BF16),
            pltpu.VMEM(block, BF16),
            pltpu.VMEM(block, BF16),
            pltpu.VMEM(block, BF16),
            pltpu.VMEM((16, N), BF16),
            pltpu.VMEM(wide, BF16),
            pltpu.VMEM((COLS, N, CH), BF16),
            pltpu.VMEM((COLS, N, CH), BF16),
            pltpu.VMEM((HEADS, N, N), F32),
            pltpu.VMEM((COLS, 3 * CH, N), BF16),
            pltpu.VMEM((COLS, CH, N), F32),
            pltpu.VMEM((COLS, CH, N), F32),
            pltpu.VMEM((COLS, CH, N), BF16),
            pltpu.VMEM((COLS, 4 * CH, N), BF16),
            pltpu.VMEM((HEADS, N, N), F32),
            pltpu.VMEM((COLS, N, CH), BF16),
            pltpu.VMEM(block, BF16),
            pltpu.VMEM(block, BF16),
            pltpu.VMEM(block, BF16),
            pltpu.VMEM(block, BF16),
            pltpu.VMEM(wide, BF16),
            pltpu.VMEM(wide, BF16),
            pltpu.VMEM((group * 16, CH), F32),
            pltpu.VMEM(block, BF16),
            pltpu.VMEM(block, BF16),
            pltpu.VMEM((16, CH), BF16),
            pltpu.VMEM(block, BF16),
            pltpu.VMEM((8, CH), F32),
            pltpu.VMEM((group, 8, CH), F32),
            pltpu.SemaphoreType.DMA((9,)),
            pltpu.SemaphoreType.DMA((9,)),
        ],
        compiler_params=pltpu.CompilerParams(
            collective_id=0, has_side_effects=True, vmem_limit_bytes=40 * 2**20
        ),
    )(
        pair_state,
        cotangent,
        length,
        norm_gain.reshape(1, CH),
        norm_shift.reshape(1, CH),
        w_in,
        w_bias,
        w_out,
    )
    return (*out[:5], out[5].reshape(CH), out[6].reshape(CH))


def solution(mesh):
    split = P(("dp", "dap"), None, None)
    return jax.shard_map(
        functools.partial(per_device, mesh.shape["dap"]),
        mesh=mesh,
        in_specs=(split, split, P("dp"), P(), P(), P(), P(), P()),
        out_specs=(split, split, P("dp", None), P("dp", None), P("dp", None), P("dp"), P("dp")),
        check_vma=False,
    )
```

```python
import functools
import math

import jax
import jax.numpy as jnp
from jax import lax
from jax.experimental import pallas as pl
from jax.experimental.pallas import tpu as pltpu
from jax.sharding import PartitionSpec as P

EPS = 1e-05
NEG = -1000000000.0
LOG2E = 1.4426950408889634
MESH = pl.DeviceIdType.MESH
F32 = jnp.float32
BF16 = jnp.bfloat16
ROWS = 4
COLS = 4
HEADS = 4
DIM = 32
N = 256
CH = 128


def nn(a, b):
    return lax.dot_general(a, b, (((1,), (0,)), ((), ())), preferred_element_type=F32)


def nt(a, b):
    return lax.dot_general(a, b, (((1,), (1,)), ((), ())), preferred_element_type=F32)


def tn(a, b):
    return lax.dot_general(a, b, (((0,), (0,)), ((), ())), preferred_element_type=F32)


def place(source_of):
    o = lax.broadcasted_iota(jnp.int32, (256, 256), 0)
    i = lax.broadcasted_iota(jnp.int32, (256, 256), 1)
    return jnp.where(source_of(o) == i, 1.0, 0.0).astype(BF16)


def rec_to_erc(o):
    return ((o >> 2) & 3) * 64 + ((o >> 4) << 2) + (o & 3)


def erc_to_cer(o):
    return ((o >> 2) & 15) * 16 + (o & 3) * 4 + (o >> 6)


def erc_to_rec(o):
    return ((o >> 2) & 15) * 16 + (o >> 6) * 4 + (o & 3)


def cer_to_erc(o):
    return (o & 3) * 64 + (o >> 4) * 4 + ((o >> 2) & 3)


def kernel(
    group,
    x_hbm,
    cot_hbm,
    len_ref,
    gain_hbm,
    shift_hbm,
    win_hbm,
    wb_hbm,
    wo_hbm,
    upd_hbm,
    gp_hbm,
    gwin_hbm,
    gwo_hbm,
    gwb_hbm,
    gg_hbm,
    gs_hbm,
    upd_ref,
    gp_ref,
    gwin_ref,
    gwo_ref,
    gwb_ref,
    gg_ref,
    gs_ref,
    x_ref,
    cot_ref,
    gain_ref,
    shift_ref,
    win_ref,
    wb_ref,
    wo_ref,
    normed_ref,
    inv_ref,
    np_ref,
    pair_s,
    pair_r,
    cot_s,
    cot_r,
    bias_r,
    cols_ref,
    cotc_ref,
    biasm_ref,
    proj_ref,
    gate_ref,
    dgate_ref,
    gated_ref,
    att_ref,
    tot_ref,
    p_ref,
    dproj_ref,
    bacc_ref,
    tmp_ref,
    upd_s,
    upd_r,
    dcol_s,
    dcol_r,
    bg_s,
    bg_x,
    bg_t,
    bg_r,
    par_f,
    par_s,
    par_x,
    par_t,
    par_r,
    sum_r,
    small_s,
    small_r,
    in_sem,
    out_sem,
    send_sem,
    recv_sem,
):
    me = lax.axis_index("dap")
    core = lax.rem(me, 2)
    chip = lax.div(me, 2)
    twin = me + 1 - 2 * core
    chips = group // 2
    cot_x, pair_x, bias_x, bias_w, bg_w, bg_x_, dcol_x, upd_x, par_w, par_x_, sum_x, sum_w, small_x = range(13)

    loads = [
        pltpu.make_async_copy(src, dst, in_sem.at[n])
        for n, (src, dst) in enumerate(
            (
                (x_hbm, x_ref),
                (cot_hbm, cot_ref),
                (gain_hbm, gain_ref),
                (shift_hbm, shift_ref),
                (win_hbm, win_ref),
                (wb_hbm, wb_ref),
                (wo_hbm, wo_ref),
            )
        )
    ]
    for load in loads:
        load.start()

    stores = [
        pltpu.make_async_copy(src, dst, out_sem.at[n])
        for n, (src, dst) in enumerate(
            (
                (upd_ref, upd_hbm),
                (gp_ref, gp_hbm),
                (gwin_ref, gwin_hbm),
                (gwo_ref, gwo_hbm),
                (gwb_ref, gwb_hbm),
                (gg_ref, gg_hbm),
                (gs_ref, gs_hbm),
            )
        )
    ]

    def each_peer(body):
        def step(t, carry):
            body(lax.rem(me + t, group))
            return carry

        lax.fori_loop(1, group, step, 0)

    def each_chip(body):
        def step(t, carry):
            body(lax.rem(chip + t, chips))
            return carry

        lax.fori_loop(1, chips, step, 0)

    def copy(which, src, dst, device):
        return pltpu.make_async_remote_copy(
            src_ref=src,
            dst_ref=dst,
            send_sem=send_sem.at[which],
            recv_sem=recv_sem.at[which],
            device_id={"dap": device},
            device_id_type=MESH,
        )

    sent = []

    def send(which, source_of, dest):
        each_peer(lambda e: copy(which, source_of(e), dest.at[me], e).start())
        sent.append((which, dest.at[pl.ds(0, group - 1)]))

    def wait_recv(which, part):
        pltpu.make_async_copy(part, part, recv_sem.at[which]).wait()

    def wait_send(which, part):
        pltpu.make_async_copy(part, part, send_sem.at[which]).wait()

    barrier = pltpu.get_barrier_semaphore()
    each_peer(
        lambda e: pl.semaphore_signal(barrier, inc=1, device_id={"dap": e}, device_id_type=MESH)
    )

    rec_erc = place(rec_to_erc)
    erc_cer = place(erc_to_cer)
    erc_rec = place(erc_to_rec)
    cer_erc = place(cer_to_erc)
    row_of = lax.broadcasted_iota(jnp.int32, (16, CH), 0)
    pick = jnp.where(
        (lax.broadcasted_iota(jnp.int32, (16, HEADS), 0) & 3)
        == lax.broadcasted_iota(jnp.int32, (16, HEADS), 1),
        1.0,
        0.0,
    ).astype(BF16)

    for load in loads:
        load.wait()
    gain = gain_ref[...]
    shift = shift_ref[...]
    wb16 = nn(pick, wb_ref[...])
    wbr = [jnp.where((row_of >> 2) == r, wb16, 0.0).astype(BF16) for r in range(ROWS)]
    bias = jnp.zeros((16, N), F32)
    for r in range(ROWS):
        x = x_ref[r].astype(F32)
        mean = jnp.mean(x, -1, keepdims=True)
        cen = x - mean
        var = jnp.mean(cen * cen, -1, keepdims=True)
        inv = lax.rsqrt(var + EPS)
        normed = cen * inv
        normed_ref[r] = normed
        inv_ref[r] = jnp.broadcast_to(inv, (N, CH))
        low = (normed * gain + shift).astype(BF16)
        np_ref[r] = low
        bias += nt(wbr[r], low)
    for b in range(4):
        block = jnp.concatenate([np_ref[r, 64 * b : 64 * b + 64, :] for r in range(ROWS)], 0)
        pair_s[16 * b : 16 * b + 16] = nn(rec_erc, block).astype(BF16).reshape(16, 16, CH)
    for b in range(4):
        block = jnp.concatenate([cot_ref[r, 64 * b : 64 * b + 64, :] for r in range(ROWS)], 0)
        cot_s[16 * b : 16 * b + 16] = nn(rec_erc, block).astype(BF16).reshape(16, 16, CH)
    bias_r[chip, core] = bias.astype(BF16)
    pair_r[me] = pair_s[me]
    cot_r[me] = cot_s[me]

    pl.semaphore_wait(barrier, group - 1)

    def first(q):
        copy(pair_x, pair_s.at[2 * q + core], pair_r.at[me], 2 * q + core).start()
        copy(bias_x, bias_r.at[chip, core], bias_r.at[chip, core], 2 * q + core).start()
        copy(pair_x, pair_s.at[2 * q + 1 - core], pair_r.at[me], 2 * q + 1 - core).start()

    each_chip(first)
    copy(pair_x, pair_s.at[twin], pair_r.at[me], twin).start()
    sent.append((pair_x, pair_r.at[pl.ds(0, group - 1)]))
    sent.append((bias_x, bias_r.at[pl.ds(0, chips - 1), 0]))
    send(cot_x, lambda e: cot_s.at[e], cot_r)

    w_in = win_ref[...]
    w_in_t = jnp.transpose(w_in.astype(F32)).astype(BF16)
    w_out = wo_ref[...]

    wait_recv(pair_x, pair_r.at[pl.ds(0, group - 1)])
    for b in range(4):
        got = nn(erc_cer, pair_r[16 * b : 16 * b + 16].reshape(256, CH)).astype(BF16)
        for c in range(COLS):
            cols_ref[c, 64 * b : 64 * b + 64, :] = got[64 * c : 64 * c + 64]
    for j in range(COLS):
        projected = nt(w_in_t, cols_ref[j])
        proj_ref[j] = projected[: 3 * CH].astype(BF16)
        gate_ref[j] = jax.nn.sigmoid(projected[3 * CH :])

    wait_recv(bias_x, bias_r.at[pl.ds(0, chips - 1), 0])
    share = copy(bias_w, bias_r.at[:, core], bias_r.at[:, core], twin)
    share.start()
    share.wait()
    key = lax.broadcasted_iota(jnp.int32, (64, N), 0)
    for b in range(4):
        block = bias_r[8 * b : 8 * b + 8].reshape(256, N)
        got = nn(erc_cer, block) * LOG2E
        mask = jnp.where(key + 64 * b < len_ref[0], 0.0, NEG)
        for h in range(HEADS):
            biasm_ref[h, 64 * b : 64 * b + 64, :] = got[64 * h : 64 * h + 64] + mask

    scale = 1.0 / math.sqrt(DIM)

    def forward(j, carry):
        for h in range(HEADS):
            rows = slice(DIM * h, DIM * h + DIM)
            q = proj_ref[j, DIM * h : DIM * h + DIM, :]
            k = proj_ref[j, CH + DIM * h : CH + DIM * h + DIM, :]
            v = proj_ref[j, 2 * CH + DIM * h : 2 * CH + DIM * h + DIM, :]
            s = tn(k, q) * (scale * LOG2E) + biasm_ref[h]
            p = jnp.exp2(s - jnp.max(s, 0, keepdims=True))
            inv_total = 1.0 / jnp.sum(p, 0, keepdims=True)
            p_low = p.astype(BF16)
            p_ref[HEADS * j + h] = p_low
            att = nn(v, p_low) * inv_total
            att_ref[j, rows, :] = att
            tot_ref[j, h : h + 1, :] = inv_total
            gated_ref[j, rows, :] = (gate_ref[j, rows, :] * att).astype(BF16)
        return carry

    lax.fori_loop(0, COLS, forward, 0)

    for j in range(COLS):
        tmp_ref[j] = tn(gated_ref[j], w_out).astype(BF16)
    for b in range(4):
        block = jnp.concatenate([tmp_ref[j, 64 * b : 64 * b + 64, :] for j in range(COLS)], 0)
        upd_s[16 * b : 16 * b + 16] = nn(cer_erc, block).astype(BF16).reshape(16, 16, CH)
    upd_r[me] = upd_s[me]
    send(upd_x, lambda e: upd_s.at[e], upd_r)

    wait_recv(cot_x, cot_r.at[pl.ds(0, group - 1)])
    for b in range(4):
        got = nn(erc_cer, cot_r[16 * b : 16 * b + 16].reshape(256, CH)).astype(BF16)
        for c in range(COLS):
            cotc_ref[c, 64 * b : 64 * b + 64, :] = got[64 * c : 64 * c + 64]
    for j in range(COLS):
        dgate_ref[j] = nt(w_out, cotc_ref[j])

    bacc_ref[...] = jnp.zeros_like(bacc_ref)

    def backward(j, carry):
        for h in range(HEADS):
            rows = slice(DIM * h, DIM * h + DIM)
            q = proj_ref[j, DIM * h : DIM * h + DIM, :]
            k = proj_ref[j, CH + DIM * h : CH + DIM * h + DIM, :]
            v = proj_ref[j, 2 * CH + DIM * h : 2 * CH + DIM * h + DIM, :]
            att = att_ref[j, rows, :]
            gate = gate_ref[j, rows, :]
            dgated = dgate_ref[j, rows, :]
            datt = ((dgated * gate) * tot_ref[j, h : h + 1, :]).astype(BF16)
            delta = jnp.sum(datt.astype(F32) * att, 0, keepdims=True)
            p_low = p_ref[HEADS * j + h]
            ds = p_low.astype(F32) * (tn(v, datt) - delta)
            bacc_ref[h] += ds
            ds_low = ds.astype(BF16)
            dq = nn(k, ds_low) * scale
            dk = nt(q, ds_low) * scale
            dv = nt(datt, p_low)
            dg = dgated * att * gate * (1.0 - gate)
            dproj_ref[j, DIM * h : DIM * h + DIM, :] = dq.astype(BF16)
            dproj_ref[j, CH + DIM * h : CH + DIM * h + DIM, :] = dk.astype(BF16)
            dproj_ref[j, 2 * CH + DIM * h : 2 * CH + DIM * h + DIM, :] = dv.astype(BF16)
            dproj_ref[j, 3 * CH + DIM * h : 3 * CH + DIM * h + DIM, :] = dg.astype(BF16)
        return carry

    lax.fori_loop(0, COLS, backward, 0)

    for b in range(4):
        block = jnp.concatenate([bacc_ref[h, 64 * b : 64 * b + 64, :] for h in range(HEADS)], 0)
        got = nn(cer_erc, block.astype(BF16)).astype(BF16)
        bg_s[8 * b : 8 * b + 8] = got.reshape(8, 2, 16, N)
    bg_pass = copy(bg_w, bg_s.at[:, 1 - core], bg_x, twin)
    bg_pass.start()

    for j in range(COLS):
        tmp_ref[j] = tn(dproj_ref[j], w_in_t).astype(BF16)
    for b in range(4):
        block = jnp.concatenate([tmp_ref[j, 64 * b : 64 * b + 64, :] for j in range(COLS)], 0)
        dcol_s[16 * b : 16 * b + 16] = nn(cer_erc, block).astype(BF16).reshape(16, 16, CH)
    dcol_r[me] = dcol_s[me]
    send(dcol_x, lambda e: dcol_s.at[e], dcol_r)

    bg_pass.wait()
    for q in range(chips):
        bg_t[q] = (bg_s[q, core].astype(F32) + bg_x[q].astype(F32)).astype(BF16)
    bg_r[chip] = bg_t[chip]
    each_chip(lambda q: copy(bg_x_, bg_t.at[q], bg_r.at[chip], 2 * q + core).start())
    sent.append((bg_x_, bg_r.at[pl.ds(0, chips - 1)]))

    g_in = nn(dproj_ref[0], cols_ref[0])
    g_out = nn(gated_ref[0], cotc_ref[0])
    for j in range(1, COLS):
        g_in += nn(dproj_ref[j], cols_ref[j])
        g_out += nn(gated_ref[j], cotc_ref[j])
    par_f[...] = jnp.zeros_like(par_f)
    for e in range(group):
        par_f[16 * e : 16 * e + 8, :] = g_in[8 * e : 8 * e + 8]
    par_f[pl.ds(8, group, stride=16), :] = g_out[:group]
    par_f[pl.ds(9, group, stride=16), :] = g_out[group:]
    par_s[...] = par_f[...].astype(BF16).reshape(chips, 2, 16, CH)
    par_pass = copy(par_w, par_s.at[:, 1 - core], par_x, twin)
    par_pass.start()
    par_pass.wait()
    for q in range(chips):
        par_t[q] = (par_s[q, core].astype(F32) + par_x[q].astype(F32)).astype(BF16)
    par_r[chip] = par_t[chip]
    each_chip(lambda q: copy(par_x_, par_t.at[q], par_r.at[chip], 2 * q + core).start())
    sent.append((par_x_, par_r.at[pl.ds(0, chips - 1)]))

    wait_recv(bg_x_, bg_r.at[pl.ds(0, chips - 1)])
    bsum = bg_r[0].astype(F32)
    for s in range(1, chips):
        bsum += bg_r[s].astype(F32)
    bsum = bsum.astype(BF16)
    wait_recv(dcol_x, dcol_r.at[pl.ds(0, group - 1)])
    for b in range(4):
        got = nn(erc_rec, dcol_r[16 * b : 16 * b + 16].reshape(256, CH)).astype(BF16)
        for r in range(ROWS):
            tmp_ref[r, 64 * b : 64 * b + 64, :] = got[64 * r : 64 * r + 64]
    gwb = jnp.zeros((16, CH), F32)
    grad_gain = jnp.zeros((1, CH), F32)
    grad_shift = jnp.zeros((1, CH), F32)
    for r in range(ROWS):
        normed = normed_ref[r]
        dn = tmp_ref[r].astype(F32) + tn(bsum, wbr[r])
        att_ref[r, 0:CH, 0:CH] = dn[0:CH]
        att_ref[r, 0:CH, CH:] = dn[CH:]
        gwb += jnp.where((row_of >> 2) == r, nn(bsum, np_ref[r]), 0.0)
        grad_gain += jnp.sum(dn * normed, 0, keepdims=True)
        grad_shift += jnp.sum(dn, 0, keepdims=True)
    small_s[...] = jnp.zeros_like(small_s)
    small_s[0:4, :] = gwb[0:4] + gwb[4:8] + gwb[8:12] + gwb[12:16]
    small_s[4:5, :] = grad_gain
    small_s[5:6, :] = grad_shift
    small_r[me] = small_s[...]
    send(small_x, lambda e: small_s, small_r)

    wait_recv(par_x_, par_r.at[pl.ds(0, chips - 1)])
    total = par_r[0].astype(F32)
    for s in range(1, chips):
        total += par_r[s].astype(F32)
    sum_r[chip, core] = total.astype(BF16)
    each_chip(
        lambda q: copy(sum_x, sum_r.at[chip, core], sum_r.at[chip, core], 2 * q + core).start()
    )
    sent.append((sum_x, sum_r.at[pl.ds(0, chips - 1), 0]))

    for r in range(ROWS):
        normed = normed_ref[r]
        dn = jnp.concatenate([att_ref[r, 0:CH, 0:CH], att_ref[r, 0:CH, CH:]], 0)
        scaled = dn * gain
        mean_s = jnp.mean(scaled, -1, keepdims=True)
        mean_sn = jnp.mean(scaled * normed, -1, keepdims=True)
        gp_ref[r] = (inv_ref[r] * (scaled - mean_s - normed * mean_sn)).astype(BF16)

    stores[1].start()

    wait_recv(upd_x, upd_r.at[pl.ds(0, group - 1)])
    for b in range(4):
        got = nn(erc_rec, upd_r[16 * b : 16 * b + 16].reshape(256, CH)).astype(BF16)
        for r in range(ROWS):
            upd_ref[r, 64 * b : 64 * b + 64, :] = got[64 * r : 64 * r + 64]
    stores[0].start()

    wait_recv(sum_x, sum_r.at[pl.ds(0, chips - 1), 0])
    sum_pass = copy(sum_w, sum_r.at[:, core], sum_r.at[:, core], twin)
    sum_pass.start()

    wait_recv(small_x, small_r.at[pl.ds(0, group - 1)])
    small = small_r[0]
    for s in range(1, group):
        small += small_r[s]
    gwb_ref[...] = small[0:HEADS]
    gg_ref[...] = small[4:5]
    gs_ref[...] = small[5:6]
    for n in (4, 5, 6):
        stores[n].start()

    sum_pass.wait()
    par_f[...] = sum_r[...].astype(F32).reshape(group * 16, CH)
    gwo_ref[0:group, :] = par_f[pl.ds(8, group, stride=16), :]
    gwo_ref[group:, :] = par_f[pl.ds(9, group, stride=16), :]
    stores[3].start()
    for q in range(4):
        part = jnp.concatenate(
            [par_f[16 * e : 16 * e + 8, :] for e in range(16 * q, 16 * q + 16)], 0
        )
        gwin_ref[:, CH * q : CH * q + CH] = jnp.transpose(part)
    stores[2].start()

    for which, part in sent:
        wait_send(which, part)
    for store in stores:
        store.wait()


def finish(*refs):
    count = 7
    sources, results, held = refs[:count], refs[count : 2 * count], refs[2 * count : 3 * count]
    in_sem, out_sem = refs[3 * count :]
    loads = [pltpu.make_async_copy(sources[n], held[n], in_sem.at[n]) for n in range(count)]
    stores = [pltpu.make_async_copy(held[n], results[n], out_sem.at[n]) for n in range(count)]
    for load in loads:
        load.start()
    for load, store in zip(loads, stores):
        load.wait()
        store.start()
    for store in stores:
        store.wait()


def per_device(group, pair_state, cotangent, length, norm_gain, norm_shift, w_in, w_bias, w_out):
    vmem = pl.BlockSpec(memory_space=pltpu.VMEM)
    smem = pl.BlockSpec(memory_space=pltpu.SMEM)
    hbm = pl.BlockSpec(memory_space=pltpu.HBM)
    chips = group // 2
    block = (group, 16, CH)
    shapes = (
        jax.ShapeDtypeStruct((ROWS, N, CH), BF16),
        jax.ShapeDtypeStruct((ROWS, N, CH), BF16),
        jax.ShapeDtypeStruct((CH, 4 * CH), F32),
        jax.ShapeDtypeStruct((CH, CH), F32),
        jax.ShapeDtypeStruct((HEADS, CH), F32),
        jax.ShapeDtypeStruct((1, CH), F32),
        jax.ShapeDtypeStruct((1, CH), F32),
    )
    out = pl.pallas_call(
        functools.partial(kernel, group),
        out_shape=shapes,
        in_specs=[hbm, hbm, smem] + [hbm] * 5,
        out_specs=[hbm] * 7,
        scratch_shapes=[pltpu.VMEM(s.shape, s.dtype) for s in shapes]
        + [
            pltpu.VMEM((ROWS, N, CH), BF16),
            pltpu.VMEM((ROWS, N, CH), BF16),
            pltpu.VMEM((1, CH), F32),
            pltpu.VMEM((1, CH), F32),
            pltpu.VMEM((CH, 4 * CH), BF16),
            pltpu.VMEM((HEADS, CH), BF16),
            pltpu.VMEM((CH, CH), BF16),
            pltpu.VMEM((ROWS, N, CH), F32),
            pltpu.VMEM((ROWS, N, CH), F32),
            pltpu.VMEM((ROWS, N, CH), BF16),
            pltpu.VMEM(block, BF16),
            pltpu.VMEM(block, BF16),
            pltpu.VMEM(block, BF16),
            pltpu.VMEM(block, BF16),
            pltpu.VMEM((chips, 2, 16, N), BF16),
            pltpu.VMEM((COLS, N, CH), BF16),
            pltpu.VMEM((COLS, N, CH), BF16),
            pltpu.VMEM((HEADS, N, N), F32),
            pltpu.VMEM((COLS, 3 * CH, N), BF16),
            pltpu.VMEM((COLS, CH, N), F32),
            pltpu.VMEM((COLS, CH, N), F32),
            pltpu.VMEM((COLS, CH, N), BF16),
            pltpu.VMEM((COLS, CH, N), F32),
            pltpu.VMEM((COLS, 8, N), F32),
            pltpu.VMEM((COLS * HEADS, N, N), BF16),
            pltpu.VMEM((COLS, 4 * CH, N), BF16),
            pltpu.VMEM((HEADS, N, N), F32),
            pltpu.VMEM((COLS, N, CH), BF16),
            pltpu.VMEM(block, BF16),
            pltpu.VMEM(block, BF16),
            pltpu.VMEM(block, BF16),
            pltpu.VMEM(block, BF16),
            pltpu.VMEM((chips, 2, 16, N), BF16),
            pltpu.VMEM((chips, 16, N), BF16),
            pltpu.VMEM((chips, 16, N), BF16),
            pltpu.VMEM((chips, 16, N), BF16),
            pltpu.VMEM((group * 16, CH), F32),
            pltpu.VMEM((chips, 2, 16, CH), BF16),
            pltpu.VMEM((chips, 16, CH), BF16),
            pltpu.VMEM((chips, 16, CH), BF16),
            pltpu.VMEM((chips, 16, CH), BF16),
            pltpu.VMEM((chips, 2, 16, CH), BF16),
            pltpu.VMEM((8, CH), F32),
            pltpu.VMEM((group, 8, CH), F32),
            pltpu.SemaphoreType.DMA((7,)),
            pltpu.SemaphoreType.DMA((7,)),
            pltpu.SemaphoreType.DMA((13,)),
            pltpu.SemaphoreType.DMA((13,)),
        ],
        compiler_params=pltpu.CompilerParams(
            collective_id=0, has_side_effects=True, vmem_limit_bytes=60 * 2**20
        ),
    )(
        pair_state,
        cotangent,
        length,
        norm_gain.reshape(1, CH),
        norm_shift.reshape(1, CH),
        w_in,
        w_bias.T,
        w_out,
    )
    out = pl.pallas_call(
        finish,
        out_shape=shapes,
        in_specs=[hbm] * 7,
        out_specs=[hbm] * 7,
        scratch_shapes=[pltpu.VMEM(s.shape, s.dtype) for s in shapes]
        + [pltpu.SemaphoreType.DMA((7,)), pltpu.SemaphoreType.DMA((7,))],
        compiler_params=pltpu.CompilerParams(vmem_limit_bytes=60 * 2**20),
    )(*out)
    return (*out[:4], out[4].T, out[5].reshape(CH), out[6].reshape(CH))


def solution(mesh):
    split = P(("dp", "dap"), None, None)
    return jax.shard_map(
        functools.partial(per_device, mesh.shape["dap"]),
        mesh=mesh,
        in_specs=(split, split, P("dp"), P(), P(), P(), P(), P()),
        out_specs=(split, split, P("dp", None), P("dp", None), P("dp", None), P("dp"), P("dp")),
        check_vma=False,
    )
```

```python
import functools
import math

import jax
import jax.numpy as jnp
from jax import lax
from jax.experimental import pallas as pl
from jax.experimental.pallas import tpu as pltpu
from jax.sharding import PartitionSpec as P

EPS = 1e-05
NEG = -1000000000.0
LOG2E = 1.4426950408889634
MESH = pl.DeviceIdType.MESH
F32 = jnp.float32
BF16 = jnp.bfloat16
ROWS = 4
COLS = 4
HEADS = 4
DIM = 32
N = 256
CH = 128


def nn(a, b):
    return lax.dot_general(a, b, (((1,), (0,)), ((), ())), preferred_element_type=F32)


def nt(a, b):
    return lax.dot_general(a, b, (((1,), (1,)), ((), ())), preferred_element_type=F32)


def tn(a, b):
    return lax.dot_general(a, b, (((0,), (0,)), ((), ())), preferred_element_type=F32)


def place(source_of):
    o = lax.broadcasted_iota(jnp.int32, (256, 256), 0)
    i = lax.broadcasted_iota(jnp.int32, (256, 256), 1)
    return jnp.where(source_of(o) == i, 1.0, 0.0).astype(BF16)


def rec_to_erc(o):
    return ((o >> 2) & 3) * 64 + ((o >> 4) << 2) + (o & 3)


def erc_to_cer(o):
    return ((o >> 2) & 15) * 16 + (o & 3) * 4 + (o >> 6)


def erc_to_rec(o):
    return ((o >> 2) & 15) * 16 + (o >> 6) * 4 + (o & 3)


def cer_to_erc(o):
    return (o & 3) * 64 + (o >> 4) * 4 + ((o >> 2) & 3)


def kernel(
    group,
    x_hbm,
    cot_hbm,
    len_ref,
    gain_hbm,
    shift_hbm,
    win_hbm,
    wb_hbm,
    wo_hbm,
    upd_hbm,
    gp_hbm,
    gwin_hbm,
    gwo_hbm,
    gwb_hbm,
    gg_hbm,
    gs_hbm,
    upd_ref,
    gp_ref,
    gwin_ref,
    gwo_ref,
    gwb_ref,
    gg_ref,
    gs_ref,
    x_ref,
    cot_ref,
    gain_ref,
    shift_ref,
    win_ref,
    wb_ref,
    wo_ref,
    normed_ref,
    inv_ref,
    np_ref,
    high_ref,
    low_ref,
    dn_ref,
    pair_s,
    pair_r,
    cot_s,
    cot_r,
    bias_r,
    cols_ref,
    cotc_ref,
    biasm_ref,
    proj_ref,
    gate_ref,
    dgate_ref,
    gated_ref,
    att_ref,
    tot_ref,
    p_ref,
    dproj_ref,
    bacc_ref,
    tmp_ref,
    upd_s,
    upd_r,
    dcol_s,
    dcol_r,
    bg_s,
    bg_x,
    bg_t,
    bg_r,
    gin_ref,
    par_f,
    par_s,
    par_x,
    par_t,
    par_r,
    sum_r,
    small_s,
    small_r,
    in_sem,
    out_sem,
    send_sem,
    recv_sem,
):
    me = lax.axis_index("dap")
    core = lax.rem(me, 2)
    chip = lax.div(me, 2)
    twin = me + 1 - 2 * core
    chips = group // 2
    cot_x, pair_x, bias_x, bias_w, bg_w, bg_x_, dcol_x, upd_x = 0, 1, 2, 3, 4, 6, 8, 9
    par_w, par_x_, sum_x, sum_w, small_x = 10, 11, 12, 13, 14

    loads = [
        pltpu.make_async_copy(src, dst, in_sem.at[n])
        for n, (src, dst) in enumerate(
            (
                (x_hbm, x_ref),
                (cot_hbm, cot_ref),
                (gain_hbm, gain_ref),
                (shift_hbm, shift_ref),
                (win_hbm, win_ref),
                (wb_hbm, wb_ref),
                (wo_hbm, wo_ref),
            )
        )
    ]
    for load in loads:
        load.start()

    stores = [
        pltpu.make_async_copy(src, dst, out_sem.at[n])
        for n, (src, dst) in enumerate(
            (
                (upd_ref, upd_hbm),
                (gp_ref, gp_hbm),
                (gwin_ref, gwin_hbm),
                (gwo_ref, gwo_hbm),
                (gwb_ref, gwb_hbm),
                (gg_ref, gg_hbm),
                (gs_ref, gs_hbm),
            )
        )
    ]

    y_at = lax.div(chip, 8)
    xs = [2 * lax.rem(lax.rem(lax.div(chip, 2), 4) + o, 4) for o in range(4)]
    zs = [lax.rem(lax.rem(chip, 2) + o, 2) for o in range(2)]
    around = [xs[x] + zs[z] for x in (2, 1, 3, 0) for z in (1, 0)]

    def row_at(n):
        return 8 * lax.rem(y_at + 2 - n + 3 * lax.div(n, 2) - 2 * lax.div(n, 3), 4)

    def each_chip(body):
        def step(n, carry):
            for offset in around:
                body(row_at(n) + offset)
            return carry

        lax.fori_loop(0, 3, step, 0)
        for offset in around[:-1]:
            body(8 * y_at + offset)

    def each_peer(body):
        def both(q):
            body(2 * q + 1 - core)
            body(2 * q + core)

        each_chip(both)
        body(twin)

    def near_peer(body):
        def step(t, carry):
            body(lax.rem(me + t, group))
            return carry

        lax.fori_loop(1, group, step, 0)

    def copy(which, src, dst, device):
        return pltpu.make_async_remote_copy(
            src_ref=src,
            dst_ref=dst,
            send_sem=send_sem.at[which],
            recv_sem=recv_sem.at[which],
            device_id={"dap": device},
            device_id_type=MESH,
        )

    sent = []

    def send(which, source_of, dest, order=each_peer):
        order(lambda e: copy(which, source_of(e), dest.at[me], e).start())
        sent.append((which, dest.at[pl.ds(0, group - 1)]))

    def wait_recv(which, part):
        pltpu.make_async_copy(part, part, recv_sem.at[which]).wait()

    def wait_send(which, part):
        pltpu.make_async_copy(part, part, send_sem.at[which]).wait()

    barrier = pltpu.get_barrier_semaphore()
    near_peer(
        lambda e: pl.semaphore_signal(barrier, inc=1, device_id={"dap": e}, device_id_type=MESH)
    )

    rec_erc = place(rec_to_erc)
    erc_cer = place(erc_to_cer)
    erc_rec = place(erc_to_rec)
    cer_erc = place(cer_to_erc)
    row_of = lax.broadcasted_iota(jnp.int32, (16, CH), 0)
    pick = jnp.where(
        (lax.broadcasted_iota(jnp.int32, (16, HEADS), 0) & 3)
        == lax.broadcasted_iota(jnp.int32, (16, HEADS), 1),
        1.0,
        0.0,
    ).astype(BF16)

    source = lax.broadcasted_iota(jnp.int32, (256, CH), 0)
    target = lax.broadcasted_iota(jnp.int32, (256, CH), 1)
    pick_in = jnp.where(
        (target >> 3) * 16 + (target & 7) == source, 1.0, 0.0
    ).astype(BF16)
    par_f[...] = jnp.zeros_like(par_f)
    row = lax.broadcasted_iota(jnp.int32, (16, 16), 0)
    col = lax.broadcasted_iota(jnp.int32, (16, 16), 1)
    heads_at = [
        [
            jnp.where(
                (((row & 3) >> 1) == pair) & ((row >> 2) * 4 + (row & 1) * 2 + half == col), 1.0, 0.0
            ).astype(BF16)
            for half in (0, 1)
        ]
        for pair in (0, 1)
    ]

    for load in loads:
        load.wait()
    gain = gain_ref[...]
    shift = shift_ref[...]
    wb16 = nn(pick, wb_ref[...])
    wbr = [jnp.where((row_of >> 2) == r, wb16, 0.0).astype(BF16) for r in range(ROWS)]
    bias = jnp.zeros((16, N), F32)
    for r in range(ROWS):
        x = x_ref[r].astype(F32)
        mean = jnp.mean(x, -1, keepdims=True)
        cen = x - mean
        var = jnp.mean(cen * cen, -1, keepdims=True)
        inv = lax.rsqrt(var + EPS)
        normed = cen * inv
        normed_ref[r] = normed
        inv_ref[r] = jnp.broadcast_to(inv, (N, CH))
        low = (normed * gain + shift).astype(BF16)
        np_ref[r] = low
        high = normed.astype(BF16)
        high_ref[r] = high
        low_ref[r] = (normed - high.astype(F32)).astype(BF16)
        bias += nt(wbr[r], low)
    for b in range(4):
        block = jnp.concatenate([np_ref[r, 64 * b : 64 * b + 64, :] for r in range(ROWS)], 0)
        pair_s[16 * b : 16 * b + 16] = nn(rec_erc, block).astype(BF16).reshape(16, 16, CH)
    for b in range(4):
        block = jnp.concatenate([cot_ref[r, 64 * b : 64 * b + 64, :] for r in range(ROWS)], 0)
        cot_s[16 * b : 16 * b + 16] = nn(rec_erc, block).astype(BF16).reshape(16, 16, CH)
    bias_r[chip, core] = bias.astype(BF16)
    pair_r[me] = pair_s[me]
    cot_r[me] = cot_s[me]

    pl.semaphore_wait(barrier, group - 1)

    each_chip(
        lambda q: copy(
            bias_x, bias_r.at[chip, core], bias_r.at[chip, core], 2 * q + core
        ).start()
    )
    sent.append((bias_x, bias_r.at[pl.ds(0, chips - 1), 0]))
    send(pair_x, lambda e: pair_s.at[e], pair_r)
    send(cot_x, lambda e: cot_s.at[e], cot_r)

    w_in = win_ref[...]
    w_in_t = jnp.transpose(w_in.astype(F32)).astype(BF16)
    w_out = wo_ref[...]

    wait_recv(bias_x, bias_r.at[pl.ds(0, chips - 1), 0])
    share = copy(bias_w, bias_r.at[:, core], bias_r.at[:, core], twin)
    share.start()

    wait_recv(pair_x, pair_r.at[pl.ds(0, group - 1)])
    for b in range(4):
        got = nn(erc_cer, pair_r[16 * b : 16 * b + 16].reshape(256, CH)).astype(BF16)
        for c in range(COLS):
            cols_ref[c, 64 * b : 64 * b + 64, :] = got[64 * c : 64 * c + 64]
    for j in range(COLS):
        projected = nt(w_in_t, cols_ref[j])
        proj_ref[j] = projected[: 3 * CH].astype(BF16)
        gate_ref[j] = jax.nn.sigmoid(projected[3 * CH :])

    share.wait()
    key = lax.broadcasted_iota(jnp.int32, (64, N), 0)
    for b in range(4):
        block = bias_r[8 * b : 8 * b + 8].reshape(256, N)
        got = nn(erc_cer, block) * LOG2E
        mask = jnp.where(key + 64 * b < len_ref[0], 0.0, NEG)
        for h in range(HEADS):
            biasm_ref[h, 64 * b : 64 * b + 64, :] = got[64 * h : 64 * h + 64] + mask

    scale = 1.0 / math.sqrt(DIM)

    def forward(j, carry):
        for h in range(HEADS):
            rows = slice(DIM * h, DIM * h + DIM)
            q = proj_ref[j, DIM * h : DIM * h + DIM, :]
            k = proj_ref[j, CH + DIM * h : CH + DIM * h + DIM, :]
            v = proj_ref[j, 2 * CH + DIM * h : 2 * CH + DIM * h + DIM, :]
            s = tn(k, q) * (scale * LOG2E) + biasm_ref[h]
            p = jnp.exp2(s - jnp.max(s, 0, keepdims=True))
            inv_total = 1.0 / jnp.sum(p, 0, keepdims=True)
            p_low = p.astype(BF16)
            p_ref[HEADS * j + h] = p_low
            att = nn(v, p_low) * inv_total
            att_ref[j, rows, :] = att
            tot_ref[j, h : h + 1, :] = inv_total
            gated_ref[j, rows, :] = (gate_ref[j, rows, :] * att).astype(BF16)
        return carry

    lax.fori_loop(0, COLS, forward, 0)

    wait_recv(cot_x, cot_r.at[pl.ds(0, group - 1)])
    for j in range(COLS):
        tmp_ref[j] = tn(gated_ref[j], w_out).astype(BF16)
    for b in range(4):
        block = jnp.concatenate([tmp_ref[j, 64 * b : 64 * b + 64, :] for j in range(COLS)], 0)
        upd_s[16 * b : 16 * b + 16] = nn(cer_erc, block).astype(BF16).reshape(16, 16, CH)
        got = nn(erc_cer, cot_r[16 * b : 16 * b + 16].reshape(256, CH)).astype(BF16)
        for c in range(COLS):
            cotc_ref[c, 64 * b : 64 * b + 64, :] = got[64 * c : 64 * c + 64]
    upd_r[me] = upd_s[me]
    for j in range(COLS):
        dgate_ref[j] = nt(w_out, cotc_ref[j])

    bacc_ref[...] = jnp.zeros_like(bacc_ref)

    def send_upd(e):
        copy(upd_x, upd_s.at[e], upd_r.at[me], e).start()

    def backward(j, heads):
        for h in heads:
            rows = slice(DIM * h, DIM * h + DIM)
            q = proj_ref[j, DIM * h : DIM * h + DIM, :]
            k = proj_ref[j, CH + DIM * h : CH + DIM * h + DIM, :]
            v = proj_ref[j, 2 * CH + DIM * h : 2 * CH + DIM * h + DIM, :]
            att = att_ref[j, rows, :]
            gate = gate_ref[j, rows, :]
            dgated = dgate_ref[j, rows, :]
            datt = ((dgated * gate) * tot_ref[j, h : h + 1, :]).astype(BF16)
            delta = jnp.sum(datt.astype(F32) * att, 0, keepdims=True)
            p_low = p_ref[HEADS * j + h]
            ds = p_low.astype(F32) * (tn(v, datt) - delta)
            bacc_ref[h] += ds
            ds_low = ds.astype(BF16)
            dq = nn(k, ds_low) * scale
            dk = nt(q, ds_low) * scale
            dv = nt(datt, p_low)
            dg = dgated * att * gate * (1.0 - gate)
            dproj_ref[j, DIM * h : DIM * h + DIM, :] = dq.astype(BF16)
            dproj_ref[j, CH + DIM * h : CH + DIM * h + DIM, :] = dk.astype(BF16)
            dproj_ref[j, 2 * CH + DIM * h : 2 * CH + DIM * h + DIM, :] = dv.astype(BF16)
            dproj_ref[j, 3 * CH + DIM * h : 3 * CH + DIM * h + DIM, :] = dg.astype(BF16)

    def gather_bias(pair):
        for b in range(4):
            block = jnp.concatenate(
                [
                    bacc_ref[h, 64 * b : 64 * b + 64, CH * half : CH * half + CH]
                    for h in (2 * pair, 2 * pair + 1)
                    for half in (0, 1)
                ],
                0,
            )
            got = nn(cer_erc, block.astype(BF16)).astype(BF16)
            bg_s[pair, 8 * b : 8 * b + 8] = got.reshape(8, 2, 16, CH)
        passing = copy(bg_w + pair, bg_s.at[pair, :, 1 - core], bg_x.at[pair], twin)
        passing.start()
        return passing

    def send_bias(pair, passing):
        passing.wait()
        for q in range(chips):
            bg_t[pair, q] = (
                bg_s[pair, q, core].astype(F32) + bg_x[pair, q].astype(F32)
            ).astype(BF16)
        bg_r[pair, chip] = bg_t[pair, chip]
        each_chip(
            lambda q: copy(
                bg_x_ + pair, bg_t.at[pair, q], bg_r.at[pair, chip], 2 * q + core
            ).start()
        )
        sent.append((bg_x_ + pair, bg_r.at[pair, pl.ds(0, chips - 1)]))

    def first_heads(j, carry):
        for offset in around[:-1]:
            send_upd(2 * (row_at(j) + offset) + 1 - core)
            send_upd(2 * (row_at(j) + offset) + core)
        backward(j, (0, 1))
        return carry

    lax.fori_loop(0, COLS, first_heads, 0)
    for n in range(3):
        send_upd(2 * (row_at(n) + around[-1]) + 1 - core)
        send_upd(2 * (row_at(n) + around[-1]) + core)
    send_upd(twin)
    sent.append((upd_x, upd_r.at[pl.ds(0, group - 1)]))

    passing = gather_bias(0)
    g_out = nn(gated_ref[0], cotc_ref[0])
    for j in range(1, COLS):
        g_out += nn(gated_ref[j], cotc_ref[j])
    par_f[pl.ds(8, group, stride=16), :] = g_out[:group]
    par_f[pl.ds(9, group, stride=16), :] = g_out[group:]

    def column_ends(j):
        tmp_ref[j] = jnp.transpose(nn(w_in, dproj_ref[j])).astype(BF16)
        g_in = nn(dproj_ref[j], cols_ref[j])
        if j == 0:
            gin_ref[...] = g_in
        else:
            gin_ref[...] += g_in

    backward(0, (2, 3))
    backward(1, (2, 3))
    column_ends(0)
    send_bias(0, passing)
    backward(2, (2, 3))
    column_ends(1)
    backward(3, (2, 3))
    column_ends(2)
    passing = gather_bias(1)
    column_ends(3)

    for b in range(4):
        block = jnp.concatenate([tmp_ref[j, 64 * b : 64 * b + 64, :] for j in range(COLS)], 0)
        dcol_s[16 * b : 16 * b + 16] = nn(cer_erc, block).astype(BF16).reshape(16, 16, CH)
    dcol_r[me] = dcol_s[me]

    for e in range(group):
        par_f[16 * e : 16 * e + 8, :] = gin_ref[8 * e : 8 * e + 8, :]
    par_s[...] = par_f[...].astype(BF16).reshape(chips, 2, 16, CH)
    par_pass = copy(par_w, par_s.at[:, 1 - core], par_x, twin)
    par_pass.start()
    send(dcol_x, lambda e: dcol_s.at[e], dcol_r)
    par_pass.wait()
    for q in range(chips):
        par_t[q] = (par_s[q, core].astype(F32) + par_x[q].astype(F32)).astype(BF16)
    par_r[chip] = par_t[chip]
    each_chip(lambda q: copy(par_x_, par_t.at[q], par_r.at[chip], 2 * q + core).start())
    sent.append((par_x_, par_r.at[pl.ds(0, chips - 1)]))
    send_bias(1, passing)

    wait_recv(upd_x, upd_r.at[pl.ds(0, group - 1)])
    for b in range(4):
        got = nn(erc_rec, upd_r[16 * b : 16 * b + 16].reshape(256, CH)).astype(BF16)
        for r in range(ROWS):
            upd_ref[r, 64 * b : 64 * b + 64, :] = got[64 * r : 64 * r + 64]
    stores[0].start()

    wait_recv(dcol_x, dcol_r.at[pl.ds(0, group - 1)])
    for b in range(4):
        got = nn(erc_rec, dcol_r[16 * b : 16 * b + 16].reshape(256, CH))
        for r in range(ROWS):
            dn_ref[r, 64 * b : 64 * b + 64, :] = got[64 * r : 64 * r + 64]
    grad_gain = jnp.zeros((1, CH), F32)
    grad_shift = jnp.zeros((1, CH), F32)
    for r in range(ROWS):
        grad_gain += jnp.sum(dn_ref[r] * normed_ref[r], 0, keepdims=True)
        grad_shift += jnp.sum(dn_ref[r], 0, keepdims=True)

    wait_recv(par_x_, par_r.at[pl.ds(0, chips - 1)])
    total = par_r[0].astype(F32)
    for s in range(1, chips):
        total += par_r[s].astype(F32)
    sum_r[chip, core] = total.astype(BF16)
    each_chip(
        lambda q: copy(sum_x, sum_r.at[chip, core], sum_r.at[chip, core], 2 * q + core).start()
    )
    sent.append((sum_x, sum_r.at[pl.ds(0, chips - 1), 0]))

    sums = []
    for pair in range(2):
        wait_recv(bg_x_ + pair, bg_r.at[pair, pl.ds(0, chips - 1)])
        bsum = bg_r[pair, 0].astype(F32)
        for s in range(1, chips):
            bsum += bg_r[pair, s].astype(F32)
        sums.append(bsum.astype(BF16))
    bsum = jnp.concatenate(
        [nn(heads_at[0][half], sums[0]) + nn(heads_at[1][half], sums[1]) for half in (0, 1)], 1
    ).astype(BF16)
    gwb = jnp.zeros((16, CH), F32)
    part = jnp.zeros((16, CH), F32)
    for r in range(ROWS):
        here = (row_of >> 2) == r
        gwb += jnp.where(here, nn(bsum, np_ref[r]), 0.0)
        part += jnp.where(here, nn(bsum, high_ref[r]) + nn(bsum, low_ref[r]), 0.0)
    grad_gain += jnp.sum(part * wb16, 0, keepdims=True)
    grad_shift += jnp.sum(jnp.sum(bsum.astype(F32), 1, keepdims=True) * wb16, 0, keepdims=True)
    small_s[0:4, :] = gwb[0:4] + gwb[4:8] + gwb[8:12] + gwb[12:16]
    small_s[4:5, :] = grad_gain
    small_s[5:6, :] = grad_shift
    small_r[me] = small_s[...]
    send(small_x, lambda e: small_s, small_r, near_peer)

    for r in range(ROWS):
        normed = normed_ref[r]
        scaled = (dn_ref[r] + tn(bsum, wbr[r])) * gain
        mean_s = jnp.mean(scaled, -1, keepdims=True)
        mean_sn = jnp.mean(scaled * normed, -1, keepdims=True)
        gp_ref[r] = (inv_ref[r] * (scaled - mean_s - normed * mean_sn)).astype(BF16)
    stores[1].start()

    wait_recv(sum_x, sum_r.at[pl.ds(0, chips - 1), 0])
    sum_pass = copy(sum_w, sum_r.at[:, core], sum_r.at[:, core], twin)
    sum_pass.start()
    sum_pass.wait()
    for q in range(4):
        rows = sum_r[8 * q : 8 * q + 8].reshape(256, CH)
        gwin_ref[:, CH * q : CH * q + CH] = tn(rows, pick_in)
    stores[2].start()
    par_f[...] = sum_r[...].astype(F32).reshape(group * 16, CH)
    gwo_ref[0:group, :] = par_f[pl.ds(8, group, stride=16), :]
    gwo_ref[group:, :] = par_f[pl.ds(9, group, stride=16), :]
    stores[3].start()

    wait_recv(small_x, small_r.at[pl.ds(0, group - 1)])
    small = small_r[0]
    for s in range(1, group):
        small += small_r[s]
    gwb_ref[...] = small[0:HEADS]
    gg_ref[...] = small[4:5]
    gs_ref[...] = small[5:6]
    for n in (4, 5, 6):
        stores[n].start()

    for which, part in sent:
        wait_send(which, part)
    for store in stores:
        store.wait()


def finish(*refs):
    count = 7
    sources, results, held = refs[:count], refs[count : 2 * count], refs[2 * count : 3 * count]
    in_sem, out_sem = refs[3 * count :]
    loads = [pltpu.make_async_copy(sources[n], held[n], in_sem.at[n]) for n in range(count)]
    stores = [pltpu.make_async_copy(held[n], results[n], out_sem.at[n]) for n in range(count)]
    for load in loads:
        load.start()
    for load, store in zip(loads, stores):
        load.wait()
        store.start()
    for store in stores:
        store.wait()


def per_device(group, pair_state, cotangent, length, norm_gain, norm_shift, w_in, w_bias, w_out):
    vmem = pl.BlockSpec(memory_space=pltpu.VMEM)
    smem = pl.BlockSpec(memory_space=pltpu.SMEM)
    hbm = pl.BlockSpec(memory_space=pltpu.HBM)
    chips = group // 2
    block = (group, 16, CH)
    shapes = (
        jax.ShapeDtypeStruct((ROWS, N, CH), BF16),
        jax.ShapeDtypeStruct((ROWS, N, CH), BF16),
        jax.ShapeDtypeStruct((CH, 4 * CH), F32),
        jax.ShapeDtypeStruct((CH, CH), F32),
        jax.ShapeDtypeStruct((HEADS, CH), F32),
        jax.ShapeDtypeStruct((1, CH), F32),
        jax.ShapeDtypeStruct((1, CH), F32),
    )
    out = pl.pallas_call(
        functools.partial(kernel, group),
        out_shape=shapes,
        in_specs=[hbm, hbm, smem] + [hbm] * 5,
        out_specs=[hbm] * 7,
        scratch_shapes=[pltpu.VMEM(s.shape, s.dtype) for s in shapes]
        + [
            pltpu.VMEM((ROWS, N, CH), BF16),
            pltpu.VMEM((ROWS, N, CH), BF16),
            pltpu.VMEM((1, CH), F32),
            pltpu.VMEM((1, CH), F32),
            pltpu.VMEM((CH, 4 * CH), BF16),
            pltpu.VMEM((HEADS, CH), BF16),
            pltpu.VMEM((CH, CH), BF16),
            pltpu.VMEM((ROWS, N, CH), F32),
            pltpu.VMEM((ROWS, N, CH), F32),
            pltpu.VMEM((ROWS, N, CH), BF16),
            pltpu.VMEM((ROWS, N, CH), BF16),
            pltpu.VMEM((ROWS, N, CH), BF16),
            pltpu.VMEM((ROWS, N, CH), F32),
            pltpu.VMEM(block, BF16),
            pltpu.VMEM(block, BF16),
            pltpu.VMEM(block, BF16),
            pltpu.VMEM(block, BF16),
            pltpu.VMEM((chips, 2, 16, N), BF16),
            pltpu.VMEM((COLS, N, CH), BF16),
            pltpu.VMEM((COLS, N, CH), BF16),
            pltpu.VMEM((HEADS, N, N), F32),
            pltpu.VMEM((COLS, 3 * CH, N), BF16),
            pltpu.VMEM((COLS, CH, N), F32),
            pltpu.VMEM((COLS, CH, N), F32),
            pltpu.VMEM((COLS, CH, N), BF16),
            pltpu.VMEM((COLS, CH, N), F32),
            pltpu.VMEM((COLS, 8, N), F32),
            pltpu.VMEM((COLS * HEADS, N, N), BF16),
            pltpu.VMEM((COLS, 4 * CH, N), BF16),
            pltpu.VMEM((HEADS, N, N), F32),
            pltpu.VMEM((COLS, N, CH), BF16),
            pltpu.VMEM(block, BF16),
            pltpu.VMEM(block, BF16),
            pltpu.VMEM(block, BF16),
            pltpu.VMEM(block, BF16),
            pltpu.VMEM((2, chips, 2, 16, CH), BF16),
            pltpu.VMEM((2, chips, 16, CH), BF16),
            pltpu.VMEM((2, chips, 16, CH), BF16),
            pltpu.VMEM((2, chips, 16, CH), BF16),
            pltpu.VMEM((4 * CH, CH), F32),
            pltpu.VMEM((group * 16, CH), F32),
            pltpu.VMEM((chips, 2, 16, CH), BF16),
            pltpu.VMEM((chips, 16, CH), BF16),
            pltpu.VMEM((chips, 16, CH), BF16),
            pltpu.VMEM((chips, 16, CH), BF16),
            pltpu.VMEM((chips, 2, 16, CH), BF16),
            pltpu.VMEM((6, CH), F32),
            pltpu.VMEM((group, 6, CH), F32),
            pltpu.SemaphoreType.DMA((7,)),
            pltpu.SemaphoreType.DMA((7,)),
            pltpu.SemaphoreType.DMA((15,)),
            pltpu.SemaphoreType.DMA((15,)),
        ],
        compiler_params=pltpu.CompilerParams(
            collective_id=0, has_side_effects=True, vmem_limit_bytes=60 * 2**20
        ),
    )(
        pair_state,
        cotangent,
        length,
        norm_gain.reshape(1, CH),
        norm_shift.reshape(1, CH),
        w_in,
        w_bias.T,
        w_out,
    )
    out = pl.pallas_call(
        finish,
        out_shape=shapes,
        in_specs=[hbm] * 7,
        out_specs=[hbm] * 7,
        scratch_shapes=[pltpu.VMEM(s.shape, s.dtype) for s in shapes]
        + [pltpu.SemaphoreType.DMA((7,)), pltpu.SemaphoreType.DMA((7,))],
        compiler_params=pltpu.CompilerParams(vmem_limit_bytes=60 * 2**20),
    )(*out)
    return (*out[:4], out[4].T, out[5].reshape(CH), out[6].reshape(CH))


def solution(mesh):
    split = P(("dp", "dap"), None, None)
    return jax.shard_map(
        functools.partial(per_device, mesh.shape["dap"]),
        mesh=mesh,
        in_specs=(split, split, P("dp"), P(), P(), P(), P(), P()),
        out_specs=(split, split, P("dp", None), P("dp", None), P("dp", None), P("dp"), P("dp")),
        check_vma=False,
    )
```

```python
import functools
import math

import jax
import jax.numpy as jnp
from jax import lax
from jax.experimental import pallas as pl
from jax.experimental.pallas import tpu as pltpu
from jax.sharding import PartitionSpec as P

EPS = 1e-05
NEG = -1000000000.0
LOG2E = 1.4426950408889634
MESH = pl.DeviceIdType.MESH
F32 = jnp.float32
BF16 = jnp.bfloat16
ROWS = 4
COLS = 4
HEADS = 4
DIM = 32
N = 256
CH = 128


def nn(a, b):
    return lax.dot_general(a, b, (((1,), (0,)), ((), ())), preferred_element_type=F32)


def nt(a, b):
    return lax.dot_general(a, b, (((1,), (1,)), ((), ())), preferred_element_type=F32)


def tn(a, b):
    return lax.dot_general(a, b, (((0,), (0,)), ((), ())), preferred_element_type=F32)


def place(source_of):
    o = lax.broadcasted_iota(jnp.int32, (256, 256), 0)
    i = lax.broadcasted_iota(jnp.int32, (256, 256), 1)
    return jnp.where(source_of(o) == i, 1.0, 0.0).astype(BF16)


def rec_to_erc(o):
    return ((o >> 2) & 3) * 64 + ((o >> 4) << 2) + (o & 3)


def erc_to_cer(o):
    return ((o >> 2) & 15) * 16 + (o & 3) * 4 + (o >> 6)


def erc_to_rec(o):
    return ((o >> 2) & 15) * 16 + (o >> 6) * 4 + (o & 3)


def cer_to_erc(o):
    return (o & 3) * 64 + (o >> 4) * 4 + ((o >> 2) & 3)


def kernel(
    group,
    x_hbm,
    cot_hbm,
    len_ref,
    gain_hbm,
    shift_hbm,
    win_hbm,
    wb_hbm,
    wo_hbm,
    upd_hbm,
    gp_hbm,
    gwin_hbm,
    gwo_hbm,
    gwb_hbm,
    gg_hbm,
    gs_hbm,
    upd_ref,
    gp_ref,
    gwin_ref,
    gwo_ref,
    gwb_ref,
    gg_ref,
    gs_ref,
    x_ref,
    cot_ref,
    gain_ref,
    shift_ref,
    win_ref,
    wb_ref,
    wo_ref,
    normed_ref,
    inv_ref,
    np_ref,
    high_ref,
    low_ref,
    dn_ref,
    pair_s,
    pair_r,
    cot_s,
    cot_r,
    bias_r,
    cols_ref,
    cotc_ref,
    biasm_ref,
    proj_ref,
    gate_ref,
    dgate_ref,
    gated_ref,
    att_ref,
    tot_ref,
    p_ref,
    dproj_ref,
    bacc_ref,
    tmp_ref,
    upd_s,
    upd_r,
    dcol_s,
    dcol_r,
    bg_s,
    bg_x,
    bg_t,
    bg_r,
    score_ref,
    datt_ref,
    delta_ref,
    ds_ref,
    par_f,
    par_s,
    par_x,
    par_t,
    par_r,
    sum_r,
    small_s,
    small_r,
    in_sem,
    out_sem,
    send_sem,
    recv_sem,
):
    me = lax.axis_index("dap")
    core = lax.rem(me, 2)
    chip = lax.div(me, 2)
    twin = me + 1 - 2 * core
    chips = group // 2
    cot_x, pair_x, bias_x, bias_w, bg_w, bg_x_, dcol_x, upd_x = 0, 1, 2, 3, 4, 6, 8, 9
    par_w, par_x_, sum_x, sum_w, small_x = 10, 11, 12, 13, 14

    loads = [
        pltpu.make_async_copy(src, dst, in_sem.at[n])
        for n, (src, dst) in enumerate(
            (
                (x_hbm, x_ref),
                (cot_hbm, cot_ref),
                (gain_hbm, gain_ref),
                (shift_hbm, shift_ref),
                (win_hbm, win_ref),
                (wb_hbm, wb_ref),
                (wo_hbm, wo_ref),
            )
        )
    ]
    for load in loads:
        load.start()

    stores = [
        pltpu.make_async_copy(src, dst, out_sem.at[n])
        for n, (src, dst) in enumerate(
            (
                (upd_ref, upd_hbm),
                (gp_ref, gp_hbm),
                (gwin_ref, gwin_hbm),
                (gwo_ref, gwo_hbm),
                (gwb_ref, gwb_hbm),
                (gg_ref, gg_hbm),
                (gs_ref, gs_hbm),
            )
        )
    ]

    y_at = lax.div(chip, 8)
    xs = [2 * lax.rem(lax.rem(lax.div(chip, 2), 4) + o, 4) for o in range(4)]
    zs = [lax.rem(lax.rem(chip, 2) + o, 2) for o in range(2)]
    around = [xs[x] + zs[z] for x in (2, 1, 3, 0) for z in (1, 0)]

    def row_at(n):
        return 8 * lax.rem(y_at + 2 - n + 3 * (n // 2) - 2 * (n // 3), 4)

    def each_chip(body):
        def step(n, carry):
            for offset in around:
                body(8 * lax.rem(y_at + 2 - n + 3 * lax.div(n, 2), 4) + offset)
            return carry

        lax.fori_loop(0, 3, step, 0)
        for offset in around[:-1]:
            body(8 * y_at + offset)

    def each_peer(body):
        def both(q):
            body(2 * q + 1 - core)
            body(2 * q + core)

        each_chip(both)
        body(twin)

    def near_peer(body):
        def step(t, carry):
            body(lax.rem(me + t, group))
            return carry

        lax.fori_loop(1, group, step, 0)

    def copy(which, src, dst, device):
        return pltpu.make_async_remote_copy(
            src_ref=src,
            dst_ref=dst,
            send_sem=send_sem.at[which],
            recv_sem=recv_sem.at[which],
            device_id={"dap": device},
            device_id_type=MESH,
        )

    sent = []

    def send(which, source_of, dest, order=each_peer):
        order(lambda e: copy(which, source_of(e), dest.at[me], e).start())
        sent.append((which, dest.at[pl.ds(0, group - 1)]))

    def wait_recv(which, part):
        pltpu.make_async_copy(part, part, recv_sem.at[which]).wait()

    def wait_send(which, part):
        pltpu.make_async_copy(part, part, send_sem.at[which]).wait()

    barrier = pltpu.get_barrier_semaphore()
    near_peer(
        lambda e: pl.semaphore_signal(barrier, inc=1, device_id={"dap": e}, device_id_type=MESH)
    )

    rec_erc = place(rec_to_erc)
    erc_cer = place(erc_to_cer)
    erc_rec = place(erc_to_rec)
    cer_erc = place(cer_to_erc)
    row_of = lax.broadcasted_iota(jnp.int32, (16, CH), 0)
    pick = jnp.where(
        (lax.broadcasted_iota(jnp.int32, (16, HEADS), 0) & 3)
        == lax.broadcasted_iota(jnp.int32, (16, HEADS), 1),
        1.0,
        0.0,
    ).astype(BF16)

    source = lax.broadcasted_iota(jnp.int32, (256, CH), 0)
    target = lax.broadcasted_iota(jnp.int32, (256, CH), 1)
    pick_in = jnp.where(
        (target >> 3) * 16 + (target & 7) == source, 1.0, 0.0
    ).astype(BF16)
    par_f[...] = jnp.zeros_like(par_f)
    row = lax.broadcasted_iota(jnp.int32, (16, 16), 0)
    col = lax.broadcasted_iota(jnp.int32, (16, 16), 1)
    heads_at = [
        [
            jnp.where(
                (((row & 3) >> 1) == pair) & ((row >> 2) * 4 + (row & 1) * 2 + half == col), 1.0, 0.0
            ).astype(BF16)
            for half in (0, 1)
        ]
        for pair in (0, 1)
    ]

    for load in loads:
        load.wait()
    gain = gain_ref[...]
    shift = shift_ref[...]
    wb16 = nn(pick, wb_ref[...])
    wbr = [jnp.where((row_of >> 2) == r, wb16, 0.0).astype(BF16) for r in range(ROWS)]
    bias = jnp.zeros((16, N), F32)
    for r in range(ROWS):
        x = x_ref[r].astype(F32)
        mean = jnp.mean(x, -1, keepdims=True)
        cen = x - mean
        var = jnp.mean(cen * cen, -1, keepdims=True)
        inv = lax.rsqrt(var + EPS)
        normed = cen * inv
        normed_ref[r] = normed
        inv_ref[r] = jnp.broadcast_to(inv, (N, CH))
        low = (normed * gain + shift).astype(BF16)
        np_ref[r] = low
        high = normed.astype(BF16)
        high_ref[r] = high
        low_ref[r] = (normed - high.astype(F32)).astype(BF16)
        bias += nt(wbr[r], low)
    for b in range(4):
        block = jnp.concatenate([np_ref[r, 64 * b : 64 * b + 64, :] for r in range(ROWS)], 0)
        pair_s[16 * b : 16 * b + 16] = nn(rec_erc, block).astype(BF16).reshape(16, 16, CH)
    for b in range(4):
        block = jnp.concatenate([cot_ref[r, 64 * b : 64 * b + 64, :] for r in range(ROWS)], 0)
        cot_s[16 * b : 16 * b + 16] = nn(rec_erc, block).astype(BF16).reshape(16, 16, CH)
    bias_r[chip, core] = bias.astype(BF16)
    pair_r[me] = pair_s[me]
    cot_r[me] = cot_s[me]

    pl.semaphore_wait(barrier, group - 1)

    each_chip(
        lambda q: copy(
            bias_x, bias_r.at[chip, core], bias_r.at[chip, core], 2 * q + core
        ).start()
    )
    sent.append((bias_x, bias_r.at[pl.ds(0, chips - 1), 0]))
    send(pair_x, lambda e: pair_s.at[e], pair_r)
    send(cot_x, lambda e: cot_s.at[e], cot_r)

    w_in = win_ref[...]
    w_in_t = jnp.transpose(w_in.astype(F32)).astype(BF16)
    w_out = wo_ref[...]

    wait_recv(bias_x, bias_r.at[pl.ds(0, chips - 1), 0])
    share = copy(bias_w, bias_r.at[:, core], bias_r.at[:, core], twin)
    share.start()

    wait_recv(pair_x, pair_r.at[pl.ds(0, group - 1)])
    for b in range(4):
        got = nn(erc_cer, pair_r[16 * b : 16 * b + 16].reshape(256, CH)).astype(BF16)
        for c in range(COLS):
            cols_ref[c, 64 * b : 64 * b + 64, :] = got[64 * c : 64 * c + 64]
    for j in range(COLS):
        projected = nt(w_in_t, cols_ref[j])
        proj_ref[j] = projected[: 3 * CH].astype(BF16)
        gate_ref[j] = jax.nn.sigmoid(projected[3 * CH :])

    share.wait()
    key = lax.broadcasted_iota(jnp.int32, (64, N), 0)
    for b in range(4):
        block = bias_r[8 * b : 8 * b + 8].reshape(256, N)
        got = nn(erc_cer, block) * LOG2E
        mask = jnp.where(key + 64 * b < len_ref[0], 0.0, NEG)
        for h in range(HEADS):
            biasm_ref[h, 64 * b : 64 * b + 64, :] = got[64 * h : 64 * h + 64] + mask

    scale = 1.0 / math.sqrt(DIM)

    units = [(j, h) for j in range(COLS) for h in range(HEADS)]

    def part_of(which, j, h):
        first = CH * which + DIM * h
        return proj_ref[j, first : first + DIM, :]

    for j, h in units:
        raw = tn(part_of(1, j, h), part_of(0, j, h))
        score_ref[HEADS * j + h] = raw * (scale * LOG2E) + biasm_ref[h]
    for j, h in units:
        score = score_ref[HEADS * j + h]
        p = jnp.exp2(score - jnp.max(score, 0, keepdims=True))
        tot_ref[j, h : h + 1, :] = 1.0 / jnp.sum(p, 0, keepdims=True)
        p_ref[HEADS * j + h] = p.astype(BF16)
    for j, h in units:
        rows = slice(DIM * h, DIM * h + DIM)
        att = nn(part_of(2, j, h), p_ref[HEADS * j + h]) * tot_ref[j, h : h + 1, :]
        att_ref[j, rows, :] = att
        gated_ref[j, rows, :] = (gate_ref[j, rows, :] * att).astype(BF16)

    wait_recv(cot_x, cot_r.at[pl.ds(0, group - 1)])
    for j in range(COLS):
        tmp_ref[j] = tn(gated_ref[j], w_out).astype(BF16)
    for b in range(4):
        block = jnp.concatenate([tmp_ref[j, 64 * b : 64 * b + 64, :] for j in range(COLS)], 0)
        upd_s[16 * b : 16 * b + 16] = nn(cer_erc, block).astype(BF16).reshape(16, 16, CH)
        got = nn(erc_cer, cot_r[16 * b : 16 * b + 16].reshape(256, CH)).astype(BF16)
        for c in range(COLS):
            cotc_ref[c, 64 * b : 64 * b + 64, :] = got[64 * c : 64 * c + 64]
    upd_r[me] = upd_s[me]
    for j in range(COLS):
        dgate_ref[j] = nt(w_out, cotc_ref[j])

    def send_upd(e):
        copy(upd_x, upd_s.at[e], upd_r.at[me], e).start()

    def score_grads(heads):
        for j in range(COLS):
            for h in heads:
                rows = slice(DIM * h, DIM * h + DIM)
                att = att_ref[j, rows, :]
                gate = gate_ref[j, rows, :]
                dgated = dgate_ref[j, rows, :]
                datt = ((dgated * gate) * tot_ref[j, h : h + 1, :]).astype(BF16)
                datt_ref[j, rows, :] = datt
                delta_ref[j, h : h + 1, :] = jnp.sum(datt.astype(F32) * att, 0, keepdims=True)
                dg = dgated * att * gate * (1.0 - gate)
                dproj_ref[j, 3 * CH + DIM * h : 3 * CH + DIM * h + DIM, :] = dg.astype(BF16)
        for h in heads:
            for j in range(COLS):
                rows = slice(DIM * h, DIM * h + DIM)
                dweights = tn(part_of(2, j, h), datt_ref[j, rows, :])
                p = p_ref[HEADS * j + h].astype(F32)
                ds = p * (dweights - delta_ref[j, h : h + 1, :])
                if j == 0:
                    bacc_ref[h] = ds
                else:
                    bacc_ref[h] += ds
                ds_ref[HEADS * j + h] = ds.astype(BF16)

    def input_grads(heads):
        for which in range(3):
            for j in range(COLS):
                for h in heads:
                    ds = ds_ref[HEADS * j + h]
                    if which == 0:
                        grad = nn(part_of(1, j, h), ds) * scale
                    elif which == 1:
                        grad = nt(part_of(0, j, h), ds) * scale
                    else:
                        rows = slice(DIM * h, DIM * h + DIM)
                        grad = nt(datt_ref[j, rows, :], p_ref[HEADS * j + h])
                    first = CH * which + DIM * h
                    dproj_ref[j, first : first + DIM, :] = grad.astype(BF16)

    def gather_bias(pair):
        for b in range(4):
            block = jnp.concatenate(
                [
                    bacc_ref[h, 64 * b : 64 * b + 64, CH * half : CH * half + CH]
                    for h in (2 * pair, 2 * pair + 1)
                    for half in (0, 1)
                ],
                0,
            )
            got = nn(cer_erc, block.astype(BF16)).astype(BF16)
            bg_s[pair, 8 * b : 8 * b + 8] = got.reshape(8, 2, 16, CH)
        passing = copy(bg_w + pair, bg_s.at[pair, :, 1 - core], bg_x.at[pair], twin)
        passing.start()
        return passing

    def send_bias(pair, passing):
        passing.wait()
        for q in range(chips):
            bg_t[pair, q] = (
                bg_s[pair, q, core].astype(F32) + bg_x[pair, q].astype(F32)
            ).astype(BF16)
        bg_r[pair, chip] = bg_t[pair, chip]
        each_chip(
            lambda q: copy(
                bg_x_ + pair, bg_t.at[pair, q], bg_r.at[pair, chip], 2 * q + core
            ).start()
        )
        sent.append((bg_x_ + pair, bg_r.at[pair, pl.ds(0, chips - 1)]))

    for j in range(COLS):
        for offset in around[:-1]:
            send_upd(2 * (row_at(j) + offset) + 1 - core)
            send_upd(2 * (row_at(j) + offset) + core)
    for n in range(3):
        send_upd(2 * (row_at(n) + around[-1]) + 1 - core)
        send_upd(2 * (row_at(n) + around[-1]) + core)
    send_upd(twin)
    sent.append((upd_x, upd_r.at[pl.ds(0, group - 1)]))

    score_grads((0, 1))
    first_pass = gather_bias(0)
    score_grads((2, 3))
    second_pass = gather_bias(1)
    input_grads((0, 1))
    send_bias(0, first_pass)
    send_bias(1, second_pass)
    input_grads((2, 3))

    g_out = nn(gated_ref[0], cotc_ref[0])
    g_in = nn(dproj_ref[0], cols_ref[0])
    for j in range(1, COLS):
        g_out += nn(gated_ref[j], cotc_ref[j])
        g_in += nn(dproj_ref[j], cols_ref[j])
    par_f[pl.ds(8, group, stride=16), :] = g_out[:group]
    par_f[pl.ds(9, group, stride=16), :] = g_out[group:]
    for j in range(COLS):
        tmp_ref[j] = jnp.transpose(nn(w_in, dproj_ref[j])).astype(BF16)

    for b in range(4):
        block = jnp.concatenate([tmp_ref[j, 64 * b : 64 * b + 64, :] for j in range(COLS)], 0)
        dcol_s[16 * b : 16 * b + 16] = nn(cer_erc, block).astype(BF16).reshape(16, 16, CH)
    dcol_r[me] = dcol_s[me]

    for e in range(group):
        par_f[16 * e : 16 * e + 8, :] = g_in[8 * e : 8 * e + 8]
    par_s[...] = par_f[...].astype(BF16).reshape(chips, 2, 16, CH)
    par_pass = copy(par_w, par_s.at[:, 1 - core], par_x, twin)
    par_pass.start()
    send(dcol_x, lambda e: dcol_s.at[e], dcol_r)
    par_pass.wait()
    for q in range(chips):
        par_t[q] = (par_s[q, core].astype(F32) + par_x[q].astype(F32)).astype(BF16)
    par_r[chip] = par_t[chip]
    each_chip(lambda q: copy(par_x_, par_t.at[q], par_r.at[chip], 2 * q + core).start())
    sent.append((par_x_, par_r.at[pl.ds(0, chips - 1)]))

    wait_recv(upd_x, upd_r.at[pl.ds(0, group - 1)])
    for b in range(4):
        got = nn(erc_rec, upd_r[16 * b : 16 * b + 16].reshape(256, CH)).astype(BF16)
        for r in range(ROWS):
            upd_ref[r, 64 * b : 64 * b + 64, :] = got[64 * r : 64 * r + 64]
    stores[0].start()

    wait_recv(dcol_x, dcol_r.at[pl.ds(0, group - 1)])
    for b in range(4):
        got = nn(erc_rec, dcol_r[16 * b : 16 * b + 16].reshape(256, CH))
        for r in range(ROWS):
            dn_ref[r, 64 * b : 64 * b + 64, :] = got[64 * r : 64 * r + 64]
    grad_gain = jnp.zeros((1, CH), F32)
    grad_shift = jnp.zeros((1, CH), F32)
    for r in range(ROWS):
        grad_gain += jnp.sum(dn_ref[r] * normed_ref[r], 0, keepdims=True)
        grad_shift += jnp.sum(dn_ref[r], 0, keepdims=True)

    wait_recv(par_x_, par_r.at[pl.ds(0, chips - 1)])
    total = par_r[0].astype(F32)
    for s in range(1, chips):
        total += par_r[s].astype(F32)
    sum_r[chip, core] = total.astype(BF16)
    each_chip(
        lambda q: copy(sum_x, sum_r.at[chip, core], sum_r.at[chip, core], 2 * q + core).start()
    )
    sent.append((sum_x, sum_r.at[pl.ds(0, chips - 1), 0]))

    sums = []
    for pair in range(2):
        wait_recv(bg_x_ + pair, bg_r.at[pair, pl.ds(0, chips - 1)])
        bsum = bg_r[pair, 0].astype(F32)
        for s in range(1, chips):
            bsum += bg_r[pair, s].astype(F32)
        sums.append(bsum.astype(BF16))
    bsum = jnp.concatenate(
        [nn(heads_at[0][half], sums[0]) + nn(heads_at[1][half], sums[1]) for half in (0, 1)], 1
    ).astype(BF16)
    gwb = jnp.zeros((16, CH), F32)
    part = jnp.zeros((16, CH), F32)
    for r in range(ROWS):
        here = (row_of >> 2) == r
        gwb += jnp.where(here, nn(bsum, np_ref[r]), 0.0)
        part += jnp.where(here, nn(bsum, high_ref[r]) + nn(bsum, low_ref[r]), 0.0)
    grad_gain += jnp.sum(part * wb16, 0, keepdims=True)
    grad_shift += jnp.sum(jnp.sum(bsum.astype(F32), 1, keepdims=True) * wb16, 0, keepdims=True)
    small_s[0:4, :] = gwb[0:4] + gwb[4:8] + gwb[8:12] + gwb[12:16]
    small_s[4:5, :] = grad_gain
    small_s[5:6, :] = grad_shift
    small_r[me] = small_s[...]
    send(small_x, lambda e: small_s, small_r, near_peer)

    for r in range(ROWS):
        normed = normed_ref[r]
        scaled = (dn_ref[r] + tn(bsum, wbr[r])) * gain
        mean_s = jnp.mean(scaled, -1, keepdims=True)
        mean_sn = jnp.mean(scaled * normed, -1, keepdims=True)
        gp_ref[r] = (inv_ref[r] * (scaled - mean_s - normed * mean_sn)).astype(BF16)
    stores[1].start()

    wait_recv(sum_x, sum_r.at[pl.ds(0, chips - 1), 0])
    sum_pass = copy(sum_w, sum_r.at[:, core], sum_r.at[:, core], twin)
    sum_pass.start()
    sum_pass.wait()
    for q in range(4):
        rows = sum_r[8 * q : 8 * q + 8].reshape(256, CH)
        gwin_ref[:, CH * q : CH * q + CH] = tn(rows, pick_in)
    stores[2].start()
    par_f[...] = sum_r[...].astype(F32).reshape(group * 16, CH)
    gwo_ref[0:group, :] = par_f[pl.ds(8, group, stride=16), :]
    gwo_ref[group:, :] = par_f[pl.ds(9, group, stride=16), :]
    stores[3].start()

    wait_recv(small_x, small_r.at[pl.ds(0, group - 1)])
    small = small_r[0]
    for s in range(1, group):
        small += small_r[s]
    gwb_ref[...] = small[0:HEADS]
    gg_ref[...] = small[4:5]
    gs_ref[...] = small[5:6]
    for n in (4, 5, 6):
        stores[n].start()

    for which, part in sent:
        wait_send(which, part)
    for store in stores:
        store.wait()


def finish(*refs):
    count = 7
    sources, results, held = refs[:count], refs[count : 2 * count], refs[2 * count : 3 * count]
    in_sem, out_sem = refs[3 * count :]
    loads = [pltpu.make_async_copy(sources[n], held[n], in_sem.at[n]) for n in range(count)]
    stores = [pltpu.make_async_copy(held[n], results[n], out_sem.at[n]) for n in range(count)]
    for load in loads:
        load.start()
    for load, store in zip(loads, stores):
        load.wait()
        store.start()
    for store in stores:
        store.wait()


def per_device(group, pair_state, cotangent, length, norm_gain, norm_shift, w_in, w_bias, w_out):
    vmem = pl.BlockSpec(memory_space=pltpu.VMEM)
    smem = pl.BlockSpec(memory_space=pltpu.SMEM)
    hbm = pl.BlockSpec(memory_space=pltpu.HBM)
    chips = group // 2
    block = (group, 16, CH)
    shapes = (
        jax.ShapeDtypeStruct((ROWS, N, CH), BF16),
        jax.ShapeDtypeStruct((ROWS, N, CH), BF16),
        jax.ShapeDtypeStruct((CH, 4 * CH), F32),
        jax.ShapeDtypeStruct((CH, CH), F32),
        jax.ShapeDtypeStruct((HEADS, CH), F32),
        jax.ShapeDtypeStruct((1, CH), F32),
        jax.ShapeDtypeStruct((1, CH), F32),
    )
    out = pl.pallas_call(
        functools.partial(kernel, group),
        out_shape=shapes,
        in_specs=[hbm, hbm, smem] + [hbm] * 5,
        out_specs=[hbm] * 7,
        scratch_shapes=[pltpu.VMEM(s.shape, s.dtype) for s in shapes]
        + [
            pltpu.VMEM((ROWS, N, CH), BF16),
            pltpu.VMEM((ROWS, N, CH), BF16),
            pltpu.VMEM((1, CH), F32),
            pltpu.VMEM((1, CH), F32),
            pltpu.VMEM((CH, 4 * CH), BF16),
            pltpu.VMEM((HEADS, CH), BF16),
            pltpu.VMEM((CH, CH), BF16),
            pltpu.VMEM((ROWS, N, CH), F32),
            pltpu.VMEM((ROWS, N, CH), F32),
            pltpu.VMEM((ROWS, N, CH), BF16),
            pltpu.VMEM((ROWS, N, CH), BF16),
            pltpu.VMEM((ROWS, N, CH), BF16),
            pltpu.VMEM((ROWS, N, CH), F32),
            pltpu.VMEM(block, BF16),
            pltpu.VMEM(block, BF16),
            pltpu.VMEM(block, BF16),
            pltpu.VMEM(block, BF16),
            pltpu.VMEM((chips, 2, 16, N), BF16),
            pltpu.VMEM((COLS, N, CH), BF16),
            pltpu.VMEM((COLS, N, CH), BF16),
            pltpu.VMEM((HEADS, N, N), F32),
            pltpu.VMEM((COLS, 3 * CH, N), BF16),
            pltpu.VMEM((COLS, CH, N), F32),
            pltpu.VMEM((COLS, CH, N), F32),
            pltpu.VMEM((COLS, CH, N), BF16),
            pltpu.VMEM((COLS, CH, N), F32),
            pltpu.VMEM((COLS, 8, N), F32),
            pltpu.VMEM((COLS * HEADS, N, N), BF16),
            pltpu.VMEM((COLS, 4 * CH, N), BF16),
            pltpu.VMEM((HEADS, N, N), F32),
            pltpu.VMEM((COLS, N, CH), BF16),
            pltpu.VMEM(block, BF16),
            pltpu.VMEM(block, BF16),
            pltpu.VMEM(block, BF16),
            pltpu.VMEM(block, BF16),
            pltpu.VMEM((2, chips, 2, 16, CH), BF16),
            pltpu.VMEM((2, chips, 16, CH), BF16),
            pltpu.VMEM((2, chips, 16, CH), BF16),
            pltpu.VMEM((2, chips, 16, CH), BF16),
            pltpu.VMEM((COLS * HEADS, N, N), F32),
            pltpu.VMEM((COLS, CH, N), BF16),
            pltpu.VMEM((COLS, 8, N), F32),
            pltpu.VMEM((COLS * HEADS, N, N), BF16),
            pltpu.VMEM((group * 16, CH), F32),
            pltpu.VMEM((chips, 2, 16, CH), BF16),
            pltpu.VMEM((chips, 16, CH), BF16),
            pltpu.VMEM((chips, 16, CH), BF16),
            pltpu.VMEM((chips, 16, CH), BF16),
            pltpu.VMEM((chips, 2, 16, CH), BF16),
            pltpu.VMEM((6, CH), F32),
            pltpu.VMEM((group, 6, CH), F32),
            pltpu.SemaphoreType.DMA((7,)),
            pltpu.SemaphoreType.DMA((7,)),
            pltpu.SemaphoreType.DMA((15,)),
            pltpu.SemaphoreType.DMA((15,)),
        ],
        compiler_params=pltpu.CompilerParams(
            collective_id=0, has_side_effects=True, vmem_limit_bytes=60 * 2**20
        ),
    )(
        pair_state,
        cotangent,
        length,
        norm_gain.reshape(1, CH),
        norm_shift.reshape(1, CH),
        w_in,
        w_bias.T,
        w_out,
    )
    out = pl.pallas_call(
        finish,
        out_shape=shapes,
        in_specs=[hbm] * 7,
        out_specs=[hbm] * 7,
        scratch_shapes=[pltpu.VMEM(s.shape, s.dtype) for s in shapes]
        + [pltpu.SemaphoreType.DMA((7,)), pltpu.SemaphoreType.DMA((7,))],
        compiler_params=pltpu.CompilerParams(vmem_limit_bytes=60 * 2**20),
    )(*out)
    return (*out[:4], out[4].T, out[5].reshape(CH), out[6].reshape(CH))


def solution(mesh):
    split = P(("dp", "dap"), None, None)
    return jax.shard_map(
        functools.partial(per_device, mesh.shape["dap"]),
        mesh=mesh,
        in_specs=(split, split, P("dp"), P(), P(), P(), P(), P()),
        out_specs=(split, split, P("dp", None), P("dp", None), P("dp", None), P("dp"), P("dp")),
        check_vma=False,
    )
```

```python
import functools
import math

import jax
import jax.numpy as jnp
from jax import lax
from jax.experimental import pallas as pl
from jax.experimental.pallas import tpu as pltpu
from jax.sharding import PartitionSpec as P

EPS = 1e-05
NEG = -1000000000.0
LOG2E = 1.4426950408889634
MESH = pl.DeviceIdType.MESH
F32 = jnp.float32
BF16 = jnp.bfloat16
ROWS = 4
COLS = 4
HEADS = 4
DIM = 32
N = 256
CH = 128


def nn(a, b):
    return lax.dot_general(a, b, (((1,), (0,)), ((), ())), preferred_element_type=F32)


def nt(a, b):
    return lax.dot_general(a, b, (((1,), (1,)), ((), ())), preferred_element_type=F32)


def tn(a, b):
    return lax.dot_general(a, b, (((0,), (0,)), ((), ())), preferred_element_type=F32)


def place(source_of):
    o = lax.broadcasted_iota(jnp.int32, (256, 256), 0)
    i = lax.broadcasted_iota(jnp.int32, (256, 256), 1)
    return jnp.where(source_of(o) == i, 1.0, 0.0).astype(BF16)


def rec_to_erc(o):
    return ((o >> 2) & 3) * 64 + ((o >> 4) << 2) + (o & 3)


def erc_to_cer(o):
    return ((o >> 2) & 15) * 16 + (o & 3) * 4 + (o >> 6)


def erc_to_rec(o):
    return ((o >> 2) & 15) * 16 + (o >> 6) * 4 + (o & 3)


def cer_to_erc(o):
    return (o & 3) * 64 + (o >> 4) * 4 + ((o >> 2) & 3)


def kernel(
    group,
    x_hbm,
    cot_hbm,
    len_ref,
    gain_hbm,
    shift_hbm,
    win_hbm,
    wb_hbm,
    wo_hbm,
    upd_hbm,
    gp_hbm,
    gwin_hbm,
    gwo_hbm,
    gwb_hbm,
    gg_hbm,
    gs_hbm,
    upd_ref,
    gp_ref,
    gwin_ref,
    gwo_ref,
    gwb_ref,
    gg_ref,
    gs_ref,
    x_ref,
    cot_ref,
    gain_ref,
    shift_ref,
    win_ref,
    wb_ref,
    wo_ref,
    normed_ref,
    inv_ref,
    np_ref,
    high_ref,
    low_ref,
    dn_ref,
    pair_s,
    pair_r,
    cot_s,
    cot_r,
    bias_r,
    cols_ref,
    cotc_ref,
    biasm_ref,
    proj_ref,
    gate_ref,
    dgate_ref,
    gated_ref,
    att_ref,
    tot_ref,
    p_ref,
    dproj_ref,
    bacc_ref,
    tmp_ref,
    upd_s,
    upd_r,
    dcol_s,
    dcol_r,
    bg_s,
    bg_x,
    bg_t,
    bg_r,
    score_ref,
    datt_ref,
    delta_ref,
    ds_ref,
    par_f,
    par_s,
    par_x,
    par_t,
    par_r,
    sum_r,
    small_s,
    small_r,
    in_sem,
    out_sem,
    send_sem,
    recv_sem,
):
    me = lax.axis_index("dap")
    core = lax.rem(me, 2)
    chip = lax.div(me, 2)
    twin = me + 1 - 2 * core
    chips = group // 2
    cot_x, pair_x, bias_x, bias_w, bg_w, bg_x_, dcol_x, upd_x = 0, 1, 2, 3, 4, 6, 8, 9
    par_w, par_x_, sum_x, sum_w, small_x = 10, 11, 12, 13, 14

    loads = [
        pltpu.make_async_copy(src, dst, in_sem.at[n])
        for n, (src, dst) in enumerate(
            (
                (x_hbm, x_ref),
                (cot_hbm, cot_ref),
                (gain_hbm, gain_ref),
                (shift_hbm, shift_ref),
                (win_hbm, win_ref),
                (wb_hbm, wb_ref),
                (wo_hbm, wo_ref),
            )
        )
    ]
    for load in loads:
        load.start()

    stores = [
        pltpu.make_async_copy(src, dst, out_sem.at[n])
        for n, (src, dst) in enumerate(
            (
                (upd_ref, upd_hbm),
                (gp_ref, gp_hbm),
                (gwin_ref, gwin_hbm),
                (gwo_ref, gwo_hbm),
                (gwb_ref, gwb_hbm),
                (gg_ref, gg_hbm),
                (gs_ref, gs_hbm),
            )
        )
    ]

    y_at = lax.div(chip, 8)
    xs = [2 * lax.rem(lax.rem(lax.div(chip, 2), 4) + o, 4) for o in range(4)]
    zs = [lax.rem(lax.rem(chip, 2) + o, 2) for o in range(2)]
    around = [xs[x] + zs[z] for x in (2, 1, 3, 0) for z in (1, 0)]

    def each_chip(body, first=0, stop=4):
        def step(n, carry):
            for offset in around:
                body(8 * lax.rem(y_at + 2 - n + 3 * lax.div(n, 2), 4) + offset)
            return carry

        lax.fori_loop(first, min(stop, 3), step, 0)
        if stop == 4:
            for offset in around[:-1]:
                body(8 * y_at + offset)

    def each_peer(body, first=0, stop=4):
        def both(q):
            body(2 * q + 1 - core)
            body(2 * q + core)

        each_chip(both, first, stop)
        if stop == 4:
            body(twin)

    def near_peer(body):
        def step(t, carry):
            body(lax.rem(me + t, group))
            return carry

        lax.fori_loop(1, group, step, 0)

    def copy(which, src, dst, device):
        return pltpu.make_async_remote_copy(
            src_ref=src,
            dst_ref=dst,
            send_sem=send_sem.at[which],
            recv_sem=recv_sem.at[which],
            device_id={"dap": device},
            device_id_type=MESH,
        )

    sent = []

    def send(which, source_of, dest, order=each_peer):
        order(lambda e: copy(which, source_of(e), dest.at[me], e).start())
        sent.append((which, dest.at[pl.ds(0, group - 1)]))

    def wait_recv(which, part):
        pltpu.make_async_copy(part, part, recv_sem.at[which]).wait()

    def wait_send(which, part):
        pltpu.make_async_copy(part, part, send_sem.at[which]).wait()

    barrier = pltpu.get_barrier_semaphore()
    near_peer(
        lambda e: pl.semaphore_signal(barrier, inc=1, device_id={"dap": e}, device_id_type=MESH)
    )

    rec_erc = place(rec_to_erc)
    row_of = lax.broadcasted_iota(jnp.int32, (16, CH), 0)
    pick = jnp.where(
        (lax.broadcasted_iota(jnp.int32, (16, HEADS), 0) & 3)
        == lax.broadcasted_iota(jnp.int32, (16, HEADS), 1),
        1.0,
        0.0,
    ).astype(BF16)

    for n in (0, 2, 3, 5):
        loads[n].wait()
    gain = gain_ref[...]
    shift = shift_ref[...]
    wb16 = nn(pick, wb_ref[...])
    wbr = [jnp.where((row_of >> 2) == r, wb16, 0.0).astype(BF16) for r in range(ROWS)]
    bias = jnp.zeros((16, N), F32)
    for r in range(ROWS):
        x = x_ref[r].astype(F32)
        mean = jnp.mean(x, -1, keepdims=True)
        cen = x - mean
        var = jnp.mean(cen * cen, -1, keepdims=True)
        inv = lax.rsqrt(var + EPS)
        normed = cen * inv
        normed_ref[r] = normed
        inv_ref[r] = jnp.broadcast_to(inv, (N, CH))
        low = (normed * gain + shift).astype(BF16)
        np_ref[r] = low
        bias += nt(wbr[r], low)
    bias_r[chip, core] = bias.astype(BF16)
    for b in range(4):
        block = jnp.concatenate([np_ref[r, 64 * b : 64 * b + 64, :] for r in range(ROWS)], 0)
        pair_s[16 * b : 16 * b + 16] = nn(rec_erc, block).astype(BF16).reshape(16, 16, CH)

    pl.semaphore_wait(barrier, group - 1)
    each_chip(
        lambda q: copy(
            bias_x, bias_r.at[chip, core], bias_r.at[chip, core], 2 * q + core
        ).start()
    )
    sent.append((bias_x, bias_r.at[pl.ds(0, chips - 1), 0]))
    send(pair_x, lambda e: pair_s.at[e], pair_r)
    pair_r[me] = pair_s[me]

    for n in (1, 4, 6):
        loads[n].wait()
    for b in range(4):
        block = jnp.concatenate([cot_ref[r, 64 * b : 64 * b + 64, :] for r in range(ROWS)], 0)
        cot_s[16 * b : 16 * b + 16] = nn(rec_erc, block).astype(BF16).reshape(16, 16, CH)
    send(cot_x, lambda e: cot_s.at[e], cot_r)
    cot_r[me] = cot_s[me]

    erc_cer = place(erc_to_cer)
    erc_rec = place(erc_to_rec)
    cer_erc = place(cer_to_erc)
    source = lax.broadcasted_iota(jnp.int32, (256, CH), 0)
    target = lax.broadcasted_iota(jnp.int32, (256, CH), 1)
    pick_in = jnp.where(
        (target >> 3) * 16 + (target & 7) == source, 1.0, 0.0
    ).astype(BF16)
    par_f[...] = jnp.zeros_like(par_f)
    row = lax.broadcasted_iota(jnp.int32, (16, 16), 0)
    col = lax.broadcasted_iota(jnp.int32, (16, 16), 1)
    heads_at = [
        [
            jnp.where(
                (((row & 3) >> 1) == pair) & ((row >> 2) * 4 + (row & 1) * 2 + half == col), 1.0, 0.0
            ).astype(BF16)
            for half in (0, 1)
        ]
        for pair in (0, 1)
    ]
    for r in range(ROWS):
        high = normed_ref[r].astype(BF16)
        high_ref[r] = high
        low_ref[r] = (normed_ref[r] - high.astype(F32)).astype(BF16)

    w_in = win_ref[...]
    w_in_t = jnp.transpose(w_in.astype(F32)).astype(BF16)
    w_out = wo_ref[...]

    wait_recv(bias_x, bias_r.at[pl.ds(0, chips - 1), 0])
    share = copy(bias_w, bias_r.at[:, core], bias_r.at[:, core], twin)
    share.start()

    wait_recv(pair_x, pair_r.at[pl.ds(0, group - 1)])
    for b in range(4):
        got = nn(erc_cer, pair_r[16 * b : 16 * b + 16].reshape(256, CH)).astype(BF16)
        for c in range(COLS):
            cols_ref[c, 64 * b : 64 * b + 64, :] = got[64 * c : 64 * c + 64]
    for j in range(COLS):
        projected = nt(w_in_t, cols_ref[j])
        proj_ref[j] = projected[: 3 * CH].astype(BF16)
        gate_ref[j] = jax.nn.sigmoid(projected[3 * CH :])

    share.wait()
    key = lax.broadcasted_iota(jnp.int32, (64, N), 0)
    for b in range(4):
        block = bias_r[8 * b : 8 * b + 8].reshape(256, N)
        got = nn(erc_cer, block) * LOG2E
        mask = jnp.where(key + 64 * b < len_ref[0], 0.0, NEG)
        for h in range(HEADS):
            biasm_ref[h, 64 * b : 64 * b + 64, :] = got[64 * h : 64 * h + 64] + mask

    scale = 1.0 / math.sqrt(DIM)

    units = [(j, h) for j in range(COLS) for h in range(HEADS)]

    def part_of(which, j, h):
        first = CH * which + DIM * h
        return proj_ref[j, first : first + DIM, :]

    for j, h in units:
        raw = tn(part_of(1, j, h), part_of(0, j, h))
        score_ref[HEADS * j + h] = raw * (scale * LOG2E) + biasm_ref[h]
    for j, h in units:
        score = score_ref[HEADS * j + h]
        p = jnp.exp2(score - jnp.max(score, 0, keepdims=True))
        tot_ref[j, h : h + 1, :] = 1.0 / jnp.sum(p, 0, keepdims=True)
        p_ref[HEADS * j + h] = p.astype(BF16)
    for j, h in units:
        rows = slice(DIM * h, DIM * h + DIM)
        att = nn(part_of(2, j, h), p_ref[HEADS * j + h]) * tot_ref[j, h : h + 1, :]
        att_ref[j, rows, :] = att
        gated_ref[j, rows, :] = (gate_ref[j, rows, :] * att).astype(BF16)

    wait_recv(cot_x, cot_r.at[pl.ds(0, group - 1)])
    for b in range(4):
        got = nn(erc_cer, cot_r[16 * b : 16 * b + 16].reshape(256, CH)).astype(BF16)
        for c in range(COLS):
            cotc_ref[c, 64 * b : 64 * b + 64, :] = got[64 * c : 64 * c + 64]
    for j in range(COLS):
        dgate_ref[j] = nt(w_out, cotc_ref[j])

    def score_grads(heads):
        for j in range(COLS):
            for h in heads:
                rows = slice(DIM * h, DIM * h + DIM)
                att = att_ref[j, rows, :]
                gate = gate_ref[j, rows, :]
                dgated = dgate_ref[j, rows, :]
                datt = ((dgated * gate) * tot_ref[j, h : h + 1, :]).astype(BF16)
                datt_ref[j, rows, :] = datt
                delta_ref[j, h : h + 1, :] = jnp.sum(datt.astype(F32) * att, 0, keepdims=True)
                dg = dgated * att * gate * (1.0 - gate)
                dproj_ref[j, 3 * CH + DIM * h : 3 * CH + DIM * h + DIM, :] = dg.astype(BF16)
        for h in heads:
            for j in range(COLS):
                rows = slice(DIM * h, DIM * h + DIM)
                dweights = tn(part_of(2, j, h), datt_ref[j, rows, :])
                p = p_ref[HEADS * j + h].astype(F32)
                ds = p * (dweights - delta_ref[j, h : h + 1, :])
                if j == 0:
                    bacc_ref[h] = ds
                else:
                    bacc_ref[h] += ds
                ds_ref[HEADS * j + h] = ds.astype(BF16)

    def input_grads(heads):
        for which in range(3):
            for j in range(COLS):
                for h in heads:
                    ds = ds_ref[HEADS * j + h]
                    if which == 0:
                        grad = nn(part_of(1, j, h), ds) * scale
                    elif which == 1:
                        grad = nt(part_of(0, j, h), ds) * scale
                    else:
                        rows = slice(DIM * h, DIM * h + DIM)
                        grad = nt(datt_ref[j, rows, :], p_ref[HEADS * j + h])
                    first = CH * which + DIM * h
                    dproj_ref[j, first : first + DIM, :] = grad.astype(BF16)

    def gather_bias(pair):
        for b in range(4):
            block = jnp.concatenate(
                [
                    bacc_ref[h, 64 * b : 64 * b + 64, CH * half : CH * half + CH]
                    for h in (2 * pair, 2 * pair + 1)
                    for half in (0, 1)
                ],
                0,
            )
            got = nn(cer_erc, block.astype(BF16)).astype(BF16)
            bg_s[8 * b : 8 * b + 8, :, 16 * pair : 16 * pair + 16] = got.reshape(8, 2, 16, CH)

    every = tuple(range(HEADS))
    score_grads(every)
    gather_bias(0)
    gather_bias(1)
    bg_pass = copy(bg_w, bg_s.at[:, 1 - core], bg_x, twin)
    bg_pass.start()
    input_grads((0, 1))
    bg_pass.wait()
    for q in range(chips):
        bg_t[q] = (bg_s[q, core].astype(F32) + bg_x[q].astype(F32)).astype(BF16)
    each_chip(lambda q: copy(bg_x_, bg_t.at[q], bg_r.at[chip], 2 * q + core).start())
    sent.append((bg_x_, bg_r.at[pl.ds(0, chips - 1)]))
    bg_r[chip] = bg_t[chip]
    input_grads((2, 3))

    g_out = nn(gated_ref[0], cotc_ref[0])
    g_in = nn(dproj_ref[0], cols_ref[0])
    for j in range(1, COLS):
        g_out += nn(gated_ref[j], cotc_ref[j])
        g_in += nn(dproj_ref[j], cols_ref[j])
    par_f[pl.ds(8, group, stride=16), :] = g_out[:group]
    par_f[pl.ds(9, group, stride=16), :] = g_out[group:]
    for e in range(group):
        par_f[16 * e : 16 * e + 8, :] = g_in[8 * e : 8 * e + 8]
    par_s[...] = par_f[...].astype(BF16).reshape(chips, 2, 16, CH)
    par_pass = copy(par_w, par_s.at[:, 1 - core], par_x, twin)
    par_pass.start()

    for j in range(COLS):
        tmp_ref[j] = jnp.transpose(nn(w_in, dproj_ref[j])).astype(BF16)
    for b in range(4):
        block = jnp.concatenate([tmp_ref[j, 64 * b : 64 * b + 64, :] for j in range(COLS)], 0)
        dcol_s[16 * b : 16 * b + 16] = nn(cer_erc, block).astype(BF16).reshape(16, 16, CH)

    def send_dcol(e):
        copy(dcol_x, dcol_s.at[e], dcol_r.at[me], e).start()

    each_peer(send_dcol, 0, 2)
    par_pass.wait()
    for q in range(chips):
        par_t[q] = (par_s[q, core].astype(F32) + par_x[q].astype(F32)).astype(BF16)
    each_chip(lambda q: copy(par_x_, par_t.at[q], par_r.at[chip], 2 * q + core).start())
    sent.append((par_x_, par_r.at[pl.ds(0, chips - 1)]))
    each_peer(send_dcol, 2, 4)
    sent.append((dcol_x, dcol_r.at[pl.ds(0, group - 1)]))
    par_r[chip] = par_t[chip]
    dcol_r[me] = dcol_s[me]

    for j in range(COLS):
        tmp_ref[j] = tn(gated_ref[j], w_out).astype(BF16)
    for b in range(4):
        block = jnp.concatenate([tmp_ref[j, 64 * b : 64 * b + 64, :] for j in range(COLS)], 0)
        upd_s[16 * b : 16 * b + 16] = nn(cer_erc, block).astype(BF16).reshape(16, 16, CH)
    send(upd_x, lambda e: upd_s.at[e], upd_r)
    upd_r[me] = upd_s[me]

    wait_recv(bg_x_, bg_r.at[pl.ds(0, chips - 1)])
    sums = bg_r[0].astype(F32)
    for s in range(1, chips):
        sums += bg_r[s].astype(F32)
    sums = sums.astype(BF16)
    bsum = jnp.concatenate(
        [nn(heads_at[0][half], sums[:16]) + nn(heads_at[1][half], sums[16:]) for half in (0, 1)],
        1,
    ).astype(BF16)
    gwb = jnp.zeros((16, CH), F32)
    part = jnp.zeros((16, CH), F32)
    for r in range(ROWS):
        here = (row_of >> 2) == r
        gwb += jnp.where(here, nn(bsum, np_ref[r]), 0.0)
        part += jnp.where(here, nn(bsum, high_ref[r]) + nn(bsum, low_ref[r]), 0.0)
    small_s[0:4, :] = gwb[0:4] + gwb[4:8] + gwb[8:12] + gwb[12:16]
    grad_gain = jnp.sum(part * wb16, 0, keepdims=True)
    grad_shift = jnp.sum(jnp.sum(bsum.astype(F32), 1, keepdims=True) * wb16, 0, keepdims=True)

    wait_recv(par_x_, par_r.at[pl.ds(0, chips - 1)])
    total = par_r[0].astype(F32)
    for s in range(1, chips):
        total += par_r[s].astype(F32)
    sum_r[chip, core] = total.astype(BF16)
    each_chip(
        lambda q: copy(sum_x, sum_r.at[chip, core], sum_r.at[chip, core], 2 * q + core).start()
    )
    sent.append((sum_x, sum_r.at[pl.ds(0, chips - 1), 0]))

    wait_recv(dcol_x, dcol_r.at[pl.ds(0, group - 1)])
    for b in range(4):
        got = nn(erc_rec, dcol_r[16 * b : 16 * b + 16].reshape(256, CH))
        for r in range(ROWS):
            dn_ref[r, 64 * b : 64 * b + 64, :] = got[64 * r : 64 * r + 64]
    for r in range(ROWS):
        grad_gain += jnp.sum(dn_ref[r] * normed_ref[r], 0, keepdims=True)
        grad_shift += jnp.sum(dn_ref[r], 0, keepdims=True)
    small_s[4:5, :] = grad_gain
    small_s[5:6, :] = grad_shift
    send(small_x, lambda e: small_s, small_r, near_peer)
    small_r[me] = small_s[...]

    for r in range(ROWS):
        normed = normed_ref[r]
        scaled = (dn_ref[r] + tn(bsum, wbr[r])) * gain
        mean_s = jnp.mean(scaled, -1, keepdims=True)
        mean_sn = jnp.mean(scaled * normed, -1, keepdims=True)
        gp_ref[r] = (inv_ref[r] * (scaled - mean_s - normed * mean_sn)).astype(BF16)
    stores[1].start()

    wait_recv(upd_x, upd_r.at[pl.ds(0, group - 1)])
    for b in range(4):
        got = nn(erc_rec, upd_r[16 * b : 16 * b + 16].reshape(256, CH)).astype(BF16)
        for r in range(ROWS):
            upd_ref[r, 64 * b : 64 * b + 64, :] = got[64 * r : 64 * r + 64]
    stores[0].start()

    wait_recv(sum_x, sum_r.at[pl.ds(0, chips - 1), 0])
    sum_pass = copy(sum_w, sum_r.at[:, core], sum_r.at[:, core], twin)
    sum_pass.start()
    sum_pass.wait()
    for q in range(4):
        rows = sum_r[8 * q : 8 * q + 8].reshape(256, CH)
        gwin_ref[:, CH * q : CH * q + CH] = tn(rows, pick_in)
    stores[2].start()
    par_f[...] = sum_r[...].astype(F32).reshape(group * 16, CH)
    gwo_ref[0:group, :] = par_f[pl.ds(8, group, stride=16), :]
    gwo_ref[group:, :] = par_f[pl.ds(9, group, stride=16), :]
    stores[3].start()

    wait_recv(small_x, small_r.at[pl.ds(0, group - 1)])
    small = small_r[0]
    for s in range(1, group):
        small += small_r[s]
    gwb_ref[...] = small[0:HEADS]
    gg_ref[...] = small[4:5]
    gs_ref[...] = small[5:6]
    for n in (4, 5, 6):
        stores[n].start()

    for which, part in sent:
        wait_send(which, part)
    for store in stores:
        store.wait()


def finish(*refs):
    count = 7
    sources, results, held = refs[:count], refs[count : 2 * count], refs[2 * count : 3 * count]
    in_sem, out_sem = refs[3 * count :]
    loads = [pltpu.make_async_copy(sources[n], held[n], in_sem.at[n]) for n in range(count)]
    stores = [pltpu.make_async_copy(held[n], results[n], out_sem.at[n]) for n in range(count)]
    for load in loads:
        load.start()
    for load, store in zip(loads, stores):
        load.wait()
        store.start()
    for store in stores:
        store.wait()


def per_device(group, pair_state, cotangent, length, norm_gain, norm_shift, w_in, w_bias, w_out):
    vmem = pl.BlockSpec(memory_space=pltpu.VMEM)
    smem = pl.BlockSpec(memory_space=pltpu.SMEM)
    hbm = pl.BlockSpec(memory_space=pltpu.HBM)
    chips = group // 2
    block = (group, 16, CH)
    shapes = (
        jax.ShapeDtypeStruct((ROWS, N, CH), BF16),
        jax.ShapeDtypeStruct((ROWS, N, CH), BF16),
        jax.ShapeDtypeStruct((CH, 4 * CH), F32),
        jax.ShapeDtypeStruct((CH, CH), F32),
        jax.ShapeDtypeStruct((HEADS, CH), F32),
        jax.ShapeDtypeStruct((1, CH), F32),
        jax.ShapeDtypeStruct((1, CH), F32),
    )
    out = pl.pallas_call(
        functools.partial(kernel, group),
        out_shape=shapes,
        in_specs=[hbm, hbm, smem] + [hbm] * 5,
        out_specs=[hbm] * 7,
        scratch_shapes=[pltpu.VMEM(s.shape, s.dtype) for s in shapes]
        + [
            pltpu.VMEM((ROWS, N, CH), BF16),
            pltpu.VMEM((ROWS, N, CH), BF16),
            pltpu.VMEM((1, CH), F32),
            pltpu.VMEM((1, CH), F32),
            pltpu.VMEM((CH, 4 * CH), BF16),
            pltpu.VMEM((HEADS, CH), BF16),
            pltpu.VMEM((CH, CH), BF16),
            pltpu.VMEM((ROWS, N, CH), F32),
            pltpu.VMEM((ROWS, N, CH), F32),
            pltpu.VMEM((ROWS, N, CH), BF16),
            pltpu.VMEM((ROWS, N, CH), BF16),
            pltpu.VMEM((ROWS, N, CH), BF16),
            pltpu.VMEM((ROWS, N, CH), F32),
            pltpu.VMEM(block, BF16),
            pltpu.VMEM(block, BF16),
            pltpu.VMEM(block, BF16),
            pltpu.VMEM(block, BF16),
            pltpu.VMEM((chips, 2, 16, N), BF16),
            pltpu.VMEM((COLS, N, CH), BF16),
            pltpu.VMEM((COLS, N, CH), BF16),
            pltpu.VMEM((HEADS, N, N), F32),
            pltpu.VMEM((COLS, 3 * CH, N), BF16),
            pltpu.VMEM((COLS, CH, N), F32),
            pltpu.VMEM((COLS, CH, N), F32),
            pltpu.VMEM((COLS, CH, N), BF16),
            pltpu.VMEM((COLS, CH, N), F32),
            pltpu.VMEM((COLS, 8, N), F32),
            pltpu.VMEM((COLS * HEADS, N, N), BF16),
            pltpu.VMEM((COLS, 4 * CH, N), BF16),
            pltpu.VMEM((HEADS, N, N), F32),
            pltpu.VMEM((COLS, N, CH), BF16),
            pltpu.VMEM(block, BF16),
            pltpu.VMEM(block, BF16),
            pltpu.VMEM(block, BF16),
            pltpu.VMEM(block, BF16),
            pltpu.VMEM((chips, 2, 32, CH), BF16),
            pltpu.VMEM((chips, 32, CH), BF16),
            pltpu.VMEM((chips, 32, CH), BF16),
            pltpu.VMEM((chips, 32, CH), BF16),
            pltpu.VMEM((COLS * HEADS, N, N), F32),
            pltpu.VMEM((COLS, CH, N), BF16),
            pltpu.VMEM((COLS, 8, N), F32),
            pltpu.VMEM((COLS * HEADS, N, N), BF16),
            pltpu.VMEM((group * 16, CH), F32),
            pltpu.VMEM((chips, 2, 16, CH), BF16),
            pltpu.VMEM((chips, 16, CH), BF16),
            pltpu.VMEM((chips, 16, CH), BF16),
            pltpu.VMEM((chips, 16, CH), BF16),
            pltpu.VMEM((chips, 2, 16, CH), BF16),
            pltpu.VMEM((6, CH), F32),
            pltpu.VMEM((group, 6, CH), F32),
            pltpu.SemaphoreType.DMA((7,)),
            pltpu.SemaphoreType.DMA((7,)),
            pltpu.SemaphoreType.DMA((15,)),
            pltpu.SemaphoreType.DMA((15,)),
        ],
        compiler_params=pltpu.CompilerParams(
            collective_id=0, has_side_effects=True, vmem_limit_bytes=60 * 2**20
        ),
    )(
        pair_state,
        cotangent,
        length,
        norm_gain.reshape(1, CH),
        norm_shift.reshape(1, CH),
        w_in,
        w_bias.T,
        w_out,
    )
    out = pl.pallas_call(
        finish,
        out_shape=shapes,
        in_specs=[hbm] * 7,
        out_specs=[hbm] * 7,
        scratch_shapes=[pltpu.VMEM(s.shape, s.dtype) for s in shapes]
        + [pltpu.SemaphoreType.DMA((7,)), pltpu.SemaphoreType.DMA((7,))],
        compiler_params=pltpu.CompilerParams(vmem_limit_bytes=60 * 2**20),
    )(*out)
    return (*out[:4], out[4].T, out[5].reshape(CH), out[6].reshape(CH))


def solution(mesh):
    split = P(("dp", "dap"), None, None)
    return jax.shard_map(
        functools.partial(per_device, mesh.shape["dap"]),
        mesh=mesh,
        in_specs=(split, split, P("dp"), P(), P(), P(), P(), P()),
        out_specs=(split, split, P("dp", None), P("dp", None), P("dp", None), P("dp"), P("dp")),
        check_vma=False,
    )
```

```python
import functools
import math

import jax
import jax.numpy as jnp
from jax import lax
from jax.experimental import pallas as pl
from jax.experimental.pallas import tpu as pltpu
from jax.sharding import PartitionSpec as P

EPS = 1e-05
NEG = -1000000000.0
LOG2E = 1.4426950408889634
MESH = pl.DeviceIdType.MESH
F32 = jnp.float32
BF16 = jnp.bfloat16
ROWS = 4
COLS = 4
HEADS = 4
DIM = 32
N = 256
CH = 128


def nn(a, b):
    return lax.dot_general(a, b, (((1,), (0,)), ((), ())), preferred_element_type=F32)


def nt(a, b):
    return lax.dot_general(a, b, (((1,), (1,)), ((), ())), preferred_element_type=F32)


def tn(a, b):
    return lax.dot_general(a, b, (((0,), (0,)), ((), ())), preferred_element_type=F32)


def place(source_of):
    o = lax.broadcasted_iota(jnp.int32, (256, 256), 0)
    i = lax.broadcasted_iota(jnp.int32, (256, 256), 1)
    return jnp.where(source_of(o) == i, 1.0, 0.0).astype(BF16)


def rec_to_erc(o):
    return ((o >> 2) & 3) * 64 + ((o >> 4) << 2) + (o & 3)


def erc_to_cer(o):
    return ((o >> 2) & 15) * 16 + (o & 3) * 4 + (o >> 6)


def erc_to_rec(o):
    return ((o >> 2) & 15) * 16 + (o >> 6) * 4 + (o & 3)


def cer_to_erc(o):
    return (o & 3) * 64 + (o >> 4) * 4 + ((o >> 2) & 3)


def kernel(
    group,
    x_hbm,
    cot_hbm,
    len_ref,
    gain_hbm,
    shift_hbm,
    win_hbm,
    wb_hbm,
    wo_hbm,
    upd_hbm,
    gp_hbm,
    gwin_hbm,
    gwo_hbm,
    gwb_hbm,
    gg_hbm,
    gs_hbm,
    upd_ref,
    gp_ref,
    gwin_ref,
    gwo_ref,
    gwb_ref,
    gg_ref,
    gs_ref,
    x_ref,
    cot_ref,
    gain_ref,
    shift_ref,
    win_ref,
    wb_ref,
    wo_ref,
    normed_ref,
    inv_ref,
    np_ref,
    high_ref,
    low_ref,
    dn_ref,
    pair_s,
    pair_r,
    cot_s,
    cot_r,
    bias_r,
    cols_ref,
    cotc_ref,
    biasm_ref,
    proj_ref,
    gate_ref,
    dgate_ref,
    gated_ref,
    att_ref,
    tot_ref,
    p_ref,
    dproj_ref,
    bacc_ref,
    tmp_ref,
    upd_s,
    upd_r,
    dcol_s,
    dcol_r,
    bg_s,
    bg_x,
    bg_t,
    bg_r,
    score_ref,
    datt_ref,
    delta_ref,
    ds_ref,
    par_f,
    par_s,
    par_x,
    par_t,
    par_r,
    sum_r,
    small_s,
    small_r,
    in_sem,
    out_sem,
    send_sem,
    recv_sem,
):
    me = lax.axis_index("dap")
    core = lax.rem(me, 2)
    chip = lax.div(me, 2)
    twin = me + 1 - 2 * core
    chips = group // 2
    cot_x, pair_x, bias_x, bias_w, bg_w, bg_x_, dcol_x, upd_x = 0, 1, 2, 3, 4, 6, 8, 9
    par_w, par_x_, sum_x, sum_w, small_x = 10, 11, 12, 13, 14

    loads = [
        pltpu.make_async_copy(src, dst, in_sem.at[n])
        for n, (src, dst) in enumerate(
            (
                (x_hbm, x_ref),
                (cot_hbm, cot_ref),
                (gain_hbm, gain_ref),
                (shift_hbm, shift_ref),
                (win_hbm, win_ref),
                (wb_hbm, wb_ref),
                (wo_hbm, wo_ref),
            )
        )
    ]
    for load in loads:
        load.start()

    stores = [
        pltpu.make_async_copy(src, dst, out_sem.at[n])
        for n, (src, dst) in enumerate(
            (
                (upd_ref, upd_hbm),
                (gp_ref, gp_hbm),
                (gwin_ref, gwin_hbm),
                (gwo_ref, gwo_hbm),
                (gwb_ref, gwb_hbm),
                (gg_ref, gg_hbm),
                (gs_ref, gs_hbm),
            )
        )
    ]

    y_at = lax.div(chip, 8)
    xs = [2 * lax.rem(lax.rem(lax.div(chip, 2), 4) + o, 4) for o in range(4)]
    zs = [lax.rem(lax.rem(chip, 2) + o, 2) for o in range(2)]
    around = [xs[x] + zs[z] for x in (2, 1, 3, 0) for z in (1, 0)]

    def each_chip(body, first=0, stop=4):
        def step(n, carry):
            for offset in around:
                body(8 * lax.rem(y_at + 2 - n + 3 * lax.div(n, 2), 4) + offset)
            return carry

        lax.fori_loop(first, min(stop, 3), step, 0)
        if stop == 4:
            for offset in around[:-1]:
                body(8 * y_at + offset)

    def each_peer(body, first=0, stop=4):
        def both(q):
            body(2 * q + 1 - core)
            body(2 * q + core)

        each_chip(both, first, stop)
        if stop == 4:
            body(twin)

    def copy(which, src, dst, device):
        return pltpu.make_async_remote_copy(
            src_ref=src,
            dst_ref=dst,
            send_sem=send_sem.at[which],
            recv_sem=recv_sem.at[which],
            device_id={"dap": device},
            device_id_type=MESH,
        )

    sent = []

    def send(which, source_of, dest):
        each_peer(lambda e: copy(which, source_of(e), dest.at[me], e).start())
        sent.append((which, dest.at[pl.ds(0, group - 1)]))

    def wait_recv(which, part):
        pltpu.make_async_copy(part, part, recv_sem.at[which]).wait()

    def wait_send(which, part):
        pltpu.make_async_copy(part, part, send_sem.at[which]).wait()

    barrier = pltpu.get_barrier_semaphore()
    each_peer(
        lambda e: pl.semaphore_signal(barrier, inc=1, device_id={"dap": e}, device_id_type=MESH)
    )

    rec_erc = place(rec_to_erc)
    row_of = lax.broadcasted_iota(jnp.int32, (16, CH), 0)
    pick = jnp.where(
        (lax.broadcasted_iota(jnp.int32, (16, HEADS), 0) & 3)
        == lax.broadcasted_iota(jnp.int32, (16, HEADS), 1),
        1.0,
        0.0,
    ).astype(BF16)

    for n in (0, 2, 3, 5):
        loads[n].wait()
    gain = gain_ref[...]
    shift = shift_ref[...]
    wb16 = nn(pick, wb_ref[...])
    wbr = [jnp.where((row_of >> 2) == r, wb16, 0.0).astype(BF16) for r in range(ROWS)]
    bias = jnp.zeros((16, N), F32)
    for r in range(ROWS):
        x = x_ref[r].astype(F32)
        mean = jnp.mean(x, -1, keepdims=True)
        cen = x - mean
        var = jnp.mean(cen * cen, -1, keepdims=True)
        inv = lax.rsqrt(var + EPS)
        normed = cen * inv
        normed_ref[r] = normed
        inv_ref[r] = jnp.broadcast_to(inv, (N, CH))
        low = (normed * gain + shift).astype(BF16)
        np_ref[r] = low
        bias += nt(wbr[r], low)
    bias_r[chip, core] = bias.astype(BF16)
    for b in range(4):
        block = jnp.concatenate([np_ref[r, 64 * b : 64 * b + 64, :] for r in range(ROWS)], 0)
        pair_s[16 * b : 16 * b + 16] = nn(rec_erc, block).astype(BF16).reshape(16, 16, CH)

    pl.semaphore_wait(barrier, group - 1)
    each_chip(
        lambda q: copy(
            bias_x, bias_r.at[chip, core], bias_r.at[chip, core], 2 * q + core
        ).start()
    )
    sent.append((bias_x, bias_r.at[pl.ds(0, chips - 1), 0]))
    send(pair_x, lambda e: pair_s.at[e], pair_r)
    pair_r[me] = pair_s[me]

    for n in (1, 4, 6):
        loads[n].wait()
    for b in range(4):
        block = jnp.concatenate([cot_ref[r, 64 * b : 64 * b + 64, :] for r in range(ROWS)], 0)
        cot_s[16 * b : 16 * b + 16] = nn(rec_erc, block).astype(BF16).reshape(16, 16, CH)
    send(cot_x, lambda e: cot_s.at[e], cot_r)
    cot_r[me] = cot_s[me]

    erc_cer = place(erc_to_cer)
    erc_rec = place(erc_to_rec)
    cer_erc = place(cer_to_erc)
    source = lax.broadcasted_iota(jnp.int32, (256, CH), 0)
    target = lax.broadcasted_iota(jnp.int32, (256, CH), 1)
    pick_in = jnp.where(
        (target >> 3) * 16 + (target & 7) == source, 1.0, 0.0
    ).astype(BF16)
    par_f[...] = jnp.zeros_like(par_f)
    row = lax.broadcasted_iota(jnp.int32, (16, 16), 0)
    col = lax.broadcasted_iota(jnp.int32, (16, 16), 1)
    heads_at = [
        [
            jnp.where(
                (((row & 3) >> 1) == pair) & ((row >> 2) * 4 + (row & 1) * 2 + half == col), 1.0, 0.0
            ).astype(BF16)
            for half in (0, 1)
        ]
        for pair in (0, 1)
    ]
    for r in range(ROWS):
        high = normed_ref[r].astype(BF16)
        high_ref[r] = high
        low_ref[r] = (normed_ref[r] - high.astype(F32)).astype(BF16)

    w_in = win_ref[...]
    w_in_t = jnp.transpose(w_in.astype(F32)).astype(BF16)
    w_out = wo_ref[...]

    wait_recv(bias_x, bias_r.at[pl.ds(0, chips - 1), 0])
    share = copy(bias_w, bias_r.at[:, core], bias_r.at[:, core], twin)
    share.start()

    wait_recv(pair_x, pair_r.at[pl.ds(0, group - 1)])
    for b in range(4):
        got = nn(erc_cer, pair_r[16 * b : 16 * b + 16].reshape(256, CH)).astype(BF16)
        for c in range(COLS):
            cols_ref[c, 64 * b : 64 * b + 64, :] = got[64 * c : 64 * c + 64]
    for j in range(COLS):
        projected = nt(w_in_t, cols_ref[j])
        proj_ref[j] = projected[: 3 * CH].astype(BF16)
        gate_ref[j] = jax.nn.sigmoid(projected[3 * CH :])

    share.wait()
    key = lax.broadcasted_iota(jnp.int32, (64, N), 0)
    for b in range(4):
        block = bias_r[8 * b : 8 * b + 8].reshape(256, N)
        got = nn(erc_cer, block) * LOG2E
        mask = jnp.where(key + 64 * b < len_ref[0], 0.0, NEG)
        for h in range(HEADS):
            biasm_ref[h, 64 * b : 64 * b + 64, :] = got[64 * h : 64 * h + 64] + mask

    scale = 1.0 / math.sqrt(DIM)

    units = [(j, h) for j in range(COLS) for h in range(HEADS)]

    def part_of(which, j, h):
        first = CH * which + DIM * h
        return proj_ref[j, first : first + DIM, :]

    for j, h in units:
        raw = tn(part_of(1, j, h), part_of(0, j, h))
        score_ref[HEADS * j + h] = raw * (scale * LOG2E) + biasm_ref[h]
    for j, h in units:
        score = score_ref[HEADS * j + h]
        p = jnp.exp2(score - jnp.max(score, 0, keepdims=True))
        tot_ref[j, h : h + 1, :] = 1.0 / jnp.sum(p, 0, keepdims=True)
        p_ref[HEADS * j + h] = p.astype(BF16)
    for j, h in units:
        rows = slice(DIM * h, DIM * h + DIM)
        att = nn(part_of(2, j, h), p_ref[HEADS * j + h]) * tot_ref[j, h : h + 1, :]
        att_ref[j, rows, :] = att
        gated_ref[j, rows, :] = (gate_ref[j, rows, :] * att).astype(BF16)

    wait_recv(cot_x, cot_r.at[pl.ds(0, group - 1)])
    for b in range(4):
        got = nn(erc_cer, cot_r[16 * b : 16 * b + 16].reshape(256, CH)).astype(BF16)
        for c in range(COLS):
            cotc_ref[c, 64 * b : 64 * b + 64, :] = got[64 * c : 64 * c + 64]
    for j in range(COLS):
        dgate_ref[j] = nt(w_out, cotc_ref[j])

    def score_grads(heads):
        for j in range(COLS):
            for h in heads:
                rows = slice(DIM * h, DIM * h + DIM)
                att = att_ref[j, rows, :]
                gate = gate_ref[j, rows, :]
                dgated = dgate_ref[j, rows, :]
                datt = ((dgated * gate) * tot_ref[j, h : h + 1, :]).astype(BF16)
                datt_ref[j, rows, :] = datt
                delta_ref[j, h : h + 1, :] = jnp.sum(datt.astype(F32) * att, 0, keepdims=True)
                dg = dgated * att * gate * (1.0 - gate)
                dproj_ref[j, 3 * CH + DIM * h : 3 * CH + DIM * h + DIM, :] = dg.astype(BF16)
        for h in heads:
            for j in range(COLS):
                rows = slice(DIM * h, DIM * h + DIM)
                dweights = tn(part_of(2, j, h), datt_ref[j, rows, :])
                p = p_ref[HEADS * j + h].astype(F32)
                ds = p * (dweights - delta_ref[j, h : h + 1, :])
                if j == 0:
                    bacc_ref[h] = ds
                else:
                    bacc_ref[h] += ds
                ds_ref[HEADS * j + h] = ds.astype(BF16)

    def input_grads(kinds):
        for which in kinds:
            for j in range(COLS):
                for h in range(HEADS):
                    ds = ds_ref[HEADS * j + h]
                    if which == 0:
                        grad = nn(part_of(1, j, h), ds) * scale
                    elif which == 1:
                        grad = nt(part_of(0, j, h), ds) * scale
                    else:
                        rows = slice(DIM * h, DIM * h + DIM)
                        grad = nt(datt_ref[j, rows, :], p_ref[HEADS * j + h])
                    first = CH * which + DIM * h
                    dproj_ref[j, first : first + DIM, :] = grad.astype(BF16)

    def gather_bias(pair):
        for b in range(4):
            block = jnp.concatenate(
                [
                    bacc_ref[h, 64 * b : 64 * b + 64, CH * half : CH * half + CH]
                    for h in (2 * pair, 2 * pair + 1)
                    for half in (0, 1)
                ],
                0,
            )
            got = nn(cer_erc, block.astype(BF16)).astype(BF16)
            bg_s[8 * b : 8 * b + 8, :, 16 * pair : 16 * pair + 16] = got.reshape(8, 2, 16, CH)

    every = tuple(range(HEADS))
    score_grads(every)
    gather_bias(0)
    gather_bias(1)
    bg_pass = copy(bg_w, bg_s.at[:, 1 - core], bg_x, twin)
    bg_pass.start()
    input_grads((0, 1))
    bg_pass.wait()
    for q in range(chips):
        bg_t[q] = (bg_s[q, core].astype(F32) + bg_x[q].astype(F32)).astype(BF16)
    each_chip(lambda q: copy(bg_x_, bg_t.at[q], bg_r.at[chip], 2 * q + core).start())
    sent.append((bg_x_, bg_r.at[pl.ds(0, chips - 1)]))
    bg_r[chip] = bg_t[chip]
    input_grads((2,))

    g_out = nn(gated_ref[0], cotc_ref[0])
    g_in = nn(dproj_ref[0], cols_ref[0])
    for j in range(1, COLS):
        g_out += nn(gated_ref[j], cotc_ref[j])
        g_in += nn(dproj_ref[j], cols_ref[j])
    par_f[pl.ds(8, group, stride=16), :] = g_out[:group]
    par_f[pl.ds(9, group, stride=16), :] = g_out[group:]
    for e in range(group):
        par_f[16 * e : 16 * e + 8, :] = g_in[8 * e : 8 * e + 8]
    par_s[...] = par_f[...].astype(BF16).reshape(chips, 2, 16, CH)
    par_pass = copy(par_w, par_s.at[:, 1 - core], par_x, twin)
    par_pass.start()

    for j in range(COLS):
        tmp_ref[j] = jnp.transpose(nn(w_in, dproj_ref[j])).astype(BF16)
    for b in range(4):
        block = jnp.concatenate([tmp_ref[j, 64 * b : 64 * b + 64, :] for j in range(COLS)], 0)
        dcol_s[16 * b : 16 * b + 16] = nn(cer_erc, block).astype(BF16).reshape(16, 16, CH)

    def send_dcol(e):
        copy(dcol_x, dcol_s.at[e], dcol_r.at[me], e).start()

    each_peer(send_dcol, 0, 2)
    par_pass.wait()
    for q in range(chips):
        par_t[q] = (par_s[q, core].astype(F32) + par_x[q].astype(F32)).astype(BF16)
    each_chip(lambda q: copy(par_x_, par_t.at[q], par_r.at[chip], 2 * q + core).start())
    sent.append((par_x_, par_r.at[pl.ds(0, chips - 1)]))
    each_peer(send_dcol, 2, 4)
    sent.append((dcol_x, dcol_r.at[pl.ds(0, group - 1)]))
    par_r[chip] = par_t[chip]
    dcol_r[me] = dcol_s[me]

    for j in range(COLS):
        tmp_ref[j] = tn(gated_ref[j], w_out).astype(BF16)
    for b in range(4):
        block = jnp.concatenate([tmp_ref[j, 64 * b : 64 * b + 64, :] for j in range(COLS)], 0)
        upd_s[16 * b : 16 * b + 16] = nn(cer_erc, block).astype(BF16).reshape(16, 16, CH)
    send(upd_x, lambda e: upd_s.at[e], upd_r)
    upd_r[me] = upd_s[me]

    wait_recv(bg_x_, bg_r.at[pl.ds(0, chips - 1)])
    sums = bg_r[0].astype(F32)
    for s in range(1, chips):
        sums += bg_r[s].astype(F32)
    sums = sums.astype(BF16)
    bsum = jnp.concatenate(
        [nn(heads_at[0][half], sums[:16]) + nn(heads_at[1][half], sums[16:]) for half in (0, 1)],
        1,
    ).astype(BF16)
    gwb = jnp.zeros((16, CH), F32)
    part = jnp.zeros((16, CH), F32)
    for r in range(ROWS):
        here = (row_of >> 2) == r
        gwb += jnp.where(here, nn(bsum, np_ref[r]), 0.0)
        part += jnp.where(here, nn(bsum, high_ref[r]) + nn(bsum, low_ref[r]), 0.0)
    small_s[0:4, :] = gwb[0:4] + gwb[4:8] + gwb[8:12] + gwb[12:16]
    grad_gain = jnp.sum(part * wb16, 0, keepdims=True)
    grad_shift = jnp.sum(jnp.sum(bsum.astype(F32), 1, keepdims=True) * wb16, 0, keepdims=True)

    wait_recv(par_x_, par_r.at[pl.ds(0, chips - 1)])
    total = par_r[0].astype(F32)
    for s in range(1, chips):
        total += par_r[s].astype(F32)
    sum_r[chip, core] = total.astype(BF16)
    each_chip(
        lambda q: copy(sum_x, sum_r.at[chip, core], sum_r.at[chip, core], 2 * q + core).start()
    )
    sent.append((sum_x, sum_r.at[pl.ds(0, chips - 1), 0]))

    wait_recv(dcol_x, dcol_r.at[pl.ds(0, group - 1)])
    for b in range(4):
        got = nn(erc_rec, dcol_r[16 * b : 16 * b + 16].reshape(256, CH))
        for r in range(ROWS):
            dn_ref[r, 64 * b : 64 * b + 64, :] = got[64 * r : 64 * r + 64]
    for r in range(ROWS):
        grad_gain += jnp.sum(dn_ref[r] * normed_ref[r], 0, keepdims=True)
        grad_shift += jnp.sum(dn_ref[r], 0, keepdims=True)
    small_s[4:5, :] = grad_gain
    small_s[5:6, :] = grad_shift
    send(small_x, lambda e: small_s, small_r)
    small_r[me] = small_s[...]

    for r in range(ROWS):
        normed = normed_ref[r]
        scaled = (dn_ref[r] + tn(bsum, wbr[r])) * gain
        mean_s = jnp.mean(scaled, -1, keepdims=True)
        mean_sn = jnp.mean(scaled * normed, -1, keepdims=True)
        gp_ref[r] = (inv_ref[r] * (scaled - mean_s - normed * mean_sn)).astype(BF16)
    stores[1].start()

    wait_recv(upd_x, upd_r.at[pl.ds(0, group - 1)])
    for b in range(4):
        got = nn(erc_rec, upd_r[16 * b : 16 * b + 16].reshape(256, CH)).astype(BF16)
        for r in range(ROWS):
            upd_ref[r, 64 * b : 64 * b + 64, :] = got[64 * r : 64 * r + 64]
    stores[0].start()

    wait_recv(sum_x, sum_r.at[pl.ds(0, chips - 1), 0])
    sum_pass = copy(sum_w, sum_r.at[:, core], sum_r.at[:, core], twin)
    sum_pass.start()
    sum_pass.wait()
    for q in range(4):
        rows = sum_r[8 * q : 8 * q + 8].reshape(256, CH)
        gwin_ref[:, CH * q : CH * q + CH] = tn(rows, pick_in)
    stores[2].start()
    par_f[...] = sum_r[...].astype(F32).reshape(group * 16, CH)
    gwo_ref[0:group, :] = par_f[pl.ds(8, group, stride=16), :]
    gwo_ref[group:, :] = par_f[pl.ds(9, group, stride=16), :]
    stores[3].start()

    wait_recv(small_x, small_r.at[pl.ds(0, group - 1)])
    small = small_r[0]
    for s in range(1, group):
        small += small_r[s]
    gwb_ref[...] = small[0:HEADS]
    gg_ref[...] = small[4:5]
    gs_ref[...] = small[5:6]
    for n in (4, 5, 6):
        stores[n].start()

    for which, part in sent:
        wait_send(which, part)
    for store in stores:
        store.wait()


def finish(*refs):
    count = 7
    sources, results, held = refs[:count], refs[count : 2 * count], refs[2 * count : 3 * count]
    in_sem, out_sem = refs[3 * count :]
    loads = [pltpu.make_async_copy(sources[n], held[n], in_sem.at[n]) for n in range(count)]
    stores = [pltpu.make_async_copy(held[n], results[n], out_sem.at[n]) for n in range(count)]
    for load in loads:
        load.start()
    for load, store in zip(loads, stores):
        load.wait()
        store.start()
    for store in stores:
        store.wait()


def per_device(group, pair_state, cotangent, length, norm_gain, norm_shift, w_in, w_bias, w_out):
    vmem = pl.BlockSpec(memory_space=pltpu.VMEM)
    smem = pl.BlockSpec(memory_space=pltpu.SMEM)
    hbm = pl.BlockSpec(memory_space=pltpu.HBM)
    chips = group // 2
    block = (group, 16, CH)
    shapes = (
        jax.ShapeDtypeStruct((ROWS, N, CH), BF16),
        jax.ShapeDtypeStruct((ROWS, N, CH), BF16),
        jax.ShapeDtypeStruct((CH, 4 * CH), F32),
        jax.ShapeDtypeStruct((CH, CH), F32),
        jax.ShapeDtypeStruct((HEADS, CH), F32),
        jax.ShapeDtypeStruct((1, CH), F32),
        jax.ShapeDtypeStruct((1, CH), F32),
    )
    out = pl.pallas_call(
        functools.partial(kernel, group),
        out_shape=shapes,
        in_specs=[hbm, hbm, smem] + [hbm] * 5,
        out_specs=[hbm] * 7,
        scratch_shapes=[pltpu.VMEM(s.shape, s.dtype) for s in shapes]
        + [
            pltpu.VMEM((ROWS, N, CH), BF16),
            pltpu.VMEM((ROWS, N, CH), BF16),
            pltpu.VMEM((1, CH), F32),
            pltpu.VMEM((1, CH), F32),
            pltpu.VMEM((CH, 4 * CH), BF16),
            pltpu.VMEM((HEADS, CH), BF16),
            pltpu.VMEM((CH, CH), BF16),
            pltpu.VMEM((ROWS, N, CH), F32),
            pltpu.VMEM((ROWS, N, CH), F32),
            pltpu.VMEM((ROWS, N, CH), BF16),
            pltpu.VMEM((ROWS, N, CH), BF16),
            pltpu.VMEM((ROWS, N, CH), BF16),
            pltpu.VMEM((ROWS, N, CH), F32),
            pltpu.VMEM(block, BF16),
            pltpu.VMEM(block, BF16),
            pltpu.VMEM(block, BF16),
            pltpu.VMEM(block, BF16),
            pltpu.VMEM((chips, 2, 16, N), BF16),
            pltpu.VMEM((COLS, N, CH), BF16),
            pltpu.VMEM((COLS, N, CH), BF16),
            pltpu.VMEM((HEADS, N, N), F32),
            pltpu.VMEM((COLS, 3 * CH, N), BF16),
            pltpu.VMEM((COLS, CH, N), F32),
            pltpu.VMEM((COLS, CH, N), F32),
            pltpu.VMEM((COLS, CH, N), BF16),
            pltpu.VMEM((COLS, CH, N), F32),
            pltpu.VMEM((COLS, 8, N), F32),
            pltpu.VMEM((COLS * HEADS, N, N), BF16),
            pltpu.VMEM((COLS, 4 * CH, N), BF16),
            pltpu.VMEM((HEADS, N, N), F32),
            pltpu.VMEM((COLS, N, CH), BF16),
            pltpu.VMEM(block, BF16),
            pltpu.VMEM(block, BF16),
            pltpu.VMEM(block, BF16),
            pltpu.VMEM(block, BF16),
            pltpu.VMEM((chips, 2, 32, CH), BF16),
            pltpu.VMEM((chips, 32, CH), BF16),
            pltpu.VMEM((chips, 32, CH), BF16),
            pltpu.VMEM((chips, 32, CH), BF16),
            pltpu.VMEM((COLS * HEADS, N, N), F32),
            pltpu.VMEM((COLS, CH, N), BF16),
            pltpu.VMEM((COLS, 8, N), F32),
            pltpu.VMEM((COLS * HEADS, N, N), BF16),
            pltpu.VMEM((group * 16, CH), F32),
            pltpu.VMEM((chips, 2, 16, CH), BF16),
            pltpu.VMEM((chips, 16, CH), BF16),
            pltpu.VMEM((chips, 16, CH), BF16),
            pltpu.VMEM((chips, 16, CH), BF16),
            pltpu.VMEM((chips, 2, 16, CH), BF16),
            pltpu.VMEM((6, CH), F32),
            pltpu.VMEM((group, 6, CH), F32),
            pltpu.SemaphoreType.DMA((7,)),
            pltpu.SemaphoreType.DMA((7,)),
            pltpu.SemaphoreType.DMA((15,)),
            pltpu.SemaphoreType.DMA((15,)),
        ],
        compiler_params=pltpu.CompilerParams(
            collective_id=0, has_side_effects=True, vmem_limit_bytes=60 * 2**20
        ),
    )(
        pair_state,
        cotangent,
        length,
        norm_gain.reshape(1, CH),
        norm_shift.reshape(1, CH),
        w_in,
        w_bias.T,
        w_out,
    )
    out = pl.pallas_call(
        finish,
        out_shape=shapes,
        in_specs=[hbm] * 7,
        out_specs=[hbm] * 7,
        scratch_shapes=[pltpu.VMEM(s.shape, s.dtype) for s in shapes]
        + [pltpu.SemaphoreType.DMA((7,)), pltpu.SemaphoreType.DMA((7,))],
        compiler_params=pltpu.CompilerParams(vmem_limit_bytes=60 * 2**20),
    )(*out)
    return (*out[:4], out[4].T, out[5].reshape(CH), out[6].reshape(CH))


def solution(mesh):
    split = P(("dp", "dap"), None, None)
    return jax.shard_map(
        functools.partial(per_device, mesh.shape["dap"]),
        mesh=mesh,
        in_specs=(split, split, P("dp"), P(), P(), P(), P(), P()),
        out_specs=(split, split, P("dp", None), P("dp", None), P("dp", None), P("dp"), P("dp")),
        check_vma=False,
    )
```

```python
import functools
import math

import jax
import jax.numpy as jnp
from jax import lax
from jax.experimental import pallas as pl
from jax.experimental.pallas import tpu as pltpu
from jax.sharding import PartitionSpec as P

EPS = 1e-05
NEG = -1000000000.0
LOG2E = 1.4426950408889634
MESH = pl.DeviceIdType.MESH
F32 = jnp.float32
BF16 = jnp.bfloat16
ROWS = 4
COLS = 4
HEADS = 4
DIM = 32
N = 256
CH = 128


def nn(a, b):
    return lax.dot_general(a, b, (((1,), (0,)), ((), ())), preferred_element_type=F32)


def nt(a, b):
    return lax.dot_general(a, b, (((1,), (1,)), ((), ())), preferred_element_type=F32)


def tn(a, b):
    return lax.dot_general(a, b, (((0,), (0,)), ((), ())), preferred_element_type=F32)


def place(source_of):
    o = lax.broadcasted_iota(jnp.int32, (256, 256), 0)
    i = lax.broadcasted_iota(jnp.int32, (256, 256), 1)
    return jnp.where(source_of(o) == i, 1.0, 0.0).astype(BF16)


def rec_to_erc(o):
    return ((o >> 2) & 3) * 64 + ((o >> 4) << 2) + (o & 3)


def erc_to_cer(o):
    return ((o >> 2) & 15) * 16 + (o & 3) * 4 + (o >> 6)


def erc_to_rec(o):
    return ((o >> 2) & 15) * 16 + (o >> 6) * 4 + (o & 3)


def cer_to_erc(o):
    return (o & 3) * 64 + (o >> 4) * 4 + ((o >> 2) & 3)


def kernel(
    group,
    x_hbm,
    cot_hbm,
    len_ref,
    gain_hbm,
    shift_hbm,
    win_hbm,
    wb_hbm,
    wo_hbm,
    upd_hbm,
    gp_hbm,
    sum_hbm,
    small_hbm,
    upd_ref,
    gp_ref,
    x_ref,
    cot_ref,
    gain_ref,
    shift_ref,
    win_ref,
    wb_ref,
    wo_ref,
    normed_ref,
    inv_ref,
    np_ref,
    high_ref,
    low_ref,
    dn_ref,
    pair_s,
    pair_r,
    cot_s,
    cot_r,
    bias_r,
    cols_ref,
    cotc_ref,
    biasm_ref,
    proj_ref,
    gate_ref,
    dgate_ref,
    gated_ref,
    att_ref,
    tot_ref,
    p_ref,
    dproj_ref,
    bacc_ref,
    tmp_ref,
    upd_s,
    upd_r,
    dcol_s,
    dcol_r,
    bg_s,
    bg_x,
    bg_t,
    bg_r,
    score_ref,
    datt_ref,
    delta_ref,
    ds_ref,
    par_f,
    par_s,
    par_x,
    par_t,
    par_r,
    sum_r,
    small_s,
    in_sem,
    out_sem,
    send_sem,
    recv_sem,
):
    me = lax.axis_index("dap")
    core = lax.rem(me, 2)
    chip = lax.div(me, 2)
    twin = me + 1 - 2 * core
    chips = group // 2
    cot_x, pair_x, bias_x, bias_w, bg_w, bg_x_, dcol_x, upd_x = 0, 1, 2, 3, 4, 6, 8, 9
    par_w, par_x_, sum_x, sum_w, small_x = 10, 11, 12, 13, 14

    loads = [
        pltpu.make_async_copy(src, dst, in_sem.at[n])
        for n, (src, dst) in enumerate(
            (
                (x_hbm, x_ref),
                (cot_hbm, cot_ref),
                (gain_hbm, gain_ref),
                (shift_hbm, shift_ref),
                (win_hbm, win_ref),
                (wb_hbm, wb_ref),
                (wo_hbm, wo_ref),
            )
        )
    ]
    for load in loads:
        load.start()

    stores = [
        pltpu.make_async_copy(src, dst, out_sem.at[n])
        for n, (src, dst) in enumerate(
            (
                (upd_ref, upd_hbm),
                (gp_ref, gp_hbm),
                (sum_r, sum_hbm.at[:, core]),
                (small_s, small_hbm.at[me]),
            )
        )
    ]

    y_at = lax.div(chip, 8)
    xs = [2 * lax.rem(lax.rem(lax.div(chip, 2), 4) + o, 4) for o in range(4)]
    zs = [lax.rem(lax.rem(chip, 2) + o, 2) for o in range(2)]
    around = [xs[x] + zs[z] for x in (2, 1, 3, 0) for z in (1, 0)]

    def each_chip(body, first=0, stop=4):
        def step(n, carry):
            for offset in around:
                body(8 * lax.rem(y_at + 2 - n + 3 * lax.div(n, 2), 4) + offset)
            return carry

        lax.fori_loop(first, min(stop, 3), step, 0)
        if stop == 4:
            for offset in around[:-1]:
                body(8 * y_at + offset)

    def each_peer(body, first=0, stop=4):
        def both(q):
            body(2 * q + 1 - core)
            body(2 * q + core)

        each_chip(both, first, stop)
        if stop == 4:
            body(twin)

    def near_peer(body):
        def step(t, carry):
            body(lax.rem(me + t, group))
            return carry

        lax.fori_loop(1, group, step, 0)

    def copy(which, src, dst, device):
        return pltpu.make_async_remote_copy(
            src_ref=src,
            dst_ref=dst,
            send_sem=send_sem.at[which],
            recv_sem=recv_sem.at[which],
            device_id={"dap": device},
            device_id_type=MESH,
        )

    sent = []

    def send(which, source_of, dest, order=each_peer):
        order(lambda e: copy(which, source_of(e), dest.at[me], e).start())
        sent.append((which, dest.at[pl.ds(0, group - 1)]))

    def wait_recv(which, part):
        pltpu.make_async_copy(part, part, recv_sem.at[which]).wait()

    def wait_send(which, part):
        pltpu.make_async_copy(part, part, send_sem.at[which]).wait()

    barrier = pltpu.get_barrier_semaphore()
    near_peer(
        lambda e: pl.semaphore_signal(barrier, inc=1, device_id={"dap": e}, device_id_type=MESH)
    )

    rec_erc = place(rec_to_erc)
    row_of = lax.broadcasted_iota(jnp.int32, (16, CH), 0)
    pick = jnp.where(
        (lax.broadcasted_iota(jnp.int32, (16, HEADS), 0) & 3)
        == lax.broadcasted_iota(jnp.int32, (16, HEADS), 1),
        1.0,
        0.0,
    ).astype(BF16)

    for n in (0, 2, 3, 5):
        loads[n].wait()
    gain = gain_ref[...]
    shift = shift_ref[...]
    wb16 = nn(pick, wb_ref[...])
    wbr = [jnp.where((row_of >> 2) == r, wb16, 0.0).astype(BF16) for r in range(ROWS)]
    bias = jnp.zeros((16, N), F32)
    for r in range(ROWS):
        x = x_ref[r].astype(F32)
        mean = jnp.mean(x, -1, keepdims=True)
        cen = x - mean
        var = jnp.mean(cen * cen, -1, keepdims=True)
        inv = lax.rsqrt(var + EPS)
        normed = cen * inv
        normed_ref[r] = normed
        inv_ref[r] = jnp.broadcast_to(inv, (N, CH))
        low = (normed * gain + shift).astype(BF16)
        np_ref[r] = low
        bias += nt(wbr[r], low)
    bias_r[chip, core] = bias.astype(BF16)
    for b in range(4):
        block = jnp.concatenate([np_ref[r, 64 * b : 64 * b + 64, :] for r in range(ROWS)], 0)
        pair_s[16 * b : 16 * b + 16] = nn(rec_erc, block).astype(BF16).reshape(16, 16, CH)

    pl.semaphore_wait(barrier, group - 1)
    each_chip(
        lambda q: copy(
            bias_x, bias_r.at[chip, core], bias_r.at[chip, core], 2 * q + core
        ).start()
    )
    sent.append((bias_x, bias_r.at[pl.ds(0, chips - 1), 0]))
    send(pair_x, lambda e: pair_s.at[e], pair_r)
    pair_r[me] = pair_s[me]

    for n in (1, 4, 6):
        loads[n].wait()
    for b in range(4):
        block = jnp.concatenate([cot_ref[r, 64 * b : 64 * b + 64, :] for r in range(ROWS)], 0)
        cot_s[16 * b : 16 * b + 16] = nn(rec_erc, block).astype(BF16).reshape(16, 16, CH)
    send(cot_x, lambda e: cot_s.at[e], cot_r)
    cot_r[me] = cot_s[me]

    erc_cer = place(erc_to_cer)
    erc_rec = place(erc_to_rec)
    cer_erc = place(cer_to_erc)
    par_f[...] = jnp.zeros_like(par_f)
    row = lax.broadcasted_iota(jnp.int32, (16, 16), 0)
    col = lax.broadcasted_iota(jnp.int32, (16, 16), 1)
    heads_at = [
        [
            jnp.where(
                (((row & 3) >> 1) == pair) & ((row >> 2) * 4 + (row & 1) * 2 + half == col), 1.0, 0.0
            ).astype(BF16)
            for half in (0, 1)
        ]
        for pair in (0, 1)
    ]
    for r in range(ROWS):
        high = normed_ref[r].astype(BF16)
        high_ref[r] = high
        low_ref[r] = (normed_ref[r] - high.astype(F32)).astype(BF16)

    w_in = win_ref[...]
    w_in_t = jnp.transpose(w_in.astype(F32)).astype(BF16)
    w_out = wo_ref[...]

    wait_recv(bias_x, bias_r.at[pl.ds(0, chips - 1), 0])
    share = copy(bias_w, bias_r.at[:, core], bias_r.at[:, core], twin)
    share.start()

    wait_recv(pair_x, pair_r.at[pl.ds(0, group - 1)])
    for b in range(4):
        got = nn(erc_cer, pair_r[16 * b : 16 * b + 16].reshape(256, CH)).astype(BF16)
        for c in range(COLS):
            cols_ref[c, 64 * b : 64 * b + 64, :] = got[64 * c : 64 * c + 64]
    for j in range(COLS):
        projected = nt(w_in_t, cols_ref[j])
        proj_ref[j] = projected[: 3 * CH].astype(BF16)
        gate_ref[j] = jax.nn.sigmoid(projected[3 * CH :])

    share.wait()
    key = lax.broadcasted_iota(jnp.int32, (64, N), 0)
    for b in range(4):
        block = bias_r[8 * b : 8 * b + 8].reshape(256, N)
        got = nn(erc_cer, block) * LOG2E
        mask = jnp.where(key + 64 * b < len_ref[0], 0.0, NEG)
        for h in range(HEADS):
            biasm_ref[h, 64 * b : 64 * b + 64, :] = got[64 * h : 64 * h + 64] + mask

    scale = 1.0 / math.sqrt(DIM)

    units = [(j, h) for j in range(COLS) for h in range(HEADS)]

    def part_of(which, j, h):
        first = CH * which + DIM * h
        return proj_ref[j, first : first + DIM, :]

    for j, h in units:
        raw = tn(part_of(1, j, h), part_of(0, j, h))
        score_ref[HEADS * j + h] = raw * (scale * LOG2E) + biasm_ref[h]
    for j, h in units:
        score = score_ref[HEADS * j + h]
        p = jnp.exp2(score - jnp.max(score, 0, keepdims=True))
        tot_ref[j, h : h + 1, :] = 1.0 / jnp.sum(p, 0, keepdims=True)
        p_ref[HEADS * j + h] = p.astype(BF16)
    for j, h in units:
        rows = slice(DIM * h, DIM * h + DIM)
        att = nn(part_of(2, j, h), p_ref[HEADS * j + h]) * tot_ref[j, h : h + 1, :]
        att_ref[j, rows, :] = att
        gated_ref[j, rows, :] = (gate_ref[j, rows, :] * att).astype(BF16)

    wait_recv(cot_x, cot_r.at[pl.ds(0, group - 1)])
    for b in range(4):
        got = nn(erc_cer, cot_r[16 * b : 16 * b + 16].reshape(256, CH)).astype(BF16)
        for c in range(COLS):
            cotc_ref[c, 64 * b : 64 * b + 64, :] = got[64 * c : 64 * c + 64]
    for j in range(COLS):
        dgate_ref[j] = nt(w_out, cotc_ref[j])

    def score_grads(heads):
        for j in range(COLS):
            for h in heads:
                rows = slice(DIM * h, DIM * h + DIM)
                att = att_ref[j, rows, :]
                gate = gate_ref[j, rows, :]
                dgated = dgate_ref[j, rows, :]
                datt = ((dgated * gate) * tot_ref[j, h : h + 1, :]).astype(BF16)
                datt_ref[j, rows, :] = datt
                delta_ref[j, h : h + 1, :] = jnp.sum(datt.astype(F32) * att, 0, keepdims=True)
                dg = dgated * att * gate * (1.0 - gate)
                dproj_ref[j, 3 * CH + DIM * h : 3 * CH + DIM * h + DIM, :] = dg.astype(BF16)
        for h in heads:
            for j in range(COLS):
                rows = slice(DIM * h, DIM * h + DIM)
                dweights = tn(part_of(2, j, h), datt_ref[j, rows, :])
                p = p_ref[HEADS * j + h].astype(F32)
                ds = p * (dweights - delta_ref[j, h : h + 1, :])
                if j == 0:
                    bacc_ref[h] = ds
                else:
                    bacc_ref[h] += ds
                ds_ref[HEADS * j + h] = ds.astype(BF16)

    def input_grads(heads):
        for which in range(3):
            for j in range(COLS):
                for h in heads:
                    ds = ds_ref[HEADS * j + h]
                    if which == 0:
                        grad = nn(part_of(1, j, h), ds) * scale
                    elif which == 1:
                        grad = nt(part_of(0, j, h), ds) * scale
                    else:
                        rows = slice(DIM * h, DIM * h + DIM)
                        grad = nt(datt_ref[j, rows, :], p_ref[HEADS * j + h])
                    first = CH * which + DIM * h
                    dproj_ref[j, first : first + DIM, :] = grad.astype(BF16)

    def gather_bias(pair):
        for b in range(4):
            block = jnp.concatenate(
                [
                    bacc_ref[h, 64 * b : 64 * b + 64, CH * half : CH * half + CH]
                    for h in (2 * pair, 2 * pair + 1)
                    for half in (0, 1)
                ],
                0,
            )
            got = nn(cer_erc, block.astype(BF16)).astype(BF16)
            bg_s[8 * b : 8 * b + 8, :, 16 * pair : 16 * pair + 16] = got.reshape(8, 2, 16, CH)

    every = tuple(range(HEADS))
    score_grads(every)
    gather_bias(0)
    gather_bias(1)
    bg_pass = copy(bg_w, bg_s.at[:, 1 - core], bg_x, twin)
    bg_pass.start()
    input_grads((0, 1))
    bg_pass.wait()
    for q in range(chips):
        bg_t[q] = (bg_s[q, core].astype(F32) + bg_x[q].astype(F32)).astype(BF16)
    each_chip(lambda q: copy(bg_x_, bg_t.at[q], bg_r.at[chip], 2 * q + core).start())
    sent.append((bg_x_, bg_r.at[pl.ds(0, chips - 1)]))
    bg_r[chip] = bg_t[chip]
    input_grads((2, 3))

    g_out = nn(gated_ref[0], cotc_ref[0])
    g_in = nn(dproj_ref[0], cols_ref[0])
    for j in range(1, COLS):
        g_out += nn(gated_ref[j], cotc_ref[j])
        g_in += nn(dproj_ref[j], cols_ref[j])
    par_f[pl.ds(8, group, stride=16), :] = g_out[:group]
    par_f[pl.ds(9, group, stride=16), :] = g_out[group:]
    for e in range(group):
        par_f[16 * e : 16 * e + 8, :] = g_in[8 * e : 8 * e + 8]
    par_s[...] = par_f[...].astype(BF16).reshape(chips, 2, 16, CH)
    par_pass = copy(par_w, par_s.at[:, 1 - core], par_x, twin)
    par_pass.start()

    for j in range(COLS):
        tmp_ref[j] = jnp.transpose(nn(w_in, dproj_ref[j])).astype(BF16)
    for b in range(4):
        block = jnp.concatenate([tmp_ref[j, 64 * b : 64 * b + 64, :] for j in range(COLS)], 0)
        dcol_s[16 * b : 16 * b + 16] = nn(cer_erc, block).astype(BF16).reshape(16, 16, CH)

    def send_dcol(e):
        copy(dcol_x, dcol_s.at[e], dcol_r.at[me], e).start()

    each_peer(send_dcol, 0, 2)
    par_pass.wait()
    for q in range(chips):
        par_t[q] = (par_s[q, core].astype(F32) + par_x[q].astype(F32)).astype(BF16)
    each_chip(lambda q: copy(par_x_, par_t.at[q], par_r.at[chip], 2 * q + core).start())
    sent.append((par_x_, par_r.at[pl.ds(0, chips - 1)]))
    each_peer(send_dcol, 2, 4)
    sent.append((dcol_x, dcol_r.at[pl.ds(0, group - 1)]))
    par_r[chip] = par_t[chip]
    dcol_r[me] = dcol_s[me]

    for j in range(COLS):
        tmp_ref[j] = tn(gated_ref[j], w_out).astype(BF16)
    for b in range(4):
        block = jnp.concatenate([tmp_ref[j, 64 * b : 64 * b + 64, :] for j in range(COLS)], 0)
        upd_s[16 * b : 16 * b + 16] = nn(cer_erc, block).astype(BF16).reshape(16, 16, CH)
    send(upd_x, lambda e: upd_s.at[e], upd_r)
    upd_r[me] = upd_s[me]

    wait_recv(bg_x_, bg_r.at[pl.ds(0, chips - 1)])
    sums = bg_r[0].astype(F32)
    for s in range(1, chips):
        sums += bg_r[s].astype(F32)
    sums = sums.astype(BF16)
    bsum = jnp.concatenate(
        [nn(heads_at[0][half], sums[:16]) + nn(heads_at[1][half], sums[16:]) for half in (0, 1)],
        1,
    ).astype(BF16)
    gwb = jnp.zeros((16, CH), F32)
    part = jnp.zeros((16, CH), F32)
    for r in range(ROWS):
        here = (row_of >> 2) == r
        gwb += jnp.where(here, nn(bsum, np_ref[r]), 0.0)
        part += jnp.where(here, nn(bsum, high_ref[r]) + nn(bsum, low_ref[r]), 0.0)
    small_s[0:4, :] = gwb[0:4] + gwb[4:8] + gwb[8:12] + gwb[12:16]
    grad_gain = jnp.sum(part * wb16, 0, keepdims=True)
    grad_shift = jnp.sum(jnp.sum(bsum.astype(F32), 1, keepdims=True) * wb16, 0, keepdims=True)

    wait_recv(par_x_, par_r.at[pl.ds(0, chips - 1)])
    total = par_r[0].astype(F32)
    for s in range(1, chips):
        total += par_r[s].astype(F32)
    sum_r[chip] = total.astype(BF16)
    each_chip(lambda q: copy(sum_x, sum_r.at[chip], sum_r.at[chip], 2 * q + core).start())
    sent.append((sum_x, sum_r.at[pl.ds(0, chips - 1)]))

    wait_recv(dcol_x, dcol_r.at[pl.ds(0, group - 1)])
    for b in range(4):
        got = nn(erc_rec, dcol_r[16 * b : 16 * b + 16].reshape(256, CH))
        for r in range(ROWS):
            dn_ref[r, 64 * b : 64 * b + 64, :] = got[64 * r : 64 * r + 64]
    for r in range(ROWS):
        grad_gain += jnp.sum(dn_ref[r] * normed_ref[r], 0, keepdims=True)
        grad_shift += jnp.sum(dn_ref[r], 0, keepdims=True)
    small_s[4:5, :] = grad_gain
    small_s[5:6, :] = grad_shift
    send(small_x, lambda e: small_s, small_hbm)
    stores[3].start()

    for r in range(ROWS):
        normed = normed_ref[r]
        scaled = (dn_ref[r] + tn(bsum, wbr[r])) * gain
        mean_s = jnp.mean(scaled, -1, keepdims=True)
        mean_sn = jnp.mean(scaled * normed, -1, keepdims=True)
        gp_ref[r] = (inv_ref[r] * (scaled - mean_s - normed * mean_sn)).astype(BF16)
    stores[1].start()

    wait_recv(upd_x, upd_r.at[pl.ds(0, group - 1)])
    for b in range(4):
        got = nn(erc_rec, upd_r[16 * b : 16 * b + 16].reshape(256, CH)).astype(BF16)
        for r in range(ROWS):
            upd_ref[r, 64 * b : 64 * b + 64, :] = got[64 * r : 64 * r + 64]
    stores[0].start()

    wait_recv(sum_x, sum_r.at[pl.ds(0, chips - 1)])
    sum_pass = copy(sum_w, sum_r, sum_hbm.at[:, core], twin)
    sum_pass.start()
    stores[2].start()
    sum_pass.wait()
    wait_recv(small_x, small_hbm.at[pl.ds(0, group - 1)])

    for which, part in sent:
        wait_send(which, part)
    for store in stores:
        store.wait()


def finish(
    group,
    upd_hbm,
    gp_hbm,
    sum_hbm,
    small_hbm,
    upd_out,
    gp_out,
    gwin_out,
    gwo_out,
    gwb_out,
    gg_out,
    gs_out,
    upd_ref,
    gp_ref,
    sum_ref,
    small_ref,
    gwin_ref,
    gwo_ref,
    gwb_ref,
    gg_ref,
    gs_ref,
    par_f,
    in_sem,
    out_sem,
):
    loads = [
        pltpu.make_async_copy(src, dst, in_sem.at[n])
        for n, (src, dst) in enumerate(
            ((sum_hbm, sum_ref), (small_hbm, small_ref), (upd_hbm, upd_ref), (gp_hbm, gp_ref))
        )
    ]
    stores = [
        pltpu.make_async_copy(src, dst, out_sem.at[n])
        for n, (src, dst) in enumerate(
            (
                (upd_ref, upd_out),
                (gp_ref, gp_out),
                (gwin_ref, gwin_out),
                (gwo_ref, gwo_out),
                (gwb_ref, gwb_out),
                (gg_ref, gg_out),
                (gs_ref, gs_out),
            )
        )
    ]
    for load in loads:
        load.start()
    source = lax.broadcasted_iota(jnp.int32, (256, CH), 0)
    target = lax.broadcasted_iota(jnp.int32, (256, CH), 1)
    pick_in = jnp.where((target >> 3) * 16 + (target & 7) == source, 1.0, 0.0).astype(BF16)

    loads[0].wait()
    for q in range(4):
        rows = sum_ref[8 * q : 8 * q + 8].reshape(256, CH)
        gwin_ref[:, CH * q : CH * q + CH] = tn(rows, pick_in)
    stores[2].start()
    par_f[...] = sum_ref[...].astype(F32).reshape(group * 16, CH)
    gwo_ref[0:group, :] = par_f[pl.ds(8, group, stride=16), :]
    gwo_ref[group:, :] = par_f[pl.ds(9, group, stride=16), :]
    stores[3].start()
    loads[1].wait()
    small = small_ref[0]
    for s in range(1, group):
        small += small_ref[s]
    gwb_ref[...] = small[0:HEADS]
    gg_ref[...] = small[4:5]
    gs_ref[...] = small[5:6]
    for n in (4, 5, 6):
        stores[n].start()
    for n in (0, 1):
        loads[2 + n].wait()
        stores[n].start()
    for store in stores:
        store.wait()


def per_device(group, pair_state, cotangent, length, norm_gain, norm_shift, w_in, w_bias, w_out):
    vmem = pl.BlockSpec(memory_space=pltpu.VMEM)
    smem = pl.BlockSpec(memory_space=pltpu.SMEM)
    hbm = pl.BlockSpec(memory_space=pltpu.HBM)
    chips = group // 2
    block = (group, 16, CH)
    shapes = (
        jax.ShapeDtypeStruct((ROWS, N, CH), BF16),
        jax.ShapeDtypeStruct((ROWS, N, CH), BF16),
        jax.ShapeDtypeStruct((CH, 4 * CH), F32),
        jax.ShapeDtypeStruct((CH, CH), F32),
        jax.ShapeDtypeStruct((HEADS, CH), F32),
        jax.ShapeDtypeStruct((1, CH), F32),
        jax.ShapeDtypeStruct((1, CH), F32),
    )
    passed = shapes[:2] + (
        jax.ShapeDtypeStruct((chips, 2, 16, CH), BF16),
        jax.ShapeDtypeStruct((group, 6, CH), F32),
    )
    out = pl.pallas_call(
        functools.partial(kernel, group),
        out_shape=passed,
        in_specs=[hbm, hbm, smem] + [hbm] * 5,
        out_specs=[hbm] * 4,
        scratch_shapes=[pltpu.VMEM(s.shape, s.dtype) for s in shapes[:2]]
        + [
            pltpu.VMEM((ROWS, N, CH), BF16),
            pltpu.VMEM((ROWS, N, CH), BF16),
            pltpu.VMEM((1, CH), F32),
            pltpu.VMEM((1, CH), F32),
            pltpu.VMEM((CH, 4 * CH), BF16),
            pltpu.VMEM((HEADS, CH), BF16),
            pltpu.VMEM((CH, CH), BF16),
            pltpu.VMEM((ROWS, N, CH), F32),
            pltpu.VMEM((ROWS, N, CH), F32),
            pltpu.VMEM((ROWS, N, CH), BF16),
            pltpu.VMEM((ROWS, N, CH), BF16),
            pltpu.VMEM((ROWS, N, CH), BF16),
            pltpu.VMEM((ROWS, N, CH), F32),
            pltpu.VMEM(block, BF16),
            pltpu.VMEM(block, BF16),
            pltpu.VMEM(block, BF16),
            pltpu.VMEM(block, BF16),
            pltpu.VMEM((chips, 2, 16, N), BF16),
            pltpu.VMEM((COLS, N, CH), BF16),
            pltpu.VMEM((COLS, N, CH), BF16),
            pltpu.VMEM((HEADS, N, N), F32),
            pltpu.VMEM((COLS, 3 * CH, N), BF16),
            pltpu.VMEM((COLS, CH, N), F32),
            pltpu.VMEM((COLS, CH, N), F32),
            pltpu.VMEM((COLS, CH, N), BF16),
            pltpu.VMEM((COLS, CH, N), F32),
            pltpu.VMEM((COLS, 8, N), F32),
            pltpu.VMEM((COLS * HEADS, N, N), BF16),
            pltpu.VMEM((COLS, 4 * CH, N), BF16),
            pltpu.VMEM((HEADS, N, N), F32),
            pltpu.VMEM((COLS, N, CH), BF16),
            pltpu.VMEM(block, BF16),
            pltpu.VMEM(block, BF16),
            pltpu.VMEM(block, BF16),
            pltpu.VMEM(block, BF16),
            pltpu.VMEM((chips, 2, 32, CH), BF16),
            pltpu.VMEM((chips, 32, CH), BF16),
            pltpu.VMEM((chips, 32, CH), BF16),
            pltpu.VMEM((chips, 32, CH), BF16),
            pltpu.VMEM((COLS * HEADS, N, N), F32),
            pltpu.VMEM((COLS, CH, N), BF16),
            pltpu.VMEM((COLS, 8, N), F32),
            pltpu.VMEM((COLS * HEADS, N, N), BF16),
            pltpu.VMEM((group * 16, CH), F32),
            pltpu.VMEM((chips, 2, 16, CH), BF16),
            pltpu.VMEM((chips, 16, CH), BF16),
            pltpu.VMEM((chips, 16, CH), BF16),
            pltpu.VMEM((chips, 16, CH), BF16),
            pltpu.VMEM((chips, 16, CH), BF16),
            pltpu.VMEM((6, CH), F32),
            pltpu.SemaphoreType.DMA((7,)),
            pltpu.SemaphoreType.DMA((7,)),
            pltpu.SemaphoreType.DMA((15,)),
            pltpu.SemaphoreType.DMA((15,)),
        ],
        compiler_params=pltpu.CompilerParams(
            collective_id=0, has_side_effects=True, vmem_limit_bytes=60 * 2**20
        ),
    )(
        pair_state,
        cotangent,
        length,
        norm_gain.reshape(1, CH),
        norm_shift.reshape(1, CH),
        w_in,
        w_bias.T,
        w_out,
    )
    out = pl.pallas_call(
        functools.partial(finish, group),
        out_shape=shapes,
        in_specs=[hbm] * 4,
        out_specs=[hbm] * 7,
        scratch_shapes=[pltpu.VMEM(s.shape, s.dtype) for s in passed]
        + [pltpu.VMEM(s.shape, s.dtype) for s in shapes[2:]]
        + [
            pltpu.VMEM((group * 16, CH), F32),
            pltpu.SemaphoreType.DMA((4,)),
            pltpu.SemaphoreType.DMA((7,)),
        ],
        compiler_params=pltpu.CompilerParams(vmem_limit_bytes=60 * 2**20),
    )(*out)
    return (*out[:4], out[4].T, out[5].reshape(CH), out[6].reshape(CH))


def solution(mesh):
    split = P(("dp", "dap"), None, None)
    return jax.shard_map(
        functools.partial(per_device, mesh.shape["dap"]),
        mesh=mesh,
        in_specs=(split, split, P("dp"), P(), P(), P(), P(), P()),
        out_specs=(split, split, P("dp", None), P("dp", None), P("dp", None), P("dp"), P("dp")),
        check_vma=False,
    )
```

```python
import functools
import math

import jax
import jax.numpy as jnp
from jax import lax
from jax.experimental import pallas as pl
from jax.experimental.pallas import tpu as pltpu
from jax.sharding import PartitionSpec as P

EPS = 1e-05
NEG = -1000000000.0
LOG2E = 1.4426950408889634
MESH = pl.DeviceIdType.MESH
F32 = jnp.float32
BF16 = jnp.bfloat16
ROWS = 4
COLS = 4
HEADS = 4
DIM = 32
N = 256
CH = 128


def nn(a, b):
    return lax.dot_general(a, b, (((1,), (0,)), ((), ())), preferred_element_type=F32)


def nt(a, b):
    return lax.dot_general(a, b, (((1,), (1,)), ((), ())), preferred_element_type=F32)


def tn(a, b):
    return lax.dot_general(a, b, (((0,), (0,)), ((), ())), preferred_element_type=F32)


def place(source_of):
    o = lax.broadcasted_iota(jnp.int32, (256, 256), 0)
    i = lax.broadcasted_iota(jnp.int32, (256, 256), 1)
    return jnp.where(source_of(o) == i, 1.0, 0.0).astype(BF16)


def rec_to_erc(o):
    return ((o >> 2) & 3) * 64 + ((o >> 4) << 2) + (o & 3)


def erc_to_cer(o):
    return ((o >> 2) & 15) * 16 + (o & 3) * 4 + (o >> 6)


def erc_to_rec(o):
    return ((o >> 2) & 15) * 16 + (o >> 6) * 4 + (o & 3)


def cer_to_erc(o):
    return (o & 3) * 64 + (o >> 4) * 4 + ((o >> 2) & 3)


def kernel(
    group,
    x_hbm,
    cot_hbm,
    len_ref,
    gain_hbm,
    shift_hbm,
    win_hbm,
    wb_hbm,
    wo_hbm,
    upd_hbm,
    gp_hbm,
    sum_hbm,
    small_hbm,
    upd_ref,
    gp_ref,
    x_ref,
    cot_ref,
    gain_ref,
    shift_ref,
    win_ref,
    wb_ref,
    wo_ref,
    normed_ref,
    inv_ref,
    np_ref,
    high_ref,
    low_ref,
    dn_ref,
    pair_s,
    pair_r,
    cot_s,
    cot_r,
    bias_r,
    cols_ref,
    cotc_ref,
    biasm_ref,
    proj_ref,
    gate_ref,
    dgate_ref,
    gated_ref,
    att_ref,
    tot_ref,
    p_ref,
    dproj_ref,
    bacc_ref,
    tmp_ref,
    upd_s,
    upd_r,
    dcol_s,
    dcol_r,
    bg_s,
    bg_x,
    bg_t,
    bg_r,
    score_ref,
    datt_ref,
    delta_ref,
    ds_ref,
    par_f,
    par_s,
    par_x,
    par_t,
    par_r,
    sum_r,
    small_s,
    in_sem,
    out_sem,
    send_sem,
    recv_sem,
):
    me = lax.axis_index("dap")
    core = lax.rem(me, 2)
    chip = lax.div(me, 2)
    twin = me + 1 - 2 * core
    chips = group // 2
    cot_x, pair_x, bias_x, bias_w, bg_w, bg_x_, dcol_x, upd_x = 0, 1, 2, 3, 4, 6, 8, 9
    par_w, par_x_, sum_x, sum_w, small_x = 10, 11, 12, 13, 14

    loads = [
        pltpu.make_async_copy(src, dst, in_sem.at[n])
        for n, (src, dst) in enumerate(
            (
                (x_hbm, x_ref),
                (cot_hbm, cot_ref),
                (gain_hbm, gain_ref),
                (shift_hbm, shift_ref),
                (win_hbm, win_ref),
                (wb_hbm, wb_ref),
                (wo_hbm, wo_ref),
            )
        )
    ]
    for load in loads:
        load.start()

    stores = [
        pltpu.make_async_copy(src, dst, out_sem.at[n])
        for n, (src, dst) in enumerate(
            (
                (upd_ref, upd_hbm),
                (gp_ref, gp_hbm),
                (sum_r, sum_hbm.at[:, core]),
                (small_s, small_hbm.at[me]),
            )
        )
    ]

    y_at = lax.div(chip, 8)
    xs = [2 * lax.rem(lax.rem(lax.div(chip, 2), 4) + o, 4) for o in range(4)]
    zs = [lax.rem(lax.rem(chip, 2) + o, 2) for o in range(2)]
    around = [xs[x] + zs[z] for x in (2, 1, 3, 0) for z in (1, 0)]

    def each_chip(body, first=0, stop=4):
        def step(n, carry):
            for offset in around:
                body(8 * lax.rem(y_at + 2 - n + 3 * lax.div(n, 2), 4) + offset)
            return carry

        lax.fori_loop(first, min(stop, 3), step, 0)
        if stop == 4:
            for offset in around[:-1]:
                body(8 * y_at + offset)

    def each_peer(body, first=0, stop=4):
        def both(q):
            body(2 * q + 1 - core)
            body(2 * q + core)

        each_chip(both, first, stop)
        if stop == 4:
            body(twin)

    def near_peer(body):
        def step(t, carry):
            body(lax.rem(me + t, group))
            return carry

        lax.fori_loop(1, group, step, 0)

    def copy(which, src, dst, device):
        return pltpu.make_async_remote_copy(
            src_ref=src,
            dst_ref=dst,
            send_sem=send_sem.at[which],
            recv_sem=recv_sem.at[which],
            device_id={"dap": device},
            device_id_type=MESH,
        )

    sent = []

    def send(which, source_of, dest, order=each_peer):
        order(lambda e: copy(which, source_of(e), dest.at[me], e).start())
        sent.append((which, dest.at[pl.ds(0, group - 1)]))

    def wait_recv(which, part):
        pltpu.make_async_copy(part, part, recv_sem.at[which]).wait()

    def wait_send(which, part):
        pltpu.make_async_copy(part, part, send_sem.at[which]).wait()

    barrier = pltpu.get_barrier_semaphore()
    near_peer(
        lambda e: pl.semaphore_signal(barrier, inc=1, device_id={"dap": e}, device_id_type=MESH)
    )

    rec_erc = place(rec_to_erc)
    row_of = lax.broadcasted_iota(jnp.int32, (16, CH), 0)
    pick = jnp.where(
        (lax.broadcasted_iota(jnp.int32, (16, HEADS), 0) & 3)
        == lax.broadcasted_iota(jnp.int32, (16, HEADS), 1),
        1.0,
        0.0,
    ).astype(BF16)

    for n in (0, 2, 3, 5):
        loads[n].wait()
    gain = gain_ref[...]
    shift = shift_ref[...]
    wb16 = nn(pick, wb_ref[...])
    wbr = [jnp.where((row_of >> 2) == r, wb16, 0.0).astype(BF16) for r in range(ROWS)]
    average = jnp.full((CH, CH), 1.0 / CH, BF16)
    bias = jnp.zeros((16, N), F32)
    for r in range(ROWS):
        x = x_ref[r].astype(F32)
        mean = nn(x_ref[r], average)
        cen = x - mean
        var = jnp.mean(cen * cen, -1, keepdims=True)
        inv = lax.rsqrt(var + EPS)
        normed = cen * inv
        normed_ref[r] = normed
        inv_ref[r] = jnp.broadcast_to(inv, (N, CH))
        low = (normed * gain + shift).astype(BF16)
        np_ref[r] = low
        bias += nt(wbr[r], low)
    bias_r[chip, core] = bias.astype(BF16)
    for b in range(4):
        block = jnp.concatenate([np_ref[r, 64 * b : 64 * b + 64, :] for r in range(ROWS)], 0)
        pair_s[16 * b : 16 * b + 16] = nn(rec_erc, block).astype(BF16).reshape(16, 16, CH)

    pl.semaphore_wait(barrier, group - 1)
    each_chip(
        lambda q: copy(
            bias_x, bias_r.at[chip, core], bias_r.at[chip, core], 2 * q + core
        ).start()
    )
    sent.append((bias_x, bias_r.at[pl.ds(0, chips - 1), 0]))
    send(pair_x, lambda e: pair_s.at[e], pair_r)
    pair_r[me] = pair_s[me]

    for n in (1, 4, 6):
        loads[n].wait()
    for b in range(4):
        block = jnp.concatenate([cot_ref[r, 64 * b : 64 * b + 64, :] for r in range(ROWS)], 0)
        cot_s[16 * b : 16 * b + 16] = nn(rec_erc, block).astype(BF16).reshape(16, 16, CH)
    send(cot_x, lambda e: cot_s.at[e], cot_r)
    cot_r[me] = cot_s[me]

    erc_cer = place(erc_to_cer)
    erc_rec = place(erc_to_rec)
    cer_erc = place(cer_to_erc)
    par_f[...] = jnp.zeros_like(par_f)
    row = lax.broadcasted_iota(jnp.int32, (16, 16), 0)
    col = lax.broadcasted_iota(jnp.int32, (16, 16), 1)
    heads_at = [
        [
            jnp.where(
                (((row & 3) >> 1) == pair) & ((row >> 2) * 4 + (row & 1) * 2 + half == col), 1.0, 0.0
            ).astype(BF16)
            for half in (0, 1)
        ]
        for pair in (0, 1)
    ]
    for r in range(ROWS):
        high = normed_ref[r].astype(BF16)
        high_ref[r] = high
        low_ref[r] = (normed_ref[r] - high.astype(F32)).astype(BF16)

    w_in = win_ref[...]
    w_in_t = jnp.transpose(w_in.astype(F32)).astype(BF16)
    w_out = wo_ref[...]

    wait_recv(bias_x, bias_r.at[pl.ds(0, chips - 1), 0])
    share = copy(bias_w, bias_r.at[:, core], bias_r.at[:, core], twin)
    share.start()

    wait_recv(pair_x, pair_r.at[pl.ds(0, group - 1)])
    for b in range(4):
        got = nn(erc_cer, pair_r[16 * b : 16 * b + 16].reshape(256, CH)).astype(BF16)
        for c in range(COLS):
            cols_ref[c, 64 * b : 64 * b + 64, :] = got[64 * c : 64 * c + 64]
    for j in range(COLS):
        projected = nt(w_in_t, cols_ref[j])
        proj_ref[j] = projected[: 3 * CH].astype(BF16)
        gate_ref[j] = jax.nn.sigmoid(projected[3 * CH :])

    share.wait()
    key = lax.broadcasted_iota(jnp.int32, (64, N), 0)
    for b in range(4):
        block = bias_r[8 * b : 8 * b + 8].reshape(256, N)
        got = nn(erc_cer, block) * LOG2E
        mask = jnp.where(key + 64 * b < len_ref[0], 0.0, NEG)
        for h in range(HEADS):
            biasm_ref[h, 64 * b : 64 * b + 64, :] = got[64 * h : 64 * h + 64] + mask

    scale = 1.0 / math.sqrt(DIM)

    units = [(j, h) for j in range(COLS) for h in range(HEADS)]

    def part_of(which, j, h):
        first = CH * which + DIM * h
        return proj_ref[j, first : first + DIM, :]

    for j, h in units:
        raw = tn(part_of(1, j, h), part_of(0, j, h))
        score_ref[HEADS * j + h] = raw * (scale * LOG2E) + biasm_ref[h]
    for j, h in units:
        score = score_ref[HEADS * j + h]
        p = jnp.exp2(score - jnp.max(score, 0, keepdims=True))
        tot_ref[j, h : h + 1, :] = 1.0 / jnp.sum(p, 0, keepdims=True)
        p_ref[HEADS * j + h] = p.astype(BF16)
    for j, h in units:
        rows = slice(DIM * h, DIM * h + DIM)
        att = nn(part_of(2, j, h), p_ref[HEADS * j + h]) * tot_ref[j, h : h + 1, :]
        att_ref[j, rows, :] = att
        gated_ref[j, rows, :] = (gate_ref[j, rows, :] * att).astype(BF16)

    wait_recv(cot_x, cot_r.at[pl.ds(0, group - 1)])
    for b in range(4):
        got = nn(erc_cer, cot_r[16 * b : 16 * b + 16].reshape(256, CH)).astype(BF16)
        for c in range(COLS):
            cotc_ref[c, 64 * b : 64 * b + 64, :] = got[64 * c : 64 * c + 64]
    for j in range(COLS):
        dgate_ref[j] = nt(w_out, cotc_ref[j])

    def score_grads(heads):
        for j in range(COLS):
            for h in heads:
                rows = slice(DIM * h, DIM * h + DIM)
                att = att_ref[j, rows, :]
                gate = gate_ref[j, rows, :]
                dgated = dgate_ref[j, rows, :]
                datt = ((dgated * gate) * tot_ref[j, h : h + 1, :]).astype(BF16)
                datt_ref[j, rows, :] = datt
                delta_ref[j, h : h + 1, :] = jnp.sum(datt.astype(F32) * att, 0, keepdims=True)
                dg = dgated * att * gate * (1.0 - gate)
                dproj_ref[j, 3 * CH + DIM * h : 3 * CH + DIM * h + DIM, :] = dg.astype(BF16)
        for h in heads:
            for j in range(COLS):
                rows = slice(DIM * h, DIM * h + DIM)
                dweights = tn(part_of(2, j, h), datt_ref[j, rows, :])
                p = p_ref[HEADS * j + h].astype(F32)
                ds = p * (dweights - delta_ref[j, h : h + 1, :])
                if j == 0:
                    bacc_ref[h] = ds
                else:
                    bacc_ref[h] += ds
                ds_ref[HEADS * j + h] = ds.astype(BF16)

    def input_grads(heads):
        for which in range(3):
            for j in range(COLS):
                for h in heads:
                    ds = ds_ref[HEADS * j + h]
                    if which == 0:
                        grad = nn(part_of(1, j, h), ds) * scale
                    elif which == 1:
                        grad = nt(part_of(0, j, h), ds) * scale
                    else:
                        rows = slice(DIM * h, DIM * h + DIM)
                        grad = nt(datt_ref[j, rows, :], p_ref[HEADS * j + h])
                    first = CH * which + DIM * h
                    dproj_ref[j, first : first + DIM, :] = grad.astype(BF16)

    def gather_bias(pair):
        for b in range(4):
            block = jnp.concatenate(
                [
                    bacc_ref[h, 64 * b : 64 * b + 64, CH * half : CH * half + CH]
                    for h in (2 * pair, 2 * pair + 1)
                    for half in (0, 1)
                ],
                0,
            )
            got = nn(cer_erc, block.astype(BF16)).astype(BF16)
            bg_s[8 * b : 8 * b + 8, :, 16 * pair : 16 * pair + 16] = got.reshape(8, 2, 16, CH)

    every = tuple(range(HEADS))
    score_grads(every)
    gather_bias(0)
    gather_bias(1)
    bg_pass = copy(bg_w, bg_s.at[:, 1 - core], bg_x, twin)
    bg_pass.start()
    input_grads((0, 1))
    bg_pass.wait()
    for q in range(chips):
        bg_t[q] = (bg_s[q, core].astype(F32) + bg_x[q].astype(F32)).astype(BF16)
    each_chip(lambda q: copy(bg_x_, bg_t.at[q], bg_r.at[chip], 2 * q + core).start())
    sent.append((bg_x_, bg_r.at[pl.ds(0, chips - 1)]))
    bg_r[chip] = bg_t[chip]
    input_grads((2, 3))

    g_out = nn(gated_ref[0], cotc_ref[0])
    g_in = nn(dproj_ref[0], cols_ref[0])
    for j in range(1, COLS):
        g_out += nn(gated_ref[j], cotc_ref[j])
        g_in += nn(dproj_ref[j], cols_ref[j])
    par_f[pl.ds(8, group, stride=16), :] = g_out[:group]
    par_f[pl.ds(9, group, stride=16), :] = g_out[group:]
    for e in range(group):
        par_f[16 * e : 16 * e + 8, :] = g_in[8 * e : 8 * e + 8]
    par_s[...] = par_f[...].astype(BF16).reshape(chips, 2, 16, CH)
    par_pass = copy(par_w, par_s.at[:, 1 - core], par_x, twin)
    par_pass.start()

    for j in range(COLS):
        tmp_ref[j] = jnp.transpose(nn(w_in, dproj_ref[j])).astype(BF16)
    for b in range(4):
        block = jnp.concatenate([tmp_ref[j, 64 * b : 64 * b + 64, :] for j in range(COLS)], 0)
        dcol_s[16 * b : 16 * b + 16] = nn(cer_erc, block).astype(BF16).reshape(16, 16, CH)

    def send_dcol(e):
        copy(dcol_x, dcol_s.at[e], dcol_r.at[me], e).start()

    each_peer(send_dcol, 0, 2)
    par_pass.wait()
    for q in range(chips):
        par_t[q] = (par_s[q, core].astype(F32) + par_x[q].astype(F32)).astype(BF16)
    each_chip(lambda q: copy(par_x_, par_t.at[q], par_r.at[chip], 2 * q + core).start())
    sent.append((par_x_, par_r.at[pl.ds(0, chips - 1)]))
    each_peer(send_dcol, 2, 4)
    sent.append((dcol_x, dcol_r.at[pl.ds(0, group - 1)]))
    par_r[chip] = par_t[chip]
    dcol_r[me] = dcol_s[me]

    for j in range(COLS):
        tmp_ref[j] = tn(gated_ref[j], w_out).astype(BF16)
    for b in range(4):
        block = jnp.concatenate([tmp_ref[j, 64 * b : 64 * b + 64, :] for j in range(COLS)], 0)
        upd_s[16 * b : 16 * b + 16] = nn(cer_erc, block).astype(BF16).reshape(16, 16, CH)
    send(upd_x, lambda e: upd_s.at[e], upd_r)
    upd_r[me] = upd_s[me]

    wait_recv(bg_x_, bg_r.at[pl.ds(0, chips - 1)])
    sums = bg_r[0].astype(F32)
    for s in range(1, chips):
        sums += bg_r[s].astype(F32)
    sums = sums.astype(BF16)
    bsum = jnp.concatenate(
        [nn(heads_at[0][half], sums[:16]) + nn(heads_at[1][half], sums[16:]) for half in (0, 1)],
        1,
    ).astype(BF16)
    gwb = jnp.zeros((16, CH), F32)
    part = jnp.zeros((16, CH), F32)
    for r in range(ROWS):
        here = (row_of >> 2) == r
        gwb += jnp.where(here, nn(bsum, np_ref[r]), 0.0)
        part += jnp.where(here, nn(bsum, high_ref[r]) + nn(bsum, low_ref[r]), 0.0)
    small_s[0:4, :] = gwb[0:4] + gwb[4:8] + gwb[8:12] + gwb[12:16]
    grad_gain = jnp.sum(part * wb16, 0, keepdims=True)
    grad_shift = jnp.sum(jnp.sum(bsum.astype(F32), 1, keepdims=True) * wb16, 0, keepdims=True)

    wait_recv(par_x_, par_r.at[pl.ds(0, chips - 1)])
    total = par_r[0].astype(F32)
    for s in range(1, chips):
        total += par_r[s].astype(F32)
    sum_r[chip] = total.astype(BF16)
    each_chip(lambda q: copy(sum_x, sum_r.at[chip], sum_r.at[chip], 2 * q + core).start())
    sent.append((sum_x, sum_r.at[pl.ds(0, chips - 1)]))

    wait_recv(dcol_x, dcol_r.at[pl.ds(0, group - 1)])
    for b in range(4):
        got = nn(erc_rec, dcol_r[16 * b : 16 * b + 16].reshape(256, CH))
        for r in range(ROWS):
            dn_ref[r, 64 * b : 64 * b + 64, :] = got[64 * r : 64 * r + 64]
    for r in range(ROWS):
        grad_gain += jnp.sum(dn_ref[r] * normed_ref[r], 0, keepdims=True)
        grad_shift += jnp.sum(dn_ref[r], 0, keepdims=True)
    small_s[4:5, :] = grad_gain
    small_s[5:6, :] = grad_shift
    send(small_x, lambda e: small_s, small_hbm)
    stores[3].start()

    for r in range(ROWS):
        normed = normed_ref[r]
        scaled = (dn_ref[r] + tn(bsum, wbr[r])) * gain
        mean_s = jnp.mean(scaled, -1, keepdims=True)
        mean_sn = jnp.mean(scaled * normed, -1, keepdims=True)
        gp_ref[r] = (inv_ref[r] * (scaled - mean_s - normed * mean_sn)).astype(BF16)
    stores[1].start()

    wait_recv(upd_x, upd_r.at[pl.ds(0, group - 1)])
    for b in range(4):
        got = nn(erc_rec, upd_r[16 * b : 16 * b + 16].reshape(256, CH)).astype(BF16)
        for r in range(ROWS):
            upd_ref[r, 64 * b : 64 * b + 64, :] = got[64 * r : 64 * r + 64]
    stores[0].start()

    wait_recv(sum_x, sum_r.at[pl.ds(0, chips - 1)])
    sum_pass = copy(sum_w, sum_r, sum_hbm.at[:, core], twin)
    sum_pass.start()
    stores[2].start()
    sum_pass.wait()
    wait_recv(small_x, small_hbm.at[pl.ds(0, group - 1)])

    for which, part in sent:
        wait_send(which, part)
    for store in stores:
        store.wait()


def finish(
    group,
    upd_hbm,
    gp_hbm,
    sum_hbm,
    small_hbm,
    upd_out,
    gp_out,
    gwin_out,
    gwo_out,
    gwb_out,
    gg_out,
    gs_out,
    upd_ref,
    gp_ref,
    sum_ref,
    small_ref,
    gwin_ref,
    gwo_ref,
    gwb_ref,
    gg_ref,
    gs_ref,
    par_f,
    in_sem,
    out_sem,
):
    loads = [
        pltpu.make_async_copy(src, dst, in_sem.at[n])
        for n, (src, dst) in enumerate(
            ((sum_hbm, sum_ref), (small_hbm, small_ref), (upd_hbm, upd_ref), (gp_hbm, gp_ref))
        )
    ]
    stores = [
        pltpu.make_async_copy(src, dst, out_sem.at[n])
        for n, (src, dst) in enumerate(
            (
                (upd_ref, upd_out),
                (gp_ref, gp_out),
                (gwin_ref, gwin_out),
                (gwo_ref, gwo_out),
                (gwb_ref, gwb_out),
                (gg_ref, gg_out),
                (gs_ref, gs_out),
            )
        )
    ]
    for load in loads:
        load.start()
    source = lax.broadcasted_iota(jnp.int32, (256, CH), 0)
    target = lax.broadcasted_iota(jnp.int32, (256, CH), 1)
    pick_in = jnp.where((target >> 3) * 16 + (target & 7) == source, 1.0, 0.0).astype(BF16)

    for n in (0, 1):
        loads[2 + n].wait()
        stores[n].start()
    loads[0].wait()
    for q in range(4):
        rows = sum_ref[8 * q : 8 * q + 8].reshape(256, CH)
        gwin_ref[:, CH * q : CH * q + CH] = tn(rows, pick_in)
    stores[2].start()
    par_f[...] = sum_ref[...].astype(F32).reshape(group * 16, CH)
    gwo_ref[0:group, :] = par_f[pl.ds(8, group, stride=16), :]
    gwo_ref[group:, :] = par_f[pl.ds(9, group, stride=16), :]
    stores[3].start()
    loads[1].wait()
    small = small_ref[0]
    for s in range(1, group):
        small += small_ref[s]
    gwb_ref[...] = small[0:HEADS]
    gg_ref[...] = small[4:5]
    gs_ref[...] = small[5:6]
    for n in (4, 5, 6):
        stores[n].start()
    for store in stores:
        store.wait()


def per_device(group, pair_state, cotangent, length, norm_gain, norm_shift, w_in, w_bias, w_out):
    vmem = pl.BlockSpec(memory_space=pltpu.VMEM)
    smem = pl.BlockSpec(memory_space=pltpu.SMEM)
    hbm = pl.BlockSpec(memory_space=pltpu.HBM)
    chips = group // 2
    block = (group, 16, CH)
    shapes = (
        jax.ShapeDtypeStruct((ROWS, N, CH), BF16),
        jax.ShapeDtypeStruct((ROWS, N, CH), BF16),
        jax.ShapeDtypeStruct((CH, 4 * CH), F32),
        jax.ShapeDtypeStruct((CH, CH), F32),
        jax.ShapeDtypeStruct((HEADS, CH), F32),
        jax.ShapeDtypeStruct((1, CH), F32),
        jax.ShapeDtypeStruct((1, CH), F32),
    )
    passed = shapes[:2] + (
        jax.ShapeDtypeStruct((chips, 2, 16, CH), BF16),
        jax.ShapeDtypeStruct((group, 6, CH), F32),
    )
    out = pl.pallas_call(
        functools.partial(kernel, group),
        out_shape=passed,
        in_specs=[hbm, hbm, smem] + [hbm] * 5,
        out_specs=[hbm] * 4,
        scratch_shapes=[pltpu.VMEM(s.shape, s.dtype) for s in shapes[:2]]
        + [
            pltpu.VMEM((ROWS, N, CH), BF16),
            pltpu.VMEM((ROWS, N, CH), BF16),
            pltpu.VMEM((1, CH), F32),
            pltpu.VMEM((1, CH), F32),
            pltpu.VMEM((CH, 4 * CH), BF16),
            pltpu.VMEM((HEADS, CH), BF16),
            pltpu.VMEM((CH, CH), BF16),
            pltpu.VMEM((ROWS, N, CH), F32),
            pltpu.VMEM((ROWS, N, CH), F32),
            pltpu.VMEM((ROWS, N, CH), BF16),
            pltpu.VMEM((ROWS, N, CH), BF16),
            pltpu.VMEM((ROWS, N, CH), BF16),
            pltpu.VMEM((ROWS, N, CH), F32),
            pltpu.VMEM(block, BF16),
            pltpu.VMEM(block, BF16),
            pltpu.VMEM(block, BF16),
            pltpu.VMEM(block, BF16),
            pltpu.VMEM((chips, 2, 16, N), BF16),
            pltpu.VMEM((COLS, N, CH), BF16),
            pltpu.VMEM((COLS, N, CH), BF16),
            pltpu.VMEM((HEADS, N, N), F32),
            pltpu.VMEM((COLS, 3 * CH, N), BF16),
            pltpu.VMEM((COLS, CH, N), F32),
            pltpu.VMEM((COLS, CH, N), F32),
            pltpu.VMEM((COLS, CH, N), BF16),
            pltpu.VMEM((COLS, CH, N), F32),
            pltpu.VMEM((COLS, 8, N), F32),
            pltpu.VMEM((COLS * HEADS, N, N), BF16),
            pltpu.VMEM((COLS, 4 * CH, N), BF16),
            pltpu.VMEM((HEADS, N, N), F32),
            pltpu.VMEM((COLS, N, CH), BF16),
            pltpu.VMEM(block, BF16),
            pltpu.VMEM(block, BF16),
            pltpu.VMEM(block, BF16),
            pltpu.VMEM(block, BF16),
            pltpu.VMEM((chips, 2, 32, CH), BF16),
            pltpu.VMEM((chips, 32, CH), BF16),
            pltpu.VMEM((chips, 32, CH), BF16),
            pltpu.VMEM((chips, 32, CH), BF16),
            pltpu.VMEM((COLS * HEADS, N, N), F32),
            pltpu.VMEM((COLS, CH, N), BF16),
            pltpu.VMEM((COLS, 8, N), F32),
            pltpu.VMEM((COLS * HEADS, N, N), BF16),
            pltpu.VMEM((group * 16, CH), F32),
            pltpu.VMEM((chips, 2, 16, CH), BF16),
            pltpu.VMEM((chips, 16, CH), BF16),
            pltpu.VMEM((chips, 16, CH), BF16),
            pltpu.VMEM((chips, 16, CH), BF16),
            pltpu.VMEM((chips, 16, CH), BF16),
            pltpu.VMEM((6, CH), F32),
            pltpu.SemaphoreType.DMA((7,)),
            pltpu.SemaphoreType.DMA((7,)),
            pltpu.SemaphoreType.DMA((15,)),
            pltpu.SemaphoreType.DMA((15,)),
        ],
        compiler_params=pltpu.CompilerParams(
            collective_id=0, has_side_effects=True, vmem_limit_bytes=60 * 2**20
        ),
    )(
        pair_state,
        cotangent,
        length,
        norm_gain.reshape(1, CH),
        norm_shift.reshape(1, CH),
        w_in,
        w_bias.T,
        w_out,
    )
    out = pl.pallas_call(
        functools.partial(finish, group),
        out_shape=shapes,
        in_specs=[hbm] * 4,
        out_specs=[hbm] * 7,
        scratch_shapes=[pltpu.VMEM(s.shape, s.dtype) for s in passed]
        + [pltpu.VMEM(s.shape, s.dtype) for s in shapes[2:]]
        + [
            pltpu.VMEM((group * 16, CH), F32),
            pltpu.SemaphoreType.DMA((4,)),
            pltpu.SemaphoreType.DMA((7,)),
        ],
        compiler_params=pltpu.CompilerParams(vmem_limit_bytes=60 * 2**20),
    )(*out)
    return (*out[:4], out[4].T, out[5].reshape(CH), out[6].reshape(CH))


def solution(mesh):
    split = P(("dp", "dap"), None, None)
    return jax.shard_map(
        functools.partial(per_device, mesh.shape["dap"]),
        mesh=mesh,
        in_specs=(split, split, P("dp"), P(), P(), P(), P(), P()),
        out_specs=(split, split, P("dp", None), P("dp", None), P("dp", None), P("dp"), P("dp")),
        check_vma=False,
    )
```
